32 devices in a mesh: dp: 8 (over y, x, core), tensor: 4 (over z).
Axes of the slice: x: 2, y: 2, z: 4, core: 2. Of those that a mesh axis runs over, the one named last changes fastest.
Arguments:
- layer_input: bfloat16 [2, 5120, 2048], P(None, 'dp'), may hold values from -6 to 6
- cotangent: float32 [2, 5120, 2048], P(None, 'dp'), may hold values from -6 to 6
- w_query: bfloat16 [2048, 2048], P('dp', 'tensor'), may hold values from -0.125 to 0.125
- w_key: bfloat16 [2048, 2048], P('dp', 'tensor'), may hold values from -0.125 to 0.125
- w_value: bfloat16 [2048, 2048], P('dp', 'tensor'), may hold values from -0.125 to 0.125
- w_output: bfloat16 [2048, 2048], P('tensor', 'dp'), may hold values from -0.125 to 0.125
- w_gate: bfloat16 [2048, 8192], P('dp', 'tensor'), may hold values from -0.125 to 0.125
- w_up: bfloat16 [2048, 8192], P('dp', 'tensor'), may hold values from -0.125 to 0.125
- w_down: bfloat16 [8192, 2048], P('tensor', 'dp'), may hold values from -0.0625 to 0.0625
- query_gain: float32 [2048], P('tensor'), may hold values from 0.1 to 1.9
- key_gain: float32 [2048], P('tensor'), may hold values from 0.1 to 1.9
- attn_gain: float32 [2048], replicated, may hold values from 0.1 to 1.9
- mlp_gain: float32 [2048], replicated, may hold values from 0.1 to 1.9
- slot_parent: int32 [2, 40], replicated, may hold values from 0 to 39, as said below
- slot_depth: int32 [2, 40], replicated, may hold values from 0 to 9, as said below
Outputs:
- layer_output: bfloat16 [2, 5120, 2048], P(None, 'dp')
- input_grad: float32 [2, 5120, 2048], P(None, ('dp', 'tensor'))
- w_query_grad: float32 [2048, 2048], P('dp', 'tensor')
- w_key_grad: float32 [2048, 2048], P('dp', 'tensor')
- w_value_grad: float32 [2048, 2048], P('dp', 'tensor')
- w_output_grad: float32 [2048, 2048], P('tensor', 'dp')
- w_gate_grad: float32 [2048, 8192], P('dp', 'tensor')
- w_up_grad: float32 [2048, 8192], P('dp', 'tensor')
- w_down_grad: float32 [8192, 2048], P('tensor', 'dp')
- query_gain_grad: float32 [2048], P('tensor')
- key_gain_grad: float32 [2048], P('tensor')
- attn_gain_grad: float32 [2048], replicated
- mlp_gain_grad: float32 [2048], replicated
The draws below stay inside these ranges and needn't reach their ends.
Inputs may be any that keep to these rules, and one draw needn't show every extreme that they name: slot_parent[b, s] is the slot of micro-batch b that holds the parent block of the block in slot s; the first trunk block of a tree names its own slot. Each of the 2 trees of a micro-batch has 20 blocks: 8 trunk blocks in a chain, 4 branch blocks whose parent is the last trunk block, and 2 leaf blocks under each branch; trees and blocks lie on slots in a random order. `slot_depth`: the depth of the block in slot s: its place along the trunk, 8 for a branch block, 9 for a leaf block; consistent with slot_parent.
All inputs are finite; a program needn't handle non-finite values.
Results may differ from the reference program's by a relative error of at most 0.023.
Values may be sent and summed in bfloat16 or wider, within the bound.
No kernel may reach another device: no remote copies, remote signals or barrier semaphores. Data moves between devices by JAX's collectives and lax.ppermute only.
A program may use at most 384 MiB of HBM per device.

```python
import jax
import jax.numpy as jnp
from jax import lax

D = 2048
HEADS = 16
FF = 8192
BLK = 128
TRUNK = 8
BRANCHES = 4
LEAVES = 2
TREE_BLOCKS = 20
MB = 2
SEG_DEV = 5
NB = 40


def tree_layout(key):
    block_ids = jnp.arange(NB, dtype=jnp.int32)
    within = block_ids % TREE_BLOCKS
    tree_base = block_ids - within
    leaf_first = TRUNK + BRANCHES
    parent_within = jnp.where(within == 0, 0, jnp.where(within < TRUNK, within - 1, jnp.where(within < leaf_first, TRUNK - 1, TRUNK + (within - leaf_first) // LEAVES)))
    depth_within = jnp.where(within < TRUNK, within, jnp.where(within < leaf_first, TRUNK, TRUNK + 1)).astype(jnp.int32)
    parent_block = tree_base + parent_within
    parents = []
    depths = []
    for micro_idx in range(MB):
        placing = jax.random.permutation(jax.random.fold_in(key, 7001 + micro_idx), NB).astype(jnp.int32)
        parents.append(jnp.zeros((NB,), jnp.int32).at[placing].set(placing[parent_block]))
        depths.append(jnp.zeros((NB,), jnp.int32).at[placing].set(depth_within))
    return (jnp.stack(parents), jnp.stack(depths))


def draw_slot_parent(key, part):
    return tree_layout(key)[0]


def draw_slot_depth(key, part):
    return tree_layout(key)[1]


def block_levels(rng, dims, cuts, low, high):
    def one(axis_at, parts):
        heights = jax.random.uniform(jax.random.fold_in(jax.random.fold_in(rng, 6), axis_at), (parts,), jnp.float32, low / len(cuts), high / len(cuts))
        return jnp.repeat(jnp.exp(heights), dims[axis_at] // parts).reshape((-1,) + (1,) * (len(dims) - axis_at - 1))

    factor_of = one(*cuts[0])
    for cut in cuts[1:]:
        factor_of = factor_of * one(*cut)
    return factor_of


def normal_values(rng, extent, width, most, split=(), kind=jnp.bfloat16):
    loudness = block_levels(rng, extent, split, -0.22, 0.18) if split else 1.0
    values = jax.random.normal(rng, extent, jnp.float32) * width * loudness
    return jnp.minimum(jnp.maximum(values, -most), most).astype(kind)


def setup_inputs(seed: int = 0) -> dict:
    keys = jax.random.split(jax.random.key(seed), 16)
    return {
        "layer_input": normal_values(keys[0], (MB, NB * BLK, D), 1.0, 6.0, ((1, 8),)),
        "cotangent": normal_values(keys[1], (MB, NB * BLK, D), 1.0, 6.0, ((1, 8),), jnp.float32),
        "w_query": normal_values(keys[2], (D, D), D ** -0.5, 0.125, ((0, 8), (1, 4))),
        "w_key": normal_values(keys[3], (D, D), D ** -0.5, 0.125, ((0, 8), (1, 4))),
        "w_value": normal_values(keys[4], (D, D), D ** -0.5, 0.125, ((0, 8), (1, 4))),
        "w_output": normal_values(keys[5], (D, D), D ** -0.5, 0.125, ((0, 4), (1, 8))),
        "w_gate": normal_values(keys[6], (D, FF), D ** -0.5, 0.125, ((0, 8), (1, 4))),
        "w_up": normal_values(keys[7], (D, FF), D ** -0.5, 0.125, ((0, 8), (1, 4))),
        "w_down": normal_values(keys[8], (FF, D), FF ** -0.5, 0.0625, ((0, 4), (1, 8))),
        "query_gain": jnp.clip(1.0 + 0.18 * jax.random.normal(keys[9], (D,), jnp.float32), 0.1, 1.9),
        "key_gain": jnp.clip(1.0 + 0.18 * jax.random.normal(keys[10], (D,), jnp.float32), 0.1, 1.9),
        "attn_gain": jnp.clip(1.0 + 0.18 * jax.random.normal(keys[11], (D,), jnp.float32), 0.1, 1.9),
        "mlp_gain": jnp.clip(1.0 + 0.18 * jax.random.normal(keys[12], (D,), jnp.float32), 0.1, 1.9),
        "slot_parent": draw_slot_parent(jax.random.fold_in(keys[15], 71), 0),
        "slot_depth": draw_slot_depth(jax.random.fold_in(keys[15], 71), 0),
    }


EPSILON = 1e-06
ROPE_BASE = 500000.0

@jax.custom_vjp
def low(v):
    return lax.optimization_barrier(v.astype(jnp.bfloat16)).astype(jnp.float32)

@jax.custom_vjp
def low_back(v):
    return v

def low_keep(v):
    return (low(v), None)

def low_pass(kept, grad):
    return (grad,)

def back_keep(v):
    return (v, None)

def back_low(kept, grad):
    return (low(grad),)
low.defvjp(low_keep, low_pass)
low_back.defvjp(back_keep, back_low)

def matmul_hi(left, right):
    return jnp.dot(left, right, preferred_element_type=jnp.float32, precision=lax.Precision.HIGHEST)

def rope_tables(depth_row):
    head_size = D // HEADS
    half_size = head_size // 2
    offsets = jnp.arange(BLK, dtype=jnp.int32)
    places = (depth_row[:, None] * BLK + offsets[None, :]).reshape(-1).astype(jnp.float32)
    frequency = ROPE_BASE ** (-2.0 * jnp.arange(half_size, dtype=jnp.float32) / head_size)
    angles = places[:, None] * frequency[None, :]
    return (jnp.cos(angles), jnp.sin(angles))

def rotate(values, cos_table, sin_table, direction):
    head_size = D // HEADS
    half_size = head_size // 2
    count = values.shape[0]
    by_head = values.reshape(count, -1, head_size)
    front_half = by_head[..., :half_size]
    back_half = by_head[..., half_size:]
    cosines = cos_table[:, None, :]
    sines = direction * sin_table[:, None, :]
    turned = jnp.concatenate([front_half * cosines - back_half * sines, back_half * cosines + front_half * sines], -1)
    return turned.reshape(count, -1)

def ancestry(parent_row):
    blocks = parent_row.shape[0]
    slot_ids = jnp.arange(blocks, dtype=jnp.int32)
    onehot = (parent_row[:, None] == slot_ids[None, :]).astype(jnp.float32)
    reach = jnp.eye(blocks, dtype=jnp.float32)
    walker = reach
    for step_idx in range(TRUNK + 1):
        walker = jnp.dot(walker, onehot, precision=lax.Precision.HIGHEST)
        reach = jnp.maximum(reach, walker)
    return reach

def path_mask(reach_rows, first_slot, blocks):
    slots_here = reach_rows.shape[0]
    mine = first_slot + jnp.arange(slots_here, dtype=jnp.int32)
    others = jnp.arange(blocks, dtype=jnp.int32)
    offsets = jnp.arange(BLK, dtype=jnp.int32)
    permitted = reach_rows > 0.5
    same_slot = mine[:, None] == others[None, :]
    causal = offsets[:, None] >= offsets[None, :]
    combined = permitted[:, None, :, None] & (jnp.logical_not(same_slot)[:, None, :, None] | causal[None, :, None, :])
    return combined.reshape(slots_here * BLK, blocks * BLK)

def rms_norm(values, gain_vec):
    return values * lax.rsqrt(lax.optimization_barrier(jnp.mean(values * values, axis=-1, keepdims=True)) + EPSILON) * gain_vec

def one_layer(tokens, params, parent_row, depth_row):
    w_query, w_key, w_value, w_output, w_gate, w_up, w_down, query_gain, key_gain, attn_gain, mlp_gain = params
    blocks = parent_row.shape[0]
    count = blocks * BLK
    head_size = D // HEADS
    scaling = head_size ** (-0.5)
    cos_table, sin_table = rope_tables(depth_row)
    query_raw = low_back(matmul_hi(tokens, w_query))
    key_raw = low_back(matmul_hi(tokens, w_key))
    values = low(low_back(matmul_hi(tokens, w_value)))
    queries = low(rotate(rms_norm(query_raw, query_gain), cos_table, sin_table, 1.0))
    keys_all = low(rotate(rms_norm(key_raw, key_gain), cos_table, sin_table, 1.0))
    keys_heads = keys_all.reshape(count, HEADS, head_size)
    values_heads = values.reshape(count, HEADS, head_size)
    reach = ancestry(parent_row)
    group_rows = SEG_DEV * BLK

    def one_group(group_idx):
        query_rows = lax.dynamic_slice_in_dim(queries, group_idx * group_rows, group_rows, 0).reshape(group_rows, HEADS, head_size)
        reach_rows = lax.dynamic_slice_in_dim(reach, group_idx * SEG_DEV, SEG_DEV, 0)
        permitted = path_mask(reach_rows, group_idx * SEG_DEV, blocks)
        scores = jnp.einsum('qhd,khd->hqk', query_rows, keys_heads, precision=lax.Precision.HIGHEST, preferred_element_type=jnp.float32) * scaling
        scores = low_back(scores)
        scores = jnp.where(permitted[None], scores, -1e+30)
        maximum = lax.optimization_barrier(jnp.max(scores, axis=-1, keepdims=True))
        expsum = jnp.exp(scores - maximum)
        probs_row = low(expsum / lax.optimization_barrier(jnp.sum(expsum, axis=-1, keepdims=True)))
        attended = jnp.einsum('hqk,khd->qhd', probs_row, values_heads, precision=lax.Precision.HIGHEST, preferred_element_type=jnp.float32)
        return attended.reshape(group_rows, D)
    attended = lax.map(jax.checkpoint(one_group), jnp.arange(count // group_rows, dtype=jnp.int32))
    attended = low(low_back(attended.reshape(count, D)))
    projected = low_back(matmul_hi(attended, w_output))
    hidden = tokens + rms_norm(projected, attn_gain)
    hidden_low = low(hidden)
    gate_pre = low_back(matmul_hi(hidden_low, w_gate))
    up_pre = low_back(matmul_hi(hidden_low, w_up))
    activated = low(jax.nn.silu(gate_pre) * up_pre)
    mlp_proj = low_back(matmul_hi(activated, w_down))
    return hidden + rms_norm(mlp_proj, mlp_gain)

def reference(layer_input, cotangent, w_query, w_key, w_value, w_output, w_gate, w_up, w_down, query_gain, key_gain, attn_gain, mlp_gain, slot_parent, slot_depth):
    params = tuple((item.astype(jnp.float32) for item in (w_query, w_key, w_value, w_output, w_gate, w_up, w_down, query_gain, key_gain, attn_gain, mlp_gain)))

    def forward(inputs, weights):
        return jnp.stack([one_layer(inputs[micro_idx], weights, slot_parent[micro_idx], slot_depth[micro_idx]) for micro_idx in range(MB)])
    result, pullback = jax.vjp(forward, layer_input.astype(jnp.float32), params)
    input_grad, grads = pullback(cotangent)
    return (result.astype(jnp.bfloat16), input_grad, grads[0], grads[1], grads[2], grads[3], grads[4], grads[5], grads[6], grads[7], grads[8], grads[9], grads[10])
```

```python
import functools

import jax
import jax.numpy as jnp
from jax import lax
from jax.experimental import pallas as pl
from jax.experimental.pallas import tpu as pltpu
from jax.sharding import PartitionSpec as P

D = 2048
HEADS = 16
HEAD = D // HEADS
BLK = 128
TRUNK = 8
BRANCHES = 4
LEAVES = 2
TREE_BLOCKS = 20
MB = 2
SEG_DEV = 5
PAIR = 2 * BLK
TRUNK_ROWS = TRUNK * BLK

EPSILON = 1e-06
ROPE_BASE = 500000.0
SCALING = HEAD ** (-0.5)
VMEM_LIMIT = 56 * 1024 * 1024

f32 = jnp.float32
bf16 = jnp.bfloat16


def tree_order(parents, depths):
    blocks = parents.shape[1]
    ids = jnp.arange(blocks, dtype=jnp.int32)

    def follow(table, index):
        hot = index[:, :, None] == ids[None, None, :]
        return jnp.sum(jnp.where(hot, table[:, None, :], 0), axis=-1)

    up2 = follow(parents, parents)
    up4 = follow(up2, up2)
    up8 = follow(up4, up4)
    root = follow(up8, up8)
    is_leaf = depths == TRUNK + 1
    above = jnp.where(is_leaf, parents, 0)
    key = ((root * (TRUNK + 2) + depths) * blocks + above) * blocks + ids[None, :]
    rank = jnp.sum((key[:, None, :] < key[:, :, None]).astype(jnp.int32), axis=-1)
    return jnp.sum(
        jnp.where(rank[:, None, :] == ids[None, :, None], ids[None, None, :], 0), axis=-1
    ).astype(jnp.int32)


def rope_tables(depths):
    half = HEAD // 2
    offsets = jnp.arange(BLK, dtype=jnp.int32)
    places = (depths[:, :, None] * BLK + offsets).reshape(depths.shape[0], -1).astype(f32)
    frequency = ROPE_BASE ** (-2.0 * jnp.arange(half, dtype=f32) / HEAD)
    angles = places[:, :, None] * frequency
    cosines = jnp.cos(angles)
    sines = jnp.sin(angles)
    return (
        jnp.concatenate([cosines, cosines], -1),
        jnp.concatenate([-sines, sines], -1),
    )


def low_sum(*parts):
    total = parts[0].astype(f32)
    for part in parts[1:]:
        total = total + part.astype(f32)
    return total.astype(bf16)


def small_sum(values, axis, count):
    step = 1
    while step < count:
        values = values + lax.ppermute(values, axis, [(i, i ^ step) for i in range(count)])
        step *= 2
    return values


def line_all_reduce(chunks, count):
    if count != 4:
        return [lax.psum(chunk, "tensor") for chunk in chunks]
    index = lax.axis_index("tensor")
    inner = (index == 1) | (index == 2)
    sums = []
    for chunk in chunks:
        outer = lax.ppermute(chunk, "tensor", [(0, 1), (3, 2)])
        side = low_sum(chunk, outer)
        across = lax.ppermute(side, "tensor", [(1, 2), (2, 1)])
        total = low_sum(side, across)
        back = lax.ppermute(total, "tensor", [(1, 0), (2, 3)])
        sums.append(jnp.where(inner, total, back))
    return sums


def line_reduce_scatter(values, count):
    if count != 4:
        return lax.psum_scatter(values, "tensor", scatter_dimension=0, tiled=True).astype(f32)
    index = lax.axis_index("tensor")
    blocks = values.reshape(count, values.shape[0] // count, values.shape[1])

    def block(at):
        return lax.dynamic_index_in_dim(blocks, lax.rem(at + 2 * count, count), 0, keepdims=False)

    right = lax.ppermute(block(index + 3), "tensor", [(0, 1)])
    left = lax.ppermute(block(index - 3), "tensor", [(3, 2)])
    right = lax.ppermute(low_sum(block(index + 2), right), "tensor", [(0, 1), (1, 2)])
    left = lax.ppermute(low_sum(block(index - 2), left), "tensor", [(3, 2), (2, 1)])
    right = lax.ppermute(low_sum(block(index + 1), right), "tensor", [(0, 1), (1, 2), (2, 3)])
    left = lax.ppermute(low_sum(block(index - 1), left), "tensor", [(3, 2), (2, 1), (1, 0)])
    return block(index).astype(f32) + right.astype(f32) + left.astype(f32)


def line_all_gather(values, count):
    if count != 4:
        return lax.all_gather(values, "tensor", axis=1, tiled=True)
    index = lax.axis_index("tensor")
    width = values.shape[1]
    right1 = lax.ppermute(values, "tensor", [(0, 1), (1, 2), (2, 3)])
    left1 = lax.ppermute(values, "tensor", [(3, 2), (2, 1), (1, 0)])
    right2 = lax.ppermute(right1, "tensor", [(1, 2), (2, 3)])
    left2 = lax.ppermute(left1, "tensor", [(2, 1), (1, 0)])
    right3 = lax.ppermute(right2, "tensor", [(2, 3)])
    left3 = lax.ppermute(left2, "tensor", [(1, 0)])
    whole = jnp.zeros((values.shape[0], count * width), values.dtype)
    pieces = (
        values,
        jnp.where(index >= 1, right1, left3),
        jnp.where(index >= 2, right2, left2),
        jnp.where(index >= 3, right3, left1),
    )
    for back, piece in enumerate(pieces):
        place = lax.rem(index - back + count, count) * width
        whole = lax.dynamic_update_slice(whole, piece, (0, place))
    return whole


def turn(values, cosines, sines):
    return values * cosines + pltpu.roll(values, HEAD // 2, 1) * sines


def head_cols(head, group=0, heads=0):
    start = (group * heads + head) * HEAD
    return slice(start, start + HEAD)


def pack_kernel(heads, qk_ref, v_ref, inv_ref, gain_ref, cos_ref, sin_ref, out_ref):
    cosines = cos_ref[0]
    sines = sin_ref[0]
    for head in range(heads):
        for which in range(2):
            cols = head_cols(head, which, heads)
            normed = qk_ref[0, :, cols] * inv_ref[0, :, which : which + 1] * gain_ref[:, cols]
            out_ref[head, 0, which] = turn(normed, cosines, sines).astype(bf16)
        out_ref[head, 0, 2] = v_ref[0, :, head_cols(head)].astype(bf16)


def pack_heads(qk_raw, v_raw, inverse, gains, cosines, sines, heads):
    rows = qk_raw.shape[1]
    step = rows // 2
    width = heads * HEAD
    return pl.pallas_call(
        functools.partial(pack_kernel, heads),
        grid=(MB, rows // step),
        in_specs=[
            pl.BlockSpec((1, step, 2 * width), lambda b, r: (b, r, 0)),
            pl.BlockSpec((1, step, width), lambda b, r: (b, r, 0)),
            pl.BlockSpec((1, step, 2), lambda b, r: (b, r, 0)),
            pl.BlockSpec((1, 2 * width), lambda b, r: (0, 0)),
            pl.BlockSpec((1, step, HEAD), lambda b, r: (b, r, 0)),
            pl.BlockSpec((1, step, HEAD), lambda b, r: (b, r, 0)),
        ],
        out_specs=pl.BlockSpec((heads, 1, 3, step, HEAD), lambda b, r: (0, b, 0, r, 0)),
        out_shape=jax.ShapeDtypeStruct((heads, MB, 3, rows, HEAD), bf16),
        name="pack_heads",
    )(qk_raw, v_raw, inverse, gains, cosines, sines)


def inner_kernel(heads, back_ref, qk_ref, inv_ref, gain_ref, cos_ref, sin_ref, inner_ref, part_ref):
    cosines = cos_ref[0]
    sines = -sin_ref[0]

    @pl.when((pl.program_id(0) == 0) & (pl.program_id(1) == 0))
    def _():
        part_ref[...] = jnp.zeros_like(part_ref)

    for which in range(2):
        total = None
        for head in range(heads):
            cols = head_cols(head, which, heads)
            straight = turn(back_ref[head, 0, which].astype(f32), cosines, sines)
            hat = qk_ref[0, :, cols] * inv_ref[0, :, which : which + 1]
            product = straight * hat
            part_ref[:, cols] += jnp.sum(product, axis=0, keepdims=True)
            weighted = product * gain_ref[:, cols]
            total = weighted if total is None else total + weighted
        inner_ref[0, :, which : which + 1] = jnp.sum(total, axis=1, keepdims=True)


def inner_sums(back, qk_raw, inverse, gains, cosines, sines, heads):
    rows = qk_raw.shape[1]
    step = rows // 2
    width = heads * HEAD
    return pl.pallas_call(
        functools.partial(inner_kernel, heads),
        grid=(MB, rows // step),
        in_specs=[
            pl.BlockSpec((heads, 1, 2, step, HEAD), lambda b, r: (0, b, 0, r, 0)),
            pl.BlockSpec((1, step, 2 * width), lambda b, r: (b, r, 0)),
            pl.BlockSpec((1, step, 2), lambda b, r: (b, r, 0)),
            pl.BlockSpec((1, 2 * width), lambda b, r: (0, 0)),
            pl.BlockSpec((1, step, HEAD), lambda b, r: (b, r, 0)),
            pl.BlockSpec((1, step, HEAD), lambda b, r: (b, r, 0)),
        ],
        out_specs=[
            pl.BlockSpec((1, step, 2), lambda b, r: (b, r, 0)),
            pl.BlockSpec((1, 2 * width), lambda b, r: (0, 0)),
        ],
        out_shape=[
            jax.ShapeDtypeStruct((MB, rows, 2), f32),
            jax.ShapeDtypeStruct((1, 2 * width), f32),
        ],
        name="inner_sums",
    )(back, qk_raw, inverse, gains, cosines, sines)


def unpack_kernel(
    heads, back_ref, qk_ref, inv_ref, mean_ref, gain_ref, cos_ref, sin_ref, out_ref
):
    cosines = cos_ref[0]
    sines = -sin_ref[0]
    for head in range(heads):
        for which in range(2):
            cols = head_cols(head, which, heads)
            inverse = inv_ref[0, :, which : which + 1]
            straight = turn(back_ref[head, 0, which].astype(f32), cosines, sines)
            hat = qk_ref[0, :, cols] * inverse
            grad = inverse * (straight * gain_ref[:, cols] - hat * mean_ref[0, :, which : which + 1])
            out_ref[0, :, cols] = grad.astype(bf16)
        out_ref[0, :, head_cols(head, 2, heads)] = back_ref[head, 0, 2]


def unpack_heads(back, qk_raw, inverse, means, gains, cosines, sines, heads):
    rows = qk_raw.shape[1]
    step = rows // 2
    width = heads * HEAD
    return pl.pallas_call(
        functools.partial(unpack_kernel, heads),
        grid=(MB, rows // step),
        in_specs=[
            pl.BlockSpec((heads, 1, 3, step, HEAD), lambda b, r: (0, b, 0, r, 0)),
            pl.BlockSpec((1, step, 2 * width), lambda b, r: (b, r, 0)),
            pl.BlockSpec((1, step, 2), lambda b, r: (b, r, 0)),
            pl.BlockSpec((1, step, 2), lambda b, r: (b, r, 0)),
            pl.BlockSpec((1, 2 * width), lambda b, r: (0, 0)),
            pl.BlockSpec((1, step, HEAD), lambda b, r: (b, r, 0)),
            pl.BlockSpec((1, step, HEAD), lambda b, r: (b, r, 0)),
        ],
        out_specs=pl.BlockSpec((1, step, 3 * width), lambda b, r: (b, r, 0)),
        out_shape=jax.ShapeDtypeStruct((MB, rows, 3 * width), bf16),
        name="unpack_heads",
    )(back, qk_raw, inverse, means, gains, cosines, sines)


def nt(left, right):
    return lax.dot_general(left, right, (((1,), (1,)), ((), ())), preferred_element_type=f32)


def nn(left, right):
    return lax.dot_general(left, right, (((1,), (0,)), ((), ())), preferred_element_type=f32)


def key_query_iotas(keys):
    key_at = lax.broadcasted_iota(jnp.int32, (keys, PAIR), 0)
    query_at = lax.broadcasted_iota(jnp.int32, (keys, PAIR), 1)
    return key_at, query_at


def causal_mask():
    key_at, query_at = key_query_iotas(PAIR)
    return key_at <= query_at


def apart_mask(above):
    key_at, query_at = key_query_iotas(above + PAIR)
    key_at = key_at - above
    own = (key_at <= query_at) & ((key_at < BLK) == (query_at < BLK))
    return own | (key_at < 0)


def softmax_parts(queries, trunk_keys, near_keys, mask):
    near = jnp.where(mask, nt(near_keys, queries), -1e30)
    top = jnp.max(near, axis=0, keepdims=True)
    if trunk_keys is None:
        near = jnp.exp((near - top) * SCALING)
        scale = 1.0 / jnp.sum(near, axis=0, keepdims=True)
        return None, near * scale
    far = nt(trunk_keys, queries)
    top = jnp.maximum(top, jnp.max(far, axis=0, keepdims=True))
    near = jnp.exp((near - top) * SCALING)
    far = jnp.exp((far - top) * SCALING)
    scale = 1.0 / (jnp.sum(near, axis=0, keepdims=True) + jnp.sum(far, axis=0, keepdims=True))
    return far * scale, near * scale


def places(order_ref, tree):
    def at(within):
        slot = order_ref[tree * TREE_BLOCKS + within]
        return lax.div(slot, SEG_DEV), lax.rem(slot, SEG_DEV)

    return at


def load(ref, which, *spots):
    parts = [ref[group, which, row] for group, row in spots]
    return parts[0] if len(parts) == 1 else jnp.concatenate(parts, axis=0)


def across(values):
    return jnp.transpose(values.astype(f32)).astype(bf16)


def forward_kernel(trees, order_ref, x_ref, y_ref, k_ref, vt_ref):
    def one_tree(tree, carry):
        at = places(order_ref, tree)
        for within in range(TRUNK):
            rows = slice(within * BLK, (within + 1) * BLK)
            spot = at(within)
            k_ref[rows, :] = load(x_ref, 1, spot)
            vt_ref[:, rows] = across(load(x_ref, 2, spot))

        def attend(spots, far_rows, near_keys, near_values, mask):
            queries = load(x_ref, 0, *spots)
            far, near = softmax_parts(
                queries, k_ref[:far_rows, :] if far_rows else None, near_keys, mask
            )
            summed = nn(across(near_values), near.astype(bf16))
            if far_rows:
                summed = summed + nn(vt_ref[:, :far_rows], far.astype(bf16))
            rows = jnp.transpose(summed).astype(bf16)
            y_ref[spots[0][0], spots[0][1]] = rows[:BLK]
            y_ref[spots[1][0], spots[1][1]] = rows[BLK:]

        causal = causal_mask()
        for pair in range(TRUNK // 2):
            spots = (at(2 * pair), at(2 * pair + 1))
            attend(spots, pair * PAIR, load(x_ref, 1, *spots), load(x_ref, 2, *spots), causal)
        apart = apart_mask(0)
        for pair in range(BRANCHES // 2):
            spots = (at(TRUNK + 2 * pair), at(TRUNK + 2 * pair + 1))
            attend(spots, TRUNK_ROWS, load(x_ref, 1, *spots), load(x_ref, 2, *spots), apart)
        under = apart_mask(BLK)
        for branch in range(BRANCHES):
            first = TRUNK + BRANCHES + LEAVES * branch
            spots = (at(first), at(first + 1))
            near = (at(TRUNK + branch),) + spots
            attend(spots, TRUNK_ROWS, load(x_ref, 1, *near), load(x_ref, 2, *near), under)
        return carry

    lax.fori_loop(0, trees, one_tree, 0)


def attend_forward(order, packed):
    groups = packed.shape[0]
    blocks = packed.shape[2]
    trees = groups * blocks // TREE_BLOCKS
    pairs = trees * TREE_BLOCKS * BLK * 1100
    return pl.pallas_call(
        functools.partial(forward_kernel, trees),
        in_specs=[
            pl.BlockSpec(memory_space=pltpu.SMEM),
            pl.BlockSpec(memory_space=pltpu.VMEM),
        ],
        out_specs=pl.BlockSpec(memory_space=pltpu.VMEM),
        out_shape=jax.ShapeDtypeStruct((groups, blocks, BLK, HEAD), bf16),
        scratch_shapes=[
            pltpu.VMEM((TRUNK_ROWS, HEAD), bf16),
            pltpu.VMEM((HEAD, TRUNK_ROWS), bf16),
        ],
        compiler_params=pltpu.CompilerParams(vmem_limit_bytes=VMEM_LIMIT),
        cost_estimate=pl.CostEstimate(
            flops=pairs * HEAD * 4, bytes_accessed=packed.size * 3, transcendentals=pairs
        ),
        name="attend_forward",
    )(order, packed)


def backward_kernel(
    trees, order_ref, x_ref, dy_ref, out_ref, k_ref, kt_ref, v_ref, dk_ref, dv_ref, dkb_ref, dvb_ref
):
    def one_tree(tree, carry):
        at = places(order_ref, tree)
        for within in range(TRUNK):
            rows = slice(within * BLK, (within + 1) * BLK)
            spot = at(within)
            keys = load(x_ref, 1, spot)
            k_ref[rows, :] = keys
            kt_ref[:, rows] = across(keys)
            v_ref[rows, :] = load(x_ref, 2, spot)

        def attend(spots, far_rows, near_spots, mask, start):
            queries = load(x_ref, 0, *spots)
            grads = jnp.concatenate(
                [dy_ref[spots[0][0], spots[0][1]], dy_ref[spots[1][0], spots[1][1]]], axis=0
            )
            near_keys = load(x_ref, 1, *near_spots)
            near_values = load(x_ref, 2, *near_spots)
            far, near = softmax_parts(
                queries, k_ref[:far_rows, :] if far_rows else None, near_keys, mask
            )
            near_grad = nt(near_values, grads)
            inner = jnp.sum(near * near_grad, axis=0, keepdims=True)
            if far_rows:
                far_grad = nt(v_ref[:far_rows, :], grads)
                inner = inner + jnp.sum(far * far_grad, axis=0, keepdims=True)
                far_score = (far * (far_grad - inner)).astype(bf16)
                far_dk = nn(far_score, queries)
                far_dv = nn(far.astype(bf16), grads)
                if start:
                    dk_ref[:far_rows, :] = far_dk
                    dv_ref[:far_rows, :] = far_dv
                else:
                    dk_ref[:far_rows, :] += far_dk
                    dv_ref[:far_rows, :] += far_dv
            near_score = (near * (near_grad - inner)).astype(bf16)
            turned = nn(across(near_keys), near_score)
            if far_rows:
                turned = turned + nn(kt_ref[:, :far_rows], far_score)
            rows = (jnp.transpose(turned) * SCALING).astype(bf16)
            out_ref[spots[0][0], 0, spots[0][1]] = rows[:BLK]
            out_ref[spots[1][0], 0, spots[1][1]] = rows[BLK:]
            return nn(near_score, queries), nn(near.astype(bf16), grads)

        def store(spot, key_grad, value_grad):
            out_ref[spot[0], 1, spot[1]] = (key_grad * SCALING).astype(bf16)
            out_ref[spot[0], 2, spot[1]] = value_grad.astype(bf16)

        under = apart_mask(BLK)
        for branch in range(BRANCHES):
            first = TRUNK + BRANCHES + LEAVES * branch
            spots = (at(first), at(first + 1))
            key_grad, value_grad = attend(
                spots, TRUNK_ROWS, (at(TRUNK + branch),) + spots, under, branch == 0
            )
            dkb_ref[branch] = key_grad[:BLK]
            dvb_ref[branch] = value_grad[:BLK]
            store(spots[0], key_grad[BLK : 2 * BLK], value_grad[BLK : 2 * BLK])
            store(spots[1], key_grad[2 * BLK :], value_grad[2 * BLK :])
        apart = apart_mask(0)
        for pair in range(BRANCHES // 2):
            spots = (at(TRUNK + 2 * pair), at(TRUNK + 2 * pair + 1))
            key_grad, value_grad = attend(spots, TRUNK_ROWS, spots, apart, False)
            for half in range(2):
                rows = slice(half * BLK, (half + 1) * BLK)
                branch = 2 * pair + half
                store(
                    spots[half], key_grad[rows] + dkb_ref[branch], value_grad[rows] + dvb_ref[branch]
                )
        causal = causal_mask()
        for pair in reversed(range(TRUNK // 2)):
            spots = (at(2 * pair), at(2 * pair + 1))
            key_grad, value_grad = attend(spots, pair * PAIR, spots, causal, False)
            for half in range(2):
                rows = slice(half * BLK, (half + 1) * BLK)
                held = slice(pair * PAIR + half * BLK, pair * PAIR + (half + 1) * BLK)
                store(
                    spots[half],
                    key_grad[rows] + dk_ref[held, :],
                    value_grad[rows] + dv_ref[held, :],
                )
        return carry

    lax.fori_loop(0, trees, one_tree, 0)


def attend_backward(order, packed, grads):
    groups = packed.shape[0]
    blocks = packed.shape[2]
    trees = groups * blocks // TREE_BLOCKS
    pairs = trees * TREE_BLOCKS * BLK * 1100
    return pl.pallas_call(
        functools.partial(backward_kernel, trees),
        in_specs=[
            pl.BlockSpec(memory_space=pltpu.SMEM),
            pl.BlockSpec(memory_space=pltpu.VMEM),
            pl.BlockSpec(memory_space=pltpu.VMEM),
        ],
        out_specs=pl.BlockSpec(memory_space=pltpu.VMEM),
        out_shape=jax.ShapeDtypeStruct(packed.shape, bf16),
        scratch_shapes=[
            pltpu.VMEM((TRUNK_ROWS, HEAD), bf16),
            pltpu.VMEM((HEAD, TRUNK_ROWS), bf16),
            pltpu.VMEM((TRUNK_ROWS, HEAD), bf16),
            pltpu.VMEM((TRUNK_ROWS, HEAD), f32),
            pltpu.VMEM((TRUNK_ROWS, HEAD), f32),
            pltpu.VMEM((BRANCHES, BLK, HEAD), f32),
            pltpu.VMEM((BRANCHES, BLK, HEAD), f32),
        ],
        compiler_params=pltpu.CompilerParams(vmem_limit_bytes=VMEM_LIMIT),
        cost_estimate=pl.CostEstimate(
            flops=pairs * HEAD * 10, bytes_accessed=packed.size * 5, transcendentals=pairs
        ),
        name="attend_backward",
    )(order, packed, grads)


def norm_back(gradient, normed, inverse, gain_vec):
    weighted = gradient * gain_vec
    return inverse * (weighted - normed * jnp.mean(normed * weighted, axis=-1, keepdims=True))


def inverse_norm(values):
    return lax.rsqrt(jnp.mean(values * values, axis=-1, keepdims=True) + EPSILON)


def dot(left, right):
    return jnp.dot(left, right, preferred_element_type=f32)


def dot_nt(left, right):
    return lax.dot_general(left, right, (((1,), (1,)), ((), ())), preferred_element_type=f32)


def dot_tn(left, right):
    return lax.dot_general(left, right, (((0,), (0,)), ((), ())), preferred_element_type=f32)


def shards(
    layer_input,
    cotangent,
    w_query,
    w_key,
    w_value,
    w_output,
    w_gate,
    w_up,
    w_down,
    query_gain,
    key_gain,
    attn_gain,
    mlp_gain,
    slot_parent,
    slot_depth,
):
    dp_index = lax.axis_index("dp")
    tp_index = lax.axis_index("tensor")
    dp_count = lax.axis_size("dp")
    tp_count = lax.axis_size("tensor")
    rows = layer_input.shape[1]
    share = rows // tp_count
    width = w_query.shape[1]
    heads = width // HEAD
    hidden_width = w_gate.shape[1]
    items = heads * MB
    copies = dp_count // items

    def gather_rows(shard):
        return lax.all_gather(shard, "dp", axis=0, tiled=True)

    def scatter_rows(total):
        return lax.psum_scatter(
            total.astype(bf16), "dp", scatter_dimension=0, tiled=True
        ).astype(f32)

    def exchange(pieces):
        flat = pieces.reshape((items, -1, HEAD))
        if copies > 1:
            flat = jnp.tile(flat, (copies, 1, 1))
        return lax.all_to_all(flat, "dp", split_axis=0, concat_axis=0, tiled=True)

    def give_back(pieces):
        flat = pieces.reshape((dp_count, -1, HEAD))
        return lax.all_to_all(flat, "dp", split_axis=0, concat_axis=0, tiled=True)[:items]

    w_qkv = gather_rows(jnp.concatenate([w_query, w_key, w_value], axis=1))
    w_out_t = gather_rows(line_all_gather(jnp.transpose(w_output), tp_count))
    w_gate_up = gather_rows(jnp.concatenate([w_gate, w_up], axis=1))
    w_down_t = gather_rows(jnp.transpose(w_down))

    order = tree_order(slot_parent, slot_depth)
    my_batch = lax.rem(lax.rem(dp_index, items), MB)
    my_order = lax.dynamic_index_in_dim(order, my_batch, 0, keepdims=False)
    my_depth = lax.dynamic_slice_in_dim(slot_depth, dp_index * SEG_DEV, SEG_DEV, 1)
    cosines, sines = rope_tables(my_depth)

    tokens = layer_input.reshape(MB * rows, D)
    qk_raw = dot(tokens, w_qkv[:, : 2 * width])
    v_raw = dot(tokens, w_qkv[:, 2 * width :])
    squares = jnp.stack(
        [
            jnp.sum(jnp.square(qk_raw[:, :width]), axis=-1),
            jnp.sum(jnp.square(qk_raw[:, width:]), axis=-1),
        ]
    )
    squares = small_sum(squares, "tensor", tp_count)
    inverse = jnp.transpose(lax.rsqrt(squares / D + EPSILON)).reshape(MB, rows, 2)
    qk_raw = qk_raw.reshape(MB, rows, 2 * width)
    v_raw = v_raw.reshape(MB, rows, width)
    gains = jnp.concatenate([query_gain, key_gain])[None, :]
    packed = pack_heads(qk_raw, v_raw, inverse, gains, cosines, sines, heads)
    packed = exchange(packed).reshape(dp_count, 3, SEG_DEV, BLK, HEAD)

    attended = give_back(attend_forward(my_order, packed))
    attended = attended.reshape(heads, MB, rows, HEAD).transpose(1, 2, 0, 3)
    attended = attended.reshape(MB, rows, width)

    kept = []
    outputs = []
    for batch in range(MB):
        everything = line_all_gather(attended[batch], tp_count)
        attn_proj = dot_nt(everything, w_out_t)
        attn_inv = inverse_norm(attn_proj)
        hidden = layer_input[batch].astype(f32) + attn_proj * attn_inv * attn_gain
        hidden_low = hidden.astype(bf16)
        gate_pre = dot(hidden_low, w_gate_up[:, :hidden_width])
        up_pre = dot(hidden_low, w_gate_up[:, hidden_width:])
        act_low = (jax.nn.silu(gate_pre) * up_pre).astype(bf16)
        half = rows // 2
        sums = line_all_reduce(
            [
                dot_nt(act_low[:half], w_down_t).astype(bf16),
                dot_nt(act_low[half:], w_down_t).astype(bf16),
            ],
            tp_count,
        )
        mlp_proj = jnp.concatenate(sums, axis=0).astype(f32)
        mlp_inv = inverse_norm(mlp_proj)
        mlp_normed = mlp_proj * mlp_inv
        outputs.append((hidden + mlp_normed * mlp_gain).astype(bf16))
        out_grad = cotangent[batch]
        mlp_grad = norm_back(out_grad, mlp_normed, mlp_inv, mlp_gain).astype(bf16)
        mlp_gain_part = jnp.sum(out_grad * mlp_normed, axis=0)
        act_grad = dot(mlp_grad, w_down_t)
        sigmoid_gate = jax.nn.sigmoid(gate_pre)
        up_grad = (act_grad * gate_pre * sigmoid_gate).astype(bf16)
        gate_grad = (
            act_grad * up_pre * sigmoid_gate * (1.0 + gate_pre * (1.0 - sigmoid_gate))
        ).astype(bf16)
        branch_sums = line_all_reduce(
            [
                (
                    dot_nt(gate_grad[part], w_gate_up[:, :hidden_width])
                    + dot_nt(up_grad[part], w_gate_up[:, hidden_width:])
                ).astype(bf16)
                for part in (slice(0, half), slice(half, rows))
            ],
            tp_count,
        )
        hidden_grad = out_grad + jnp.concatenate(branch_sums, axis=0).astype(f32)
        attn_normed = attn_proj * attn_inv
        proj_grad = norm_back(hidden_grad, attn_normed, attn_inv, attn_gain).astype(bf16)
        attn_gain_part = jnp.sum(hidden_grad * attn_normed, axis=0)
        own_out_t = lax.dynamic_slice_in_dim(w_out_t, tp_index * width, width, 1)
        attn_grad = dot(proj_grad, own_out_t).astype(bf16)
        kept.append(
            dict(
                hidden_low=hidden_low,
                act_low=act_low,
                mlp_grad=mlp_grad,
                up_grad=up_grad,
                gate_grad=gate_grad,
                proj_grad=proj_grad,
                attn_grad=attn_grad,
                residual=lax.dynamic_slice_in_dim(hidden_grad, tp_index * share, share, 0),
                mlp_gain_part=mlp_gain_part,
                attn_gain_part=attn_gain_part,
            )
        )

    def both(name):
        return jnp.concatenate([part[name] for part in kept], axis=0)

    hidden_low = both("hidden_low")
    down_grad = scatter_rows(dot_tn(both("mlp_grad"), both("act_low")))
    gate_up_grad = scatter_rows(
        jnp.concatenate(
            [dot_tn(hidden_low, both("gate_grad")), dot_tn(hidden_low, both("up_grad"))], axis=1
        )
    )
    output_grad = scatter_rows(dot_tn(both("proj_grad"), attended.reshape(MB * rows, width)))

    attn_grad = jnp.stack([part["attn_grad"] for part in kept])
    attn_grad = attn_grad.reshape(MB, rows, heads, HEAD).transpose(2, 0, 1, 3)
    attn_grad = exchange(attn_grad).reshape(dp_count, SEG_DEV, BLK, HEAD)
    back = give_back(attend_backward(my_order, packed, attn_grad))
    back = back.reshape(heads, MB, 3, rows, HEAD)
    inner, gain_part = inner_sums(back, qk_raw, inverse, gains, cosines, sines, heads)
    means = small_sum(jnp.transpose(inner.reshape(-1, 2)), "tensor", tp_count) / D
    means = jnp.transpose(means).reshape(MB, rows, 2)
    qkv_grad = unpack_heads(back, qk_raw, inverse, means, gains, cosines, sines, heads)

    input_parts = []
    for batch in range(MB):
        term = dot_nt(qkv_grad[batch], w_qkv).astype(bf16)
        input_parts.append(kept[batch]["residual"] + line_reduce_scatter(term, tp_count))
    qkv_weight_grad = scatter_rows(dot_tn(tokens, qkv_grad.reshape(MB * rows, 3 * width)))

    gain_sums = jnp.concatenate(
        [
            gain_part[0],
            sum(part["attn_gain_part"] for part in kept),
            sum(part["mlp_gain_part"] for part in kept),
        ]
    )
    gain_sums = small_sum(gain_sums.reshape(-1, HEAD), "dp", dp_count).reshape(-1)
    return (
        jnp.stack(outputs),
        jnp.stack(input_parts),
        qkv_weight_grad[:, :width],
        qkv_weight_grad[:, width : 2 * width],
        qkv_weight_grad[:, 2 * width :],
        jnp.transpose(output_grad),
        gate_up_grad[:, :hidden_width],
        gate_up_grad[:, hidden_width:],
        jnp.transpose(down_grad),
        gain_sums[:width],
        gain_sums[width : 2 * width],
        gain_sums[2 * width : 2 * width + D],
        gain_sums[2 * width + D :],
    )


def solution(mesh):
    in_specs = (
        P(None, "dp", None),
        P(None, "dp", None),
        P("dp", "tensor"),
        P("dp", "tensor"),
        P("dp", "tensor"),
        P("tensor", "dp"),
        P("dp", "tensor"),
        P("dp", "tensor"),
        P("tensor", "dp"),
        P("tensor"),
        P("tensor"),
        P(),
        P(),
        P(),
        P(),
    )
    out_specs = (
        P(None, "dp", None),
        P(None, ("dp", "tensor"), None),
        P("dp", "tensor"),
        P("dp", "tensor"),
        P("dp", "tensor"),
        P("tensor", "dp"),
        P("dp", "tensor"),
        P("dp", "tensor"),
        P("tensor", "dp"),
        P("tensor"),
        P("tensor"),
        P(),
        P(),
    )
    return jax.shard_map(shards, mesh=mesh, in_specs=in_specs, out_specs=out_specs, check_vma=False)
```

```python
import functools

import jax
import jax.numpy as jnp
from jax import lax
from jax.experimental import pallas as pl
from jax.experimental.pallas import tpu as pltpu
from jax.sharding import PartitionSpec as P

D = 2048
HEADS = 16
HEAD = D // HEADS
BLK = 128
TRUNK = 8
BRANCHES = 4
LEAVES = 2
TREE_BLOCKS = 20
MB = 2
SEG_DEV = 5
PAIR = 2 * BLK
TRUNK_ROWS = TRUNK * BLK
TILE = 512
LONG = 1024

EPSILON = 1e-06
ROPE_BASE = 500000.0
SCALING = HEAD ** (-0.5)
VMEM_LIMIT = 50 * 1024 * 1024

f32 = jnp.float32
bf16 = jnp.bfloat16


def tree_order(parents, depths):
    blocks = parents.shape[1]
    ids = jnp.arange(blocks, dtype=jnp.int32)

    def follow(table, index):
        hot = index[:, :, None] == ids[None, None, :]
        return jnp.sum(jnp.where(hot, table[:, None, :], 0), axis=-1)

    up2 = follow(parents, parents)
    up4 = follow(up2, up2)
    up8 = follow(up4, up4)
    root = follow(up8, up8)
    is_leaf = depths == TRUNK + 1
    above = jnp.where(is_leaf, parents, 0)
    key = ((root * (TRUNK + 2) + depths) * blocks + above) * blocks + ids[None, :]
    rank = jnp.sum((key[:, None, :] < key[:, :, None]).astype(jnp.int32), axis=-1)
    return jnp.sum(
        jnp.where(rank[:, None, :] == ids[None, :, None], ids[None, None, :], 0), axis=-1
    ).astype(jnp.int32)


def rope_tables(depths):
    half = HEAD // 2
    offsets = jnp.arange(BLK, dtype=jnp.int32)
    places = (depths[:, :, None] * BLK + offsets).reshape(depths.shape[0], -1).astype(f32)
    frequency = ROPE_BASE ** (-2.0 * jnp.arange(half, dtype=f32) / HEAD)
    angles = places[:, :, None] * frequency
    cosines = jnp.cos(angles)
    sines = jnp.sin(angles)
    return (
        jnp.concatenate([cosines, cosines], -1),
        jnp.concatenate([-sines, sines], -1),
    )


def low_sum(*parts):
    total = parts[0].astype(f32)
    for part in parts[1:]:
        total = total + part.astype(f32)
    return total.astype(bf16)


def follow(values, after):
    if after is None:
        return values
    return lax.optimization_barrier((values, after))[0]


def small_sum(values, axis, count):
    step = 1
    while step < count:
        values = values + lax.ppermute(values, axis, [(i, i ^ step) for i in range(count)])
        step *= 2
    return values


class SumLine:
    def __init__(self, count):
        self.count = count
        index = lax.axis_index("tensor")
        self.inner = (index == 1) | (index == 2)
        self.terms = []
        self.inward = []
        self.sides = []
        self.across = []
        self.totals = []
        self.outward = []
        self.sums = []

    def enter(self, term):
        if self.count != 4:
            self.sums.append(lax.psum(term, "tensor"))
            return
        self.terms.append(term)
        self.inward.append(lax.ppermute(term, "tensor", [(0, 1), (3, 2)]))

    def advance(self, after):
        if self.count != 4:
            return []
        moved = []
        if len(self.sides) < len(self.terms):
            at = len(self.sides)
            side = low_sum(follow(self.terms[at], after), self.inward[at])
            self.sides.append(side)
            moved.append(side)
        at = len(self.totals)
        if at < len(self.sides) - 1 or (at < len(self.sides) and not moved):
            total = low_sum(follow(self.sides[at], after), self.across[at])
            self.totals.append(total)
            moved.append(total)
        at = len(self.sums)
        if at < len(self.outward):
            self.sums.append(
                jnp.where(self.inner, follow(self.totals[at], after), self.outward[at])
            )
        if len(self.across) < len(self.sides):
            self.across.append(lax.ppermute(self.sides[-1], "tensor", [(1, 2), (2, 1)]))
        if len(self.outward) < len(self.totals):
            self.outward.append(lax.ppermute(self.totals[-1], "tensor", [(1, 0), (2, 3)]))
        return moved


def line_reduce_scatter(batches, count, late):
    if count != 4:
        return [
            lax.psum_scatter(values, "tensor", scatter_dimension=0, tiled=True).astype(f32)
            for values in batches
        ], None
    index = lax.axis_index("tensor")
    rights = []
    lefts = []
    blocks = [item.reshape(count, item.shape[0] // count, item.shape[1]) for item in batches]

    def block(item, at):
        return lax.dynamic_index_in_dim(item, lax.rem(at + 2 * count, count), 0, keepdims=False)

    operands = []
    for stage in range(count - 1):
        to_right = [(i, i + 1) for i in range(stage + 1)]
        to_left = [(count - 1 - i, count - 2 - i) for i in range(stage + 1)]
        for at, item in enumerate(blocks):
            right = block(item, index + count - 1 - stage)
            left = block(item, index - count + 1 + stage)
            if stage:
                right = low_sum(right, rights[at])
                left = low_sum(left, lefts[at])
                if stage == count - 2 and at == len(blocks) - 1:
                    right, left = follow((right, left), late)
                rights[at] = lax.ppermute(right, "tensor", to_right)
                lefts[at] = lax.ppermute(left, "tensor", to_left)
            else:
                rights.append(lax.ppermute(right, "tensor", to_right))
                lefts.append(lax.ppermute(left, "tensor", to_left))
            operands.append((right, left))
    sums = [
        block(item, index).astype(f32) + right.astype(f32) + left.astype(f32)
        for item, right, left in zip(blocks, rights, lefts)
    ]
    return sums, operands[-1]


def begin_all_gather(values, count):
    if count != 4:
        return values, (None,) * 4
    right1 = lax.ppermute(values, "tensor", [(0, 1), (1, 2), (2, 3)])
    left1 = lax.ppermute(values, "tensor", [(3, 2), (2, 1), (1, 0)])
    right2 = lax.ppermute(right1, "tensor", [(1, 2), (2, 3)])
    left2 = lax.ppermute(left1, "tensor", [(2, 1), (1, 0)])
    return values, (right1, left1, right2, left2)


def end_all_gather(begun, count, after=None):
    values, (right1, left1, right2, left2) = begun
    if count != 4:
        return lax.all_gather(values, "tensor", axis=1, tiled=True)
    index = lax.axis_index("tensor")
    width = values.shape[1]
    right3 = lax.ppermute(follow(right2, after), "tensor", [(2, 3)])
    left3 = lax.ppermute(follow(left2, after), "tensor", [(1, 0)])
    whole = jnp.zeros((values.shape[0], count * width), values.dtype)
    pieces = (
        values,
        jnp.where(index >= 1, right1, left3),
        jnp.where(index >= 2, right2, left2),
        jnp.where(index >= 3, right3, left1),
    )
    for back, piece in enumerate(pieces):
        place = lax.rem(index - back + count, count) * width
        whole = lax.dynamic_update_slice(whole, piece, (0, place))
    return whole


def line_all_gather(values, count):
    return end_all_gather(begin_all_gather(values, count), count)


def begin_output_weight(own, after, dp_index, dp_count, count):
    if count != 4 or dp_count % 2:
        return own, (None,) * 4
    half = own.shape[0] // 2
    mine = lax.dynamic_slice_in_dim(follow(own, after), lax.rem(dp_index, 2) * half, half, 0)
    return begin_all_gather(mine, count)


def end_output_weight(begun, after, dp_index, dp_count, count):
    if count != 4 or dp_count % 2:
        whole = lax.all_gather(begun[0], "tensor", axis=1, tiled=True)
        half = whole.shape[0] // 2
        return jnp.zeros((1,), jnp.int32), whole[:half], whole[half:]
    mine = end_all_gather(begun, count, after)
    other = lax.ppermute(mine, "dp", [(i, i ^ 1) for i in range(dp_count)])
    return lax.rem(dp_index, 2).astype(jnp.int32).reshape(1), mine, other


def turn(values, cosines, sines):
    return values * cosines + pltpu.roll(values, HEAD // 2, 1) * sines


def head_cols(head, group=0, heads=0):
    start = (group * heads + head) * HEAD
    return slice(start, start + HEAD)


def project_kernel(x_ref, *refs):
    count = len(refs) // 2 if len(refs) > 2 else 1
    weights, outs = refs[:count], refs[count:]
    for at in range(count):
        raw = jnp.dot(x_ref[0], weights[at][0], preferred_element_type=f32)
        outs[at][0] = raw.astype(outs[at].dtype)
        if len(outs) > count:
            outs[count][0, :, at : at + 1] = jnp.sum(raw * raw, axis=1, keepdims=True)


def project(tokens, weights, which, squares):
    batches, rows, _ = tokens.shape
    width = weights.shape[2]
    step = rows // 2
    dtype = f32 if squares else bf16
    out_specs = [pl.BlockSpec((1, step, width), lambda b, r: (b, r, 0))] * len(which)
    out_shape = [jax.ShapeDtypeStruct((batches, rows, width), dtype)] * len(which)
    if squares:
        out_specs.append(pl.BlockSpec((1, step, len(which)), lambda b, r: (b, r, 0)))
        out_shape.append(jax.ShapeDtypeStruct((batches, rows, len(which)), f32))
    return pl.pallas_call(
        project_kernel,
        grid=(batches, rows // step),
        in_specs=[pl.BlockSpec((1, step, D), lambda b, r: (b, r, 0))]
        + [pl.BlockSpec((1, D, width), lambda b, r, at=at: (at, 0, 0)) for at in which],
        out_specs=out_specs,
        out_shape=out_shape,
        compiler_params=pltpu.CompilerParams(vmem_limit_bytes=VMEM_LIMIT),
        cost_estimate=pl.CostEstimate(
            flops=2 * batches * rows * D * width * len(which),
            bytes_accessed=2 * batches * rows * D + 2 * D * width * len(which),
            transcendentals=0,
        ),
        name="project",
    )(tokens, *([weights] * len(which)))


def pack_kernel(heads, q_ref, k_ref, v_ref, inv_ref, gain_ref, cos_ref, sin_ref, out_ref):
    cosines = cos_ref[0]
    sines = sin_ref[0]
    for head in range(heads):
        for which in range(2):
            cols = head_cols(head, which, heads)
            raw_ref = (q_ref, k_ref)[which]
            normed = raw_ref[0, :, head_cols(head)] * inv_ref[0, :, which : which + 1] * gain_ref[:, cols]
            out_ref[head, 0, which] = turn(normed, cosines, sines).astype(bf16)
        out_ref[head, 0, 2] = v_ref[0, :, head_cols(head)]


def pack_heads(q_raw, k_raw, v_raw, inverse, gains, cosines, sines, heads):
    rows = q_raw.shape[1]
    step = rows // 2
    width = heads * HEAD
    return pl.pallas_call(
        functools.partial(pack_kernel, heads),
        grid=(MB, rows // step),
        in_specs=[
            pl.BlockSpec((1, step, width), lambda b, r: (b, r, 0)),
            pl.BlockSpec((1, step, width), lambda b, r: (b, r, 0)),
            pl.BlockSpec((1, step, width), lambda b, r: (b, r, 0)),
            pl.BlockSpec((1, step, 2), lambda b, r: (b, r, 0)),
            pl.BlockSpec((1, 2 * width), lambda b, r: (0, 0)),
            pl.BlockSpec((1, step, HEAD), lambda b, r: (b, r, 0)),
            pl.BlockSpec((1, step, HEAD), lambda b, r: (b, r, 0)),
        ],
        out_specs=pl.BlockSpec((heads, 1, 3, step, HEAD), lambda b, r: (0, b, 0, r, 0)),
        out_shape=jax.ShapeDtypeStruct((heads, MB, 3, rows, HEAD), bf16),
        name="pack_heads",
    )(q_raw, k_raw, v_raw, inverse, gains, cosines, sines)


def inner_kernel(heads, back_ref, q_ref, k_ref, inv_ref, gain_ref, cos_ref, sin_ref, inner_ref, part_ref):
    cosines = cos_ref[0]
    sines = -sin_ref[0]

    @pl.when((pl.program_id(0) == 0) & (pl.program_id(1) == 0))
    def _():
        part_ref[...] = jnp.zeros_like(part_ref)

    for which in range(2):
        total = None
        for head in range(heads):
            cols = head_cols(head, which, heads)
            straight = turn(back_ref[head, 0, which].astype(f32), cosines, sines)
            hat = (q_ref, k_ref)[which][0, :, head_cols(head)] * inv_ref[0, :, which : which + 1]
            product = straight * hat
            part_ref[:, cols] += jnp.sum(product, axis=0, keepdims=True)
            weighted = product * gain_ref[:, cols]
            total = weighted if total is None else total + weighted
        inner_ref[0, :, which : which + 1] = jnp.sum(total, axis=1, keepdims=True)


def inner_sums(back, q_raw, k_raw, inverse, gains, cosines, sines, heads):
    rows = q_raw.shape[1]
    step = rows // 2
    width = heads * HEAD
    return pl.pallas_call(
        functools.partial(inner_kernel, heads),
        grid=(MB, rows // step),
        in_specs=[
            pl.BlockSpec((heads, 1, 2, step, HEAD), lambda b, r: (0, b, 0, r, 0)),
            pl.BlockSpec((1, step, width), lambda b, r: (b, r, 0)),
            pl.BlockSpec((1, step, width), lambda b, r: (b, r, 0)),
            pl.BlockSpec((1, step, 2), lambda b, r: (b, r, 0)),
            pl.BlockSpec((1, 2 * width), lambda b, r: (0, 0)),
            pl.BlockSpec((1, step, HEAD), lambda b, r: (b, r, 0)),
            pl.BlockSpec((1, step, HEAD), lambda b, r: (b, r, 0)),
        ],
        out_specs=[
            pl.BlockSpec((1, step, 2), lambda b, r: (b, r, 0)),
            pl.BlockSpec((1, 2 * width), lambda b, r: (0, 0)),
        ],
        out_shape=[
            jax.ShapeDtypeStruct((MB, rows, 2), f32),
            jax.ShapeDtypeStruct((1, 2 * width), f32),
        ],
        name="inner_sums",
    )(back, q_raw, k_raw, inverse, gains, cosines, sines)


def unpack_kernel(
    heads,
    back_ref,
    q_ref,
    k_ref,
    inv_ref,
    mean_ref,
    gain_ref,
    cos_ref,
    sin_ref,
    wq_ref,
    wk_ref,
    wv_ref,
    grad_ref,
    term_ref,
):
    cosines = cos_ref[0]
    sines = -sin_ref[0]
    width = heads * HEAD
    for head in range(heads):
        for which in range(2):
            cols = head_cols(head, which, heads)
            inverse = inv_ref[0, :, which : which + 1]
            straight = turn(back_ref[head, 0, which].astype(f32), cosines, sines)
            hat = (q_ref, k_ref)[which][0, :, head_cols(head)] * inverse
            grad = inverse * (straight * gain_ref[:, cols] - hat * mean_ref[0, :, which : which + 1])
            grad_ref[:, cols] = grad.astype(bf16)
        grad_ref[:, head_cols(head, 2, heads)] = back_ref[head, 0, 2]
    term = nt(grad_ref[:, :width], wq_ref[0])
    term = term + nt(grad_ref[:, width : 2 * width], wk_ref[0])
    term = term + nt(grad_ref[:, 2 * width :], wv_ref[0])
    term_ref[...] = term.astype(bf16)


def unpack_heads(
    batch, back, q_raw, k_raw, inverse, means, gains, cosines, sines, weights, heads, kept
):
    rows = q_raw.shape[1]
    step = rows // 2
    width = heads * HEAD
    row_spec = lambda cols: pl.BlockSpec((1, step, cols), lambda r: (batch, r, 0))
    return chunk_call(
        functools.partial(unpack_kernel, heads),
        [
            (pl.BlockSpec((heads, 1, 3, step, HEAD), lambda r: (0, batch, 0, r, 0)), back),
            (row_spec(width), q_raw),
            (row_spec(width), k_raw),
            (row_spec(2), inverse),
            (row_spec(2), means),
            (pl.BlockSpec((1, 2 * width), lambda r: (0, 0)), gains),
            (row_spec(HEAD), cosines),
            (row_spec(HEAD), sines),
        ]
        + [(pl.BlockSpec((1, D, width), lambda r, at=at: (at, 0, 0)), weights) for at in range(3)],
        [
            (
                pl.BlockSpec((step, 3 * width), lambda r: (batch * 2 + r, 0)),
                jax.ShapeDtypeStruct((MB * rows, 3 * width), bf16),
                True,
            ),
            (
                pl.BlockSpec((step, D), lambda r: (r, 0)),
                jax.ShapeDtypeStruct((rows, D), bf16),
                False,
            ),
        ],
        kept,
        (2,),
        [],
        pl.CostEstimate(flops=6 * rows * D * width, bytes_accessed=8 * rows * D, transcendentals=0),
        "unpack_heads",
    )


def nt(left, right):
    return lax.dot_general(left, right, (((1,), (1,)), ((), ())), preferred_element_type=f32)


def nn(left, right):
    return lax.dot_general(left, right, (((1,), (0,)), ((), ())), preferred_element_type=f32)


def key_query_iotas(keys):
    key_at = lax.broadcasted_iota(jnp.int32, (keys, PAIR), 0)
    query_at = lax.broadcasted_iota(jnp.int32, (keys, PAIR), 1)
    return key_at, query_at


def causal_mask():
    key_at, query_at = key_query_iotas(PAIR)
    return key_at <= query_at


def apart_mask(above):
    key_at, query_at = key_query_iotas(above + PAIR)
    key_at = key_at - above
    own = (key_at <= query_at) & ((key_at < BLK) == (query_at < BLK))
    return own | (key_at < 0)


def softmax_parts(queries, trunk_keys, near_keys, mask):
    near = jnp.where(mask, nt(near_keys, queries), -1e30)
    top = jnp.max(near, axis=0, keepdims=True)
    if trunk_keys is None:
        near = jnp.exp((near - top) * SCALING)
        scale = 1.0 / jnp.sum(near, axis=0, keepdims=True)
        return None, near * scale
    far = nt(trunk_keys, queries)
    top = jnp.maximum(top, jnp.max(far, axis=0, keepdims=True))
    near = jnp.exp((near - top) * SCALING)
    far = jnp.exp((far - top) * SCALING)
    scale = 1.0 / (jnp.sum(near, axis=0, keepdims=True) + jnp.sum(far, axis=0, keepdims=True))
    return far * scale, near * scale


def places(order_ref, tree):
    def at(within):
        slot = order_ref[tree * TREE_BLOCKS + within]
        return lax.div(slot, SEG_DEV), lax.rem(slot, SEG_DEV)

    return at


def load(ref, which, *spots):
    parts = [ref[group, which, row] for group, row in spots]
    return parts[0] if len(parts) == 1 else jnp.concatenate(parts, axis=0)


def across(values):
    return jnp.transpose(values.astype(f32)).astype(bf16)


def forward_kernel(trees, order_ref, x_ref, y_ref, k_ref, vt_ref):
    def one_tree(tree, carry):
        at = places(order_ref, tree)
        for within in range(TRUNK):
            rows = slice(within * BLK, (within + 1) * BLK)
            spot = at(within)
            k_ref[rows, :] = load(x_ref, 1, spot)
            vt_ref[:, rows] = across(load(x_ref, 2, spot))

        def attend(spots, far_rows, near_keys, near_values, mask):
            queries = load(x_ref, 0, *spots)
            far, near = softmax_parts(
                queries, k_ref[:far_rows, :] if far_rows else None, near_keys, mask
            )
            summed = nn(across(near_values), near.astype(bf16))
            if far_rows:
                summed = summed + nn(vt_ref[:, :far_rows], far.astype(bf16))
            rows = jnp.transpose(summed).astype(bf16)
            y_ref[spots[0][0], spots[0][1]] = rows[:BLK]
            y_ref[spots[1][0], spots[1][1]] = rows[BLK:]

        causal = causal_mask()
        for pair in range(TRUNK // 2):
            spots = (at(2 * pair), at(2 * pair + 1))
            attend(spots, pair * PAIR, load(x_ref, 1, *spots), load(x_ref, 2, *spots), causal)
        apart = apart_mask(0)
        for pair in range(BRANCHES // 2):
            spots = (at(TRUNK + 2 * pair), at(TRUNK + 2 * pair + 1))
            attend(spots, TRUNK_ROWS, load(x_ref, 1, *spots), load(x_ref, 2, *spots), apart)
        under = apart_mask(BLK)
        for branch in range(BRANCHES):
            first = TRUNK + BRANCHES + LEAVES * branch
            spots = (at(first), at(first + 1))
            near = (at(TRUNK + branch),) + spots
            attend(spots, TRUNK_ROWS, load(x_ref, 1, *near), load(x_ref, 2, *near), under)
        return carry

    lax.fori_loop(0, trees, one_tree, 0)


def attend_forward(order, packed):
    groups = packed.shape[0]
    blocks = packed.shape[2]
    trees = groups * blocks // TREE_BLOCKS
    pairs = trees * TREE_BLOCKS * BLK * 1100
    return pl.pallas_call(
        functools.partial(forward_kernel, trees),
        in_specs=[
            pl.BlockSpec(memory_space=pltpu.SMEM),
            pl.BlockSpec(memory_space=pltpu.VMEM),
        ],
        out_specs=pl.BlockSpec(memory_space=pltpu.VMEM),
        out_shape=jax.ShapeDtypeStruct((groups, blocks, BLK, HEAD), bf16),
        scratch_shapes=[
            pltpu.VMEM((TRUNK_ROWS, HEAD), bf16),
            pltpu.VMEM((HEAD, TRUNK_ROWS), bf16),
        ],
        compiler_params=pltpu.CompilerParams(vmem_limit_bytes=VMEM_LIMIT),
        cost_estimate=pl.CostEstimate(
            flops=pairs * HEAD * 4, bytes_accessed=packed.size * 3, transcendentals=pairs
        ),
        name="attend_forward",
    )(order, packed)


def backward_kernel(
    trees, order_ref, x_ref, dy_ref, out_ref, k_ref, kt_ref, v_ref, dk_ref, dv_ref, dkb_ref, dvb_ref
):
    def one_tree(tree, carry):
        at = places(order_ref, tree)
        for within in range(TRUNK):
            rows = slice(within * BLK, (within + 1) * BLK)
            spot = at(within)
            keys = load(x_ref, 1, spot)
            k_ref[rows, :] = keys
            kt_ref[:, rows] = across(keys)
            v_ref[rows, :] = load(x_ref, 2, spot)

        def attend(spots, far_rows, near_spots, mask, start):
            queries = load(x_ref, 0, *spots)
            grads = jnp.concatenate(
                [dy_ref[spots[0][0], spots[0][1]], dy_ref[spots[1][0], spots[1][1]]], axis=0
            )
            near_keys = load(x_ref, 1, *near_spots)
            near_values = load(x_ref, 2, *near_spots)
            far, near = softmax_parts(
                queries, k_ref[:far_rows, :] if far_rows else None, near_keys, mask
            )
            near_grad = nt(near_values, grads)
            inner = jnp.sum(near * near_grad, axis=0, keepdims=True)
            if far_rows:
                far_grad = nt(v_ref[:far_rows, :], grads)
                inner = inner + jnp.sum(far * far_grad, axis=0, keepdims=True)
                far_score = (far * (far_grad - inner)).astype(bf16)
                far_dk = nn(far_score, queries)
                far_dv = nn(far.astype(bf16), grads)
                if start:
                    dk_ref[:far_rows, :] = far_dk
                    dv_ref[:far_rows, :] = far_dv
                else:
                    dk_ref[:far_rows, :] += far_dk
                    dv_ref[:far_rows, :] += far_dv
            near_score = (near * (near_grad - inner)).astype(bf16)
            turned = nn(across(near_keys), near_score)
            if far_rows:
                turned = turned + nn(kt_ref[:, :far_rows], far_score)
            rows = (jnp.transpose(turned) * SCALING).astype(bf16)
            out_ref[spots[0][0], 0, spots[0][1]] = rows[:BLK]
            out_ref[spots[1][0], 0, spots[1][1]] = rows[BLK:]
            return nn(near_score, queries), nn(near.astype(bf16), grads)

        def store(spot, key_grad, value_grad):
            out_ref[spot[0], 1, spot[1]] = (key_grad * SCALING).astype(bf16)
            out_ref[spot[0], 2, spot[1]] = value_grad.astype(bf16)

        under = apart_mask(BLK)
        for branch in range(BRANCHES):
            first = TRUNK + BRANCHES + LEAVES * branch
            spots = (at(first), at(first + 1))
            key_grad, value_grad = attend(
                spots, TRUNK_ROWS, (at(TRUNK + branch),) + spots, under, branch == 0
            )
            dkb_ref[branch] = key_grad[:BLK]
            dvb_ref[branch] = value_grad[:BLK]
            store(spots[0], key_grad[BLK : 2 * BLK], value_grad[BLK : 2 * BLK])
            store(spots[1], key_grad[2 * BLK :], value_grad[2 * BLK :])
        apart = apart_mask(0)
        for pair in range(BRANCHES // 2):
            spots = (at(TRUNK + 2 * pair), at(TRUNK + 2 * pair + 1))
            key_grad, value_grad = attend(spots, TRUNK_ROWS, spots, apart, False)
            for half in range(2):
                rows = slice(half * BLK, (half + 1) * BLK)
                branch = 2 * pair + half
                store(
                    spots[half], key_grad[rows] + dkb_ref[branch], value_grad[rows] + dvb_ref[branch]
                )
        causal = causal_mask()
        for pair in reversed(range(TRUNK // 2)):
            spots = (at(2 * pair), at(2 * pair + 1))
            key_grad, value_grad = attend(spots, pair * PAIR, spots, causal, False)
            for half in range(2):
                rows = slice(half * BLK, (half + 1) * BLK)
                held = slice(pair * PAIR + half * BLK, pair * PAIR + (half + 1) * BLK)
                store(
                    spots[half],
                    key_grad[rows] + dk_ref[held, :],
                    value_grad[rows] + dv_ref[held, :],
                )
        return carry

    lax.fori_loop(0, trees, one_tree, 0)


def attend_backward(order, packed, grads):
    groups = packed.shape[0]
    blocks = packed.shape[2]
    trees = groups * blocks // TREE_BLOCKS
    pairs = trees * TREE_BLOCKS * BLK * 1100
    return pl.pallas_call(
        functools.partial(backward_kernel, trees),
        in_specs=[
            pl.BlockSpec(memory_space=pltpu.SMEM),
            pl.BlockSpec(memory_space=pltpu.VMEM),
            pl.BlockSpec(memory_space=pltpu.VMEM),
        ],
        out_specs=pl.BlockSpec(memory_space=pltpu.VMEM),
        out_shape=jax.ShapeDtypeStruct(packed.shape, bf16),
        scratch_shapes=[
            pltpu.VMEM((TRUNK_ROWS, HEAD), bf16),
            pltpu.VMEM((HEAD, TRUNK_ROWS), bf16),
            pltpu.VMEM((TRUNK_ROWS, HEAD), bf16),
            pltpu.VMEM((TRUNK_ROWS, HEAD), f32),
            pltpu.VMEM((TRUNK_ROWS, HEAD), f32),
            pltpu.VMEM((BRANCHES, BLK, HEAD), f32),
            pltpu.VMEM((BRANCHES, BLK, HEAD), f32),
        ],
        compiler_params=pltpu.CompilerParams(vmem_limit_bytes=VMEM_LIMIT),
        cost_estimate=pl.CostEstimate(
            flops=pairs * HEAD * 10, bytes_accessed=packed.size * 5, transcendentals=pairs
        ),
        name="attend_backward",
    )(order, packed, grads)


def mean_square(values):
    return jnp.mean(values * values, axis=-1, keepdims=True)


def norm_back(gradient, normed, inverse, gain_vec):
    weighted = gradient * gain_vec
    return inverse * (weighted - normed * jnp.mean(normed * weighted, axis=-1, keepdims=True))


def chunk_call(kernel, ins, outs, kept, grid, scratch, cost, name):
    count = len(ins)
    specs = [spec for spec, _ in ins]
    values = [value for _, value in ins]
    aliases = {}
    if kept is not None:
        whole = [at for at, out in enumerate(outs) if out[2]]
        for at, value in zip(whole, kept):
            aliases[len(values)] = at
            specs.append(pl.BlockSpec(memory_space=pl.ANY))
            values.append(value)
    extra = len(values) - count

    def body(*refs):
        kernel(*refs[:count], *refs[count + extra :])

    return pl.pallas_call(
        body,
        grid=grid,
        in_specs=specs,
        out_specs=[out[0] for out in outs],
        out_shape=[out[1] for out in outs],
        scratch_shapes=scratch,
        input_output_aliases=aliases,
        compiler_params=pltpu.CompilerParams(vmem_limit_bytes=VMEM_LIMIT),
        cost_estimate=cost,
        name=name,
    )(*values)


def clip(step, low, count):
    return jnp.minimum(jnp.maximum(step - low, 0), count - 1)


def forward_chunk_kernel(
    first,
    second,
    core_ref,
    y_ref,
    x_ref,
    gain_ref,
    woa_ref,
    wob_ref,
    wg_ref,
    wu_ref,
    wd_ref,
    proj_ref,
    low_ref,
    act_ref,
    silu_ref,
    slope_ref,
    part_ref,
    exact_ref,
    held_ref,
):
    step = pl.program_id(0)
    half = first // 2

    def project_tile(weight_ref, side):
        at = side * half + lax.rem(step, half)
        columns = pl.ds(pl.multiple_of(at * LONG, LONG), LONG)
        exact_ref[:, columns] = nt(y_ref[...], weight_ref[...])

    @pl.when(step < half)
    def _():
        project_tile(woa_ref, core_ref[0])

    @pl.when((step >= half) & (step < first))
    def _():
        project_tile(wob_ref, 1 - core_ref[0])

    @pl.when(step == first)
    def _():
        proj = exact_ref[...]
        inverse = lax.rsqrt(mean_square(proj) + EPSILON)
        proj_ref[...] = proj.astype(bf16)
        low_ref[...] = (x_ref[...].astype(f32) + proj * inverse * gain_ref[...]).astype(bf16)

    @pl.when((step >= first) & (step < second))
    def _():
        low = low_ref[...]
        gate = nn(low, wg_ref[...])
        up = nn(low, wu_ref[...])
        sigmoid = 1.0 / (1.0 + jnp.exp(-gate))
        silu = gate * sigmoid
        act = (silu * up).astype(bf16)
        act_ref[...] = act
        held_ref[:, pl.ds(pl.multiple_of((step - first) * TILE, TILE), TILE)] = act
        silu_ref[...] = silu.astype(bf16)
        slope_ref[...] = (up * sigmoid * (1.0 + gate * (1.0 - sigmoid))).astype(bf16)

    @pl.when(step >= second)
    def _():
        part_ref[...] = nt(held_ref[...], wd_ref[...]).astype(bf16)


def forward_chunk(at, batch, part, rows, y_all, tokens, gain, w_out, w_mlp, kept):
    core, w_out_a, w_out_b = w_out
    w_gate, w_rest = w_mlp
    units = w_gate.shape[2]
    total = tokens.shape[0] * tokens.shape[1]
    tiles = D // LONG
    unit_tiles = units // TILE
    first = tiles
    second = first + unit_tiles
    half = first // 2
    unit_tile = pl.BlockSpec((rows, TILE), lambda s: (at, clip(s, first, unit_tiles)))
    wide = jax.ShapeDtypeStruct((total, units), bf16)
    narrow = jax.ShapeDtypeStruct((total, D), bf16)
    whole = pl.BlockSpec((rows, D), lambda s: (at, 0))

    def weight(which):
        return pl.BlockSpec((None, D, TILE), lambda s: (which, 0, clip(s, first, unit_tiles)))

    return chunk_call(
        functools.partial(forward_chunk_kernel, first, second),
        [
            (pl.BlockSpec(memory_space=pltpu.SMEM), core),
            (pl.BlockSpec((rows, D), lambda s: (part, 0)), y_all),
            (pl.BlockSpec((None, rows, D), lambda s: (batch, part, 0)), tokens),
            (pl.BlockSpec((1, D), lambda s: (0, 0)), gain),
            (pl.BlockSpec((LONG, D), lambda s: (clip(s, 0, half), 0)), w_out_a),
            (pl.BlockSpec((LONG, D), lambda s: (clip(s, half, half), 0)), w_out_b),
            (weight(0), w_gate),
            (weight(0), w_rest),
            (pl.BlockSpec((None, LONG, units), lambda s: (1, clip(s, second, tiles), 0)), w_rest),
        ],
        [
            (whole, narrow, True),
            (whole, narrow, True),
            (unit_tile, wide, True),
            (unit_tile, wide, True),
            (unit_tile, wide, True),
            (
                pl.BlockSpec((rows, LONG), lambda s: (0, clip(s, second, tiles))),
                jax.ShapeDtypeStruct((rows, D), bf16),
                False,
            ),
        ],
        kept,
        (second + tiles,),
        [pltpu.VMEM((rows, D), f32), pltpu.VMEM((rows, units), bf16)],
        pl.CostEstimate(
            flops=2 * rows * D * (D + 3 * units),
            bytes_accessed=2 * D * (D + 3 * units) + 16 * rows * D,
            transcendentals=rows * units,
        ),
        "forward_chunk",
    )


def middle_chunk_kernel(
    first,
    sum_ref,
    proj_ref,
    x_ref,
    grad_ref,
    attn_gain_ref,
    gain_ref,
    silu_ref,
    slope_ref,
    wd_ref,
    wg_ref,
    wu_ref,
    output_ref,
    low_ref,
    gate_ref,
    up_ref,
    gain_part_ref,
    part_ref,
    gates_ref,
    ups_ref,
):
    step = pl.program_id(0)

    @pl.when(step == 0)
    def _():
        proj = proj_ref[...].astype(f32)
        inverse = lax.rsqrt(mean_square(proj) + EPSILON)
        hidden = x_ref[...].astype(f32) + proj * inverse * attn_gain_ref[...]
        mlp = sum_ref[...].astype(f32)
        inverse = lax.rsqrt(mean_square(mlp) + EPSILON)
        normed = mlp * inverse
        grad = grad_ref[...]
        output_ref[...] = (hidden + normed * gain_ref[...]).astype(bf16)
        gain_part_ref[...] = jnp.sum(grad * normed, axis=0, keepdims=True)
        low_ref[...] = norm_back(grad, normed, inverse, gain_ref[...]).astype(bf16)

    @pl.when(step < first)
    def _():
        act_grad = nn(low_ref[...], wd_ref[...])
        up_grad = (act_grad * silu_ref[...].astype(f32)).astype(bf16)
        gate_grad = (act_grad * slope_ref[...].astype(f32)).astype(bf16)
        columns = pl.ds(pl.multiple_of(step * TILE, TILE), TILE)
        up_ref[...] = up_grad
        ups_ref[:, columns] = up_grad
        gate_ref[...] = gate_grad
        gates_ref[:, columns] = gate_grad

    @pl.when(step >= first)
    def _():
        part_ref[...] = (
            nt(gates_ref[...], wg_ref[...]) + nt(ups_ref[...], wu_ref[...])
        ).astype(bf16)


def middle_chunk(
    at, batch, part, rows, mlp_sum, proj, tokens, grad, attn_gain, gain, silu, slope, w_mlp, kept
):
    w_gate, w_rest = w_mlp
    units = w_gate.shape[2]
    total = proj.shape[0]
    tiles = D // LONG
    first = units // TILE
    whole = pl.BlockSpec((rows, D), lambda s: (at, 0))
    row_block = pl.BlockSpec((None, rows, D), lambda s: (batch, part, 0))
    line = pl.BlockSpec((1, D), lambda s: (0, 0))
    tile = pl.BlockSpec((rows, TILE), lambda s: (at, clip(s, 0, first)))
    wide = jax.ShapeDtypeStruct((total, units), bf16)
    narrow = jax.ShapeDtypeStruct((total, D), bf16)

    def weight(which):
        return pl.BlockSpec((None, LONG, units), lambda s: (which, clip(s, first, tiles), 0))

    return chunk_call(
        functools.partial(middle_chunk_kernel, first),
        [
            (pl.BlockSpec((rows, D), lambda s: (0, 0)), mlp_sum),
            (whole, proj),
            (row_block, tokens),
            (row_block, grad),
            (line, attn_gain),
            (line, gain),
            (tile, silu),
            (tile, slope),
            (pl.BlockSpec((None, D, TILE), lambda s: (1, 0, clip(s, 0, first))), w_rest),
            (weight(0), w_gate),
            (weight(0), w_rest),
        ],
        [
            (whole, narrow, True),
            (whole, narrow, True),
            (tile, wide, True),
            (tile, wide, True),
            (line, jax.ShapeDtypeStruct((1, D), f32), False),
            (
                pl.BlockSpec((rows, LONG), lambda s: (0, clip(s, first, tiles))),
                jax.ShapeDtypeStruct((rows, D), bf16),
                False,
            ),
        ],
        kept,
        (first + tiles,),
        [pltpu.VMEM((rows, units), bf16), pltpu.VMEM((rows, units), bf16)],
        pl.CostEstimate(
            flops=2 * rows * D * 3 * units,
            bytes_accessed=2 * D * 3 * units + 24 * rows * D,
            transcendentals=rows,
        ),
        "middle_chunk",
    )


def backward_chunk_kernel(
    heads, sum_ref, grad_ref, proj_ref, gain_ref, wo_ref, hidden_ref, low_ref, dy_ref, gain_part_ref
):
    hidden_grad = grad_ref[...] + sum_ref[...].astype(f32)
    proj = proj_ref[...].astype(f32)
    inverse = lax.rsqrt(mean_square(proj) + EPSILON)
    normed = proj * inverse
    hidden_ref[...] = hidden_grad
    gain_part_ref[...] = jnp.sum(hidden_grad * normed, axis=0, keepdims=True)
    low = norm_back(hidden_grad, normed, inverse, gain_ref[...]).astype(bf16)
    low_ref[...] = low
    grad = nn(low, wo_ref[...])
    for head in range(heads):
        dy_ref[head] = grad[:, head_cols(head)].astype(bf16)


def backward_chunk(at, batch, part, rows, branch_sum, grad, proj, gain, w_attn, kept):
    total = proj.shape[0]
    width = w_attn.shape[2]
    heads = width // HEAD
    whole = pl.BlockSpec((rows, D), lambda s: (at, 0))
    line = pl.BlockSpec((1, D), lambda s: (0, 0))
    return chunk_call(
        functools.partial(backward_chunk_kernel, heads),
        [
            (pl.BlockSpec((rows, D), lambda s: (0, 0)), branch_sum),
            (pl.BlockSpec((None, rows, D), lambda s: (batch, part, 0)), grad),
            (whole, proj),
            (line, gain),
            (pl.BlockSpec((None, D, width), lambda s: (3, 0, 0)), w_attn),
        ],
        [
            (whole, jax.ShapeDtypeStruct((total, D), f32), True),
            (whole, jax.ShapeDtypeStruct((total, D), bf16), True),
            (
                pl.BlockSpec((heads, rows, HEAD), lambda s: (0, at, 0)),
                jax.ShapeDtypeStruct((heads, total, HEAD), bf16),
                True,
            ),
            (line, jax.ShapeDtypeStruct((1, D), f32), False),
        ],
        kept,
        (1,),
        [],
        pl.CostEstimate(
            flops=2 * rows * D * width, bytes_accessed=16 * rows * D, transcendentals=rows
        ),
        "backward_chunk",
    )


def weight_sum_kernel(left_ref, right_ref, out_ref):
    out_ref[...] = lax.dot_general(
        left_ref[...], right_ref[...], (((0,), (0,)), ((), ())), preferred_element_type=f32
    ).astype(bf16)


def weight_sum(slots, count, left, right, units, kept):
    rows, depth = left.shape
    first = slots[0]
    return chunk_call(
        weight_sum_kernel,
        [
            (pl.BlockSpec((rows, TILE), lambda w, s: (0, s)), left),
            (pl.BlockSpec((rows, units), lambda w, s: (0, w)), right),
        ],
        [
            (
                pl.BlockSpec((None, TILE, units), lambda w, s: (first + w, s, 0)),
                jax.ShapeDtypeStruct((count, depth, units), bf16),
                True,
            )
        ],
        kept,
        (len(slots), depth // TILE),
        [],
        pl.CostEstimate(
            flops=2 * rows * depth * units * len(slots),
            bytes_accessed=2 * len(slots) * (rows * depth + rows * units + depth * units),
            transcendentals=0,
        ),
        "weight_sum",
    )


def shards(
    layer_input,
    cotangent,
    w_query,
    w_key,
    w_value,
    w_output,
    w_gate,
    w_up,
    w_down,
    query_gain,
    key_gain,
    attn_gain,
    mlp_gain,
    slot_parent,
    slot_depth,
):
    dp_index = lax.axis_index("dp")
    tp_index = lax.axis_index("tensor")
    dp_count = lax.axis_size("dp")
    tp_count = lax.axis_size("tensor")
    rows = layer_input.shape[1]
    share = rows // tp_count
    width = w_query.shape[1]
    heads = width // HEAD
    hidden_width = w_gate.shape[1]
    items = heads * MB
    copies = dp_count // items

    def gather_stack(*pieces):
        return lax.all_gather(jnp.stack(pieces), "dp", axis=1, tiled=True)

    def scatter_rows(total, dimension=0):
        return lax.psum_scatter(
            total.astype(bf16), "dp", scatter_dimension=dimension, tiled=True
        )

    def exchange(pieces):
        flat = pieces.reshape((items, -1, HEAD))
        if copies > 1:
            flat = jnp.tile(flat, (copies, 1, 1))
        return lax.all_to_all(flat, "dp", split_axis=0, concat_axis=0, tiled=True)

    def give_back(pieces):
        flat = pieces.reshape((dp_count, -1, HEAD))
        return lax.all_to_all(flat, "dp", split_axis=0, concat_axis=0, tiled=True)[:items]

    w_attn = gather_stack(w_query, w_key, w_value, jnp.transpose(w_output))
    w_gate_all = gather_stack(w_gate)

    order = tree_order(slot_parent, slot_depth)
    my_batch = lax.rem(lax.rem(dp_index, items), MB)
    my_order = lax.dynamic_index_in_dim(order, my_batch, 0, keepdims=False)
    my_depth = lax.dynamic_slice_in_dim(slot_depth, dp_index * SEG_DEV, SEG_DEV, 1)
    cosines, sines = rope_tables(my_depth)

    q_raw, k_raw, squares = project(layer_input, w_attn, (0, 1), True)
    squares = jnp.transpose(squares.reshape(MB * rows, 2))
    (v_raw,) = project(layer_input, w_attn, (2,), False)
    squares = small_sum(squares, "tensor", tp_count)
    inverse = jnp.transpose(lax.rsqrt(squares / D + EPSILON)).reshape(MB, rows, 2)
    gains = jnp.concatenate([query_gain, key_gain])[None, :]
    packed = pack_heads(q_raw, k_raw, v_raw, inverse, gains, cosines, sines, heads)
    w_out_begun = begin_output_weight(w_attn[3], packed, dp_index, dp_count, tp_count)
    packed = follow(exchange(packed), w_out_begun[1]).reshape(dp_count, 3, SEG_DEV, BLK, HEAD)
    w_out = end_output_weight(w_out_begun, packed, dp_index, dp_count, tp_count)
    w_mlp = (w_gate_all, gather_stack(*follow((w_up, jnp.transpose(w_down)), packed)))

    attended = give_back(attend_forward(my_order, packed))
    attended = attended.reshape(heads, MB, rows, HEAD).transpose(1, 2, 0, 3)
    attended = attended.reshape(MB, rows, width)

    parts = 2
    step = rows // parts
    spots = [(batch, part) for batch in range(MB) for part in range(parts)]
    begun = []
    everything = []
    for batch in range(MB):
        after = begun[-1][1][2:] if begun else None
        begun.append(begin_all_gather(follow(attended[batch], after), tp_count))
    sums = SumLine(tp_count)
    attn_gain_row = attn_gain[None, :]
    mlp_gain_row = mlp_gain[None, :]
    chunks = len(spots)
    state = dict(forward=None, middle=None, backward=None)
    mlp_gain_parts = []
    attn_gain_parts = []

    def forward(at, after):
        batch, part = spots[at]
        if batch == len(everything):
            early = sums.terms[0] if sums.terms else None
            everything.append(end_all_gather(begun[batch], tp_count, early))
        *state["forward"], term = forward_chunk(
            at,
            batch,
            part,
            step,
            follow(everything[batch], after),
            layer_input,
            attn_gain_row,
            w_out,
            w_mlp,
            state["forward"],
        )
        return term

    def middle(at, after):
        batch, part = spots[at]
        proj, _, _, silu, slope = state["forward"]
        *kept, gain_part, term = middle_chunk(
            at,
            batch,
            part,
            step,
            follow(sums.sums[at], after),
            proj,
            layer_input,
            cotangent,
            attn_gain_row,
            mlp_gain_row,
            silu,
            slope,
            w_mlp,
            state["middle"],
        )
        state["middle"] = kept
        mlp_gain_parts.append(gain_part)
        return term

    def backward(at, after):
        batch, part = spots[at]
        *kept, gain_part = backward_chunk(
            at,
            batch,
            part,
            step,
            follow(sums.sums[chunks + at], after),
            cotangent,
            state["forward"][0],
            attn_gain_row,
            w_attn,
            state["backward"],
        )
        state["backward"] = kept
        attn_gain_parts.append(gain_part)
        return gain_part

    sums.enter(forward(0, None))
    sums.enter(forward(1, None))
    last = None
    mlp_total = None
    for at in range(2 * chunks + 2):
        after = sums.terms[-1] if last is None and tp_count == 4 else last
        moved = tuple(sums.advance(after)) or None
        coming = at + 2
        if coming < chunks:
            last = forward(coming, moved)
            sums.enter(last)
        elif coming < 2 * chunks:
            last = middle(coming - chunks, moved)
            sums.enter(last)
        else:
            last = backward(coming - 2 * chunks, moved)
            turn_at = coming - 2 * chunks
            output, mlp_grad, gate_grad, up_grad = state["middle"]
            hidden_low, act = state["forward"][1:3]
            left, right = (
                (hidden_low, gate_grad),
                (hidden_low, up_grad),
                (mlp_grad, act),
                (None, None),
            )[turn_at]
            if left is not None:
                mlp_total = weight_sum(
                    (turn_at,), 3, follow(left, last), right, hidden_width, mlp_total
                )
                last = mlp_total[0]
        if coming == 3 * chunks - 1:
            break
    hidden_grad, proj_grad, attn_grad = state["backward"]
    mlp_weight_grad = scatter_rows(mlp_total[0], 1)
    attended = attended.reshape(MB * rows, width)
    attn_total = weight_sum((3,), 4, proj_grad, follow(attended, attn_grad), width, None)

    attn_grad = exchange(attn_grad).reshape(dp_count, SEG_DEV, BLK, HEAD)
    back = give_back(attend_backward(my_order, packed, attn_grad))
    back = back.reshape(heads, MB, 3, rows, HEAD)
    inner, gain_part = inner_sums(back, q_raw, k_raw, inverse, gains, cosines, sines, heads)
    means = small_sum(jnp.transpose(inner.reshape(-1, 2)), "tensor", tp_count) / D
    means = jnp.transpose(means).reshape(MB, rows, 2)
    qkv_grad = None
    terms = []
    for batch in range(MB):
        *qkv_grad, term = unpack_heads(
            batch, back, q_raw, k_raw, inverse, means, gains, cosines, sines, w_attn, heads, qkv_grad
        )
        terms.append(term)
    tokens = layer_input.reshape(MB * rows, D)
    qkv_grad = follow(qkv_grad[0], mlp_weight_grad)
    attn_total = weight_sum((0, 1, 2), 4, tokens, qkv_grad, width, attn_total)
    attn_weight_grad = scatter_rows(attn_total[0], 1)
    mlp_weight_grads = [mlp_weight_grad[at].astype(f32) for at in range(3)]
    mlp_weight_grads[2] = jnp.transpose(mlp_weight_grads[2])
    parts, last_operands = line_reduce_scatter(terms, tp_count, mlp_weight_grads)
    input_parts = [
        lax.dynamic_slice_in_dim(hidden_grad, batch * rows + tp_index * share, share, 0) + part
        for batch, part in enumerate(parts)
    ]

    gain_sums = jnp.concatenate(
        [
            gain_part[0],
            sum(attn_gain_parts)[0],
            sum(mlp_gain_parts)[0],
        ]
    )
    gain_sums = follow(gain_sums.reshape(-1, HEAD), last_operands)
    gain_sums = small_sum(gain_sums, "dp", dp_count).reshape(-1)
    return (
        output.reshape(MB, rows, D),
        jnp.stack(input_parts),
        attn_weight_grad[0].astype(f32),
        attn_weight_grad[1].astype(f32),
        attn_weight_grad[2].astype(f32),
        jnp.transpose(attn_weight_grad[3].astype(f32)),
        *mlp_weight_grads,
        gain_sums[:width],
        gain_sums[width : 2 * width],
        gain_sums[2 * width : 2 * width + D],
        gain_sums[2 * width + D :],
    )


def solution(mesh):
    in_specs = (
        P(None, "dp", None),
        P(None, "dp", None),
        P("dp", "tensor"),
        P("dp", "tensor"),
        P("dp", "tensor"),
        P("tensor", "dp"),
        P("dp", "tensor"),
        P("dp", "tensor"),
        P("tensor", "dp"),
        P("tensor"),
        P("tensor"),
        P(),
        P(),
        P(),
        P(),
    )
    out_specs = (
        P(None, "dp", None),
        P(None, ("dp", "tensor"), None),
        P("dp", "tensor"),
        P("dp", "tensor"),
        P("dp", "tensor"),
        P("tensor", "dp"),
        P("dp", "tensor"),
        P("dp", "tensor"),
        P("tensor", "dp"),
        P("tensor"),
        P("tensor"),
        P(),
        P(),
    )
    return jax.shard_map(shards, mesh=mesh, in_specs=in_specs, out_specs=out_specs, check_vma=False)
```

```python
import functools

import jax
import jax.numpy as jnp
from jax import lax
from jax.experimental import pallas as pl
from jax.experimental.pallas import tpu as pltpu
from jax.sharding import PartitionSpec as P

D = 2048
HEADS = 16
HEAD = D // HEADS
BLK = 128
TRUNK = 8
BRANCHES = 4
LEAVES = 2
TREE_BLOCKS = 20
MB = 2
SEG_DEV = 5
PAIR = 2 * BLK
TRUNK_ROWS = TRUNK * BLK
TILE = 512

EPSILON = 1e-06
ROPE_BASE = 500000.0
SCALING = HEAD ** (-0.5)
VMEM_LIMIT = 50 * 1024 * 1024

f32 = jnp.float32
bf16 = jnp.bfloat16


def tree_order(parents, depths):
    blocks = parents.shape[1]
    ids = jnp.arange(blocks, dtype=jnp.int32)

    def follow(table, index):
        hot = index[:, :, None] == ids[None, None, :]
        return jnp.sum(jnp.where(hot, table[:, None, :], 0), axis=-1)

    up2 = follow(parents, parents)
    up4 = follow(up2, up2)
    up8 = follow(up4, up4)
    root = follow(up8, up8)
    is_leaf = depths == TRUNK + 1
    above = jnp.where(is_leaf, parents, 0)
    key = ((root * (TRUNK + 2) + depths) * blocks + above) * blocks + ids[None, :]
    rank = jnp.sum((key[:, None, :] < key[:, :, None]).astype(jnp.int32), axis=-1)
    return jnp.sum(
        jnp.where(rank[:, None, :] == ids[None, :, None], ids[None, None, :], 0), axis=-1
    ).astype(jnp.int32)


def rope_tables(depths):
    half = HEAD // 2
    offsets = jnp.arange(BLK, dtype=jnp.int32)
    places = (depths[:, :, None] * BLK + offsets).reshape(depths.shape[0], -1).astype(f32)
    frequency = ROPE_BASE ** (-2.0 * jnp.arange(half, dtype=f32) / HEAD)
    angles = places[:, :, None] * frequency
    cosines = jnp.cos(angles)
    sines = jnp.sin(angles)
    return (
        jnp.concatenate([cosines, cosines], -1),
        jnp.concatenate([-sines, sines], -1),
    )


def low_sum(*parts):
    total = parts[0].astype(f32)
    for part in parts[1:]:
        total = total + part.astype(f32)
    return total.astype(bf16)


def follow(values, after):
    if after is None:
        return values
    return lax.optimization_barrier((values, after))[0]


def small_sum(values, axis, count):
    step = 1
    while step < count:
        values = values + lax.ppermute(values, axis, [(i, i ^ step) for i in range(count)])
        step *= 2
    return values


class SumLine:
    def __init__(self, count):
        self.count = count
        index = lax.axis_index("tensor")
        self.inner = (index == 1) | (index == 2)
        self.terms = []
        self.inward = []
        self.sides = []
        self.across = []
        self.totals = []
        self.outward = []
        self.sums = []

    def enter(self, term):
        if self.count != 4:
            self.sums.append(lax.psum(term, "tensor"))
            return
        self.terms.append(term)
        self.inward.append(lax.ppermute(term, "tensor", [(0, 1), (3, 2)]))

    def advance(self, after):
        if self.count != 4:
            return []
        moved = []
        if len(self.sides) < len(self.terms):
            at = len(self.sides)
            side = low_sum(follow(self.terms[at], after), self.inward[at])
            self.sides.append(side)
            moved.append(side)
        at = len(self.totals)
        if at < len(self.sides) - 1 or (at < len(self.sides) and not moved):
            total = low_sum(follow(self.sides[at], after), self.across[at])
            self.totals.append(total)
            moved.append(total)
        at = len(self.sums)
        if at < len(self.outward):
            self.sums.append(
                jnp.where(self.inner, follow(self.totals[at], after), self.outward[at])
            )
        if len(self.across) < len(self.sides):
            self.across.append(lax.ppermute(self.sides[-1], "tensor", [(1, 2), (2, 1)]))
        if len(self.outward) < len(self.totals):
            self.outward.append(lax.ppermute(self.totals[-1], "tensor", [(1, 0), (2, 3)]))
        return moved


def line_reduce_scatter(batches, count, late):
    if count != 4:
        return [
            lax.psum_scatter(values, "tensor", scatter_dimension=0, tiled=True).astype(f32)
            for values in batches
        ], None, None
    index = lax.axis_index("tensor")
    rights = []
    lefts = []
    blocks = [item.reshape(count, item.shape[0] // count, item.shape[1]) for item in batches]

    def block(item, at):
        return lax.dynamic_index_in_dim(item, lax.rem(at + 2 * count, count), 0, keepdims=False)

    operands = []
    for stage in range(count - 1):
        to_right = [(i, i + 1) for i in range(stage + 1)]
        to_left = [(count - 1 - i, count - 2 - i) for i in range(stage + 1)]
        for at, item in enumerate(blocks):
            right = block(item, index + count - 1 - stage)
            left = block(item, index - count + 1 + stage)
            if stage == 1 and at == 0:
                right, left = follow((right, left), batches[-1])
            if stage:
                right = low_sum(right, rights[at])
                left = low_sum(left, lefts[at])
                if stage == count - 2 and at == len(blocks) - 1:
                    right, left = follow((right, left), late)
                rights[at] = lax.ppermute(right, "tensor", to_right)
                lefts[at] = lax.ppermute(left, "tensor", to_left)
            else:
                rights.append(lax.ppermute(right, "tensor", to_right))
                lefts.append(lax.ppermute(left, "tensor", to_left))
            operands.append((right, left))
    sums = [
        block(item, index).astype(f32) + right.astype(f32) + left.astype(f32)
        for item, right, left in zip(blocks, rights, lefts)
    ]
    return sums, operands[len(blocks)], operands[-1]


def begin_all_gather(values, count):
    if count != 4:
        return values, None
    right = lax.ppermute(values, "tensor", [(0, 1), (1, 2), (2, 3)])
    left = lax.ppermute(values, "tensor", [(3, 2), (2, 1), (1, 0)])
    return values, (right, left)


def go_on_all_gather(begun, count):
    values, first = begun
    if count != 4:
        return values, None, None
    right = lax.ppermute(first[0], "tensor", [(1, 2), (2, 3)])
    left = lax.ppermute(first[1], "tensor", [(2, 1), (1, 0)])
    return values, first, (right, left)


def end_all_gather(begun, count, after=None):
    values, first, second = begun
    if count != 4:
        return lax.all_gather(values, "tensor", axis=1, tiled=True), None
    index = lax.axis_index("tensor")
    width = values.shape[1]
    right, left = follow(second, after)
    right = lax.ppermute(right, "tensor", [(2, 3)])
    left = lax.ppermute(left, "tensor", [(1, 0)])
    whole = jnp.zeros((values.shape[0], count * width), values.dtype)
    pieces = (
        values,
        jnp.where(index >= 1, first[0], left),
        jnp.where(index >= 2, second[0], second[1]),
        jnp.where(index >= 3, right, first[1]),
    )
    for back, piece in enumerate(pieces):
        place = lax.rem(index - back + count, count) * width
        whole = lax.dynamic_update_slice(whole, piece, (0, place))
    return whole, (right, left)


def begin_output_weight(own, after, dp_index, dp_count, count):
    if count != 4 or dp_count % 2:
        return own, None, None
    half = own.shape[0] // 2
    mine = lax.dynamic_slice_in_dim(follow(own, after), lax.rem(dp_index, 2) * half, half, 0)
    return go_on_all_gather(begin_all_gather(mine, count), count)


def end_output_weight(begun, after, dp_index, dp_count, count):
    if count != 4 or dp_count % 2:
        whole = lax.all_gather(begun[0], "tensor", axis=1, tiled=True)
        half = whole.shape[0] // 2
        return jnp.zeros((1,), jnp.int32), whole[:half], whole[half:]
    mine, _ = end_all_gather(begun, count, after)
    other = lax.ppermute(mine, "dp", [(i, i ^ 1) for i in range(dp_count)])
    return lax.rem(dp_index, 2).astype(jnp.int32).reshape(1), mine, other


def turn(values, cosines, sines):
    return values * cosines + pltpu.roll(values, HEAD // 2, 1) * sines


def head_cols(head, group=0, heads=0):
    start = (group * heads + head) * HEAD
    return slice(start, start + HEAD)


def project_kernel(x_ref, *refs):
    count = len(refs) // 2 if len(refs) > 2 else 1
    weights, outs = refs[:count], refs[count:]
    for at in range(count):
        raw = jnp.dot(x_ref[0], weights[at][0], preferred_element_type=f32)
        outs[at][0] = raw.astype(outs[at].dtype)
        if len(outs) > count:
            outs[count][0, :, at : at + 1] = jnp.sum(raw * raw, axis=1, keepdims=True)


def project(tokens, weights, which, squares):
    batches, rows, _ = tokens.shape
    width = weights.shape[2]
    step = rows // 2
    dtype = f32 if squares else bf16
    out_specs = [pl.BlockSpec((1, step, width), lambda b, r: (b, r, 0))] * len(which)
    out_shape = [jax.ShapeDtypeStruct((batches, rows, width), dtype)] * len(which)
    if squares:
        out_specs.append(pl.BlockSpec((1, step, len(which)), lambda b, r: (b, r, 0)))
        out_shape.append(jax.ShapeDtypeStruct((batches, rows, len(which)), f32))
    return pl.pallas_call(
        project_kernel,
        grid=(batches, rows // step),
        in_specs=[pl.BlockSpec((1, step, D), lambda b, r: (b, r, 0))]
        + [pl.BlockSpec((1, D, width), lambda b, r, at=at: (at, 0, 0)) for at in which],
        out_specs=out_specs,
        out_shape=out_shape,
        compiler_params=pltpu.CompilerParams(vmem_limit_bytes=VMEM_LIMIT),
        cost_estimate=pl.CostEstimate(
            flops=2 * batches * rows * D * width * len(which),
            bytes_accessed=2 * batches * rows * D + 2 * D * width * len(which),
            transcendentals=0,
        ),
        name="project",
    )(tokens, *([weights] * len(which)))


def pack_kernel(heads, q_ref, k_ref, v_ref, inv_ref, gain_ref, cos_ref, sin_ref, out_ref):
    cosines = cos_ref[0]
    sines = sin_ref[0]
    for head in range(heads):
        for which in range(2):
            cols = head_cols(head, which, heads)
            raw_ref = (q_ref, k_ref)[which]
            normed = raw_ref[0, :, head_cols(head)] * inv_ref[0, :, which : which + 1] * gain_ref[:, cols]
            out_ref[head, 0, which] = turn(normed, cosines, sines).astype(bf16)
        out_ref[head, 0, 2] = v_ref[0, :, head_cols(head)]


def pack_heads(q_raw, k_raw, v_raw, inverse, gains, cosines, sines, heads):
    rows = q_raw.shape[1]
    step = rows // 2
    width = heads * HEAD
    return pl.pallas_call(
        functools.partial(pack_kernel, heads),
        grid=(MB, rows // step),
        in_specs=[
            pl.BlockSpec((1, step, width), lambda b, r: (b, r, 0)),
            pl.BlockSpec((1, step, width), lambda b, r: (b, r, 0)),
            pl.BlockSpec((1, step, width), lambda b, r: (b, r, 0)),
            pl.BlockSpec((1, step, 2), lambda b, r: (b, r, 0)),
            pl.BlockSpec((1, 2 * width), lambda b, r: (0, 0)),
            pl.BlockSpec((1, step, HEAD), lambda b, r: (b, r, 0)),
            pl.BlockSpec((1, step, HEAD), lambda b, r: (b, r, 0)),
        ],
        out_specs=pl.BlockSpec((heads, 1, 3, step, HEAD), lambda b, r: (0, b, 0, r, 0)),
        out_shape=jax.ShapeDtypeStruct((heads, MB, 3, rows, HEAD), bf16),
        name="pack_heads",
    )(q_raw, k_raw, v_raw, inverse, gains, cosines, sines)


def inner_kernel(heads, back_ref, q_ref, k_ref, inv_ref, gain_ref, cos_ref, sin_ref, inner_ref, part_ref):
    cosines = cos_ref[0]
    sines = -sin_ref[0]

    @pl.when((pl.program_id(0) == 0) & (pl.program_id(1) == 0))
    def _():
        part_ref[...] = jnp.zeros_like(part_ref)

    for which in range(2):
        total = None
        for head in range(heads):
            cols = head_cols(head, which, heads)
            straight = turn(back_ref[head, 0, which].astype(f32), cosines, sines)
            hat = (q_ref, k_ref)[which][0, :, head_cols(head)] * inv_ref[0, :, which : which + 1]
            product = straight * hat
            part_ref[:, cols] += jnp.sum(product, axis=0, keepdims=True)
            weighted = product * gain_ref[:, cols]
            total = weighted if total is None else total + weighted
        inner_ref[0, :, which : which + 1] = jnp.sum(total, axis=1, keepdims=True)


def inner_sums(back, q_raw, k_raw, inverse, gains, cosines, sines, heads):
    rows = q_raw.shape[1]
    step = rows // 2
    width = heads * HEAD
    return pl.pallas_call(
        functools.partial(inner_kernel, heads),
        grid=(MB, rows // step),
        in_specs=[
            pl.BlockSpec((heads, 1, 2, step, HEAD), lambda b, r: (0, b, 0, r, 0)),
            pl.BlockSpec((1, step, width), lambda b, r: (b, r, 0)),
            pl.BlockSpec((1, step, width), lambda b, r: (b, r, 0)),
            pl.BlockSpec((1, step, 2), lambda b, r: (b, r, 0)),
            pl.BlockSpec((1, 2 * width), lambda b, r: (0, 0)),
            pl.BlockSpec((1, step, HEAD), lambda b, r: (b, r, 0)),
            pl.BlockSpec((1, step, HEAD), lambda b, r: (b, r, 0)),
        ],
        out_specs=[
            pl.BlockSpec((1, step, 2), lambda b, r: (b, r, 0)),
            pl.BlockSpec((1, 2 * width), lambda b, r: (0, 0)),
        ],
        out_shape=[
            jax.ShapeDtypeStruct((MB, rows, 2), f32),
            jax.ShapeDtypeStruct((1, 2 * width), f32),
        ],
        name="inner_sums",
    )(back, q_raw, k_raw, inverse, gains, cosines, sines)


def unpack_kernel(
    heads,
    back_ref,
    q_ref,
    k_ref,
    inv_ref,
    mean_ref,
    gain_ref,
    cos_ref,
    sin_ref,
    wq_ref,
    wk_ref,
    wv_ref,
    grad_ref,
    term_ref,
):
    cosines = cos_ref[0]
    sines = -sin_ref[0]
    width = heads * HEAD
    for head in range(heads):
        for which in range(2):
            cols = head_cols(head, which, heads)
            inverse = inv_ref[0, :, which : which + 1]
            straight = turn(back_ref[head, 0, which].astype(f32), cosines, sines)
            hat = (q_ref, k_ref)[which][0, :, head_cols(head)] * inverse
            grad = inverse * (straight * gain_ref[:, cols] - hat * mean_ref[0, :, which : which + 1])
            grad_ref[:, cols] = grad.astype(bf16)
        grad_ref[:, head_cols(head, 2, heads)] = back_ref[head, 0, 2]
    term = nt(grad_ref[:, :width], wq_ref[0])
    term = term + nt(grad_ref[:, width : 2 * width], wk_ref[0])
    term = term + nt(grad_ref[:, 2 * width :], wv_ref[0])
    term_ref[...] = term.astype(bf16)


def unpack_heads(
    batch, back, q_raw, k_raw, inverse, means, gains, cosines, sines, weights, heads, kept
):
    rows = q_raw.shape[1]
    step = rows // 2
    width = heads * HEAD
    row_spec = lambda cols: pl.BlockSpec((1, step, cols), lambda r: (batch, r, 0))
    return chunk_call(
        functools.partial(unpack_kernel, heads),
        [
            (pl.BlockSpec((heads, 1, 3, step, HEAD), lambda r: (0, batch, 0, r, 0)), back),
            (row_spec(width), q_raw),
            (row_spec(width), k_raw),
            (row_spec(2), inverse),
            (row_spec(2), means),
            (pl.BlockSpec((1, 2 * width), lambda r: (0, 0)), gains),
            (row_spec(HEAD), cosines),
            (row_spec(HEAD), sines),
        ]
        + [(pl.BlockSpec((1, D, width), lambda r, at=at: (at, 0, 0)), weights) for at in range(3)],
        [
            (
                pl.BlockSpec((step, 3 * width), lambda r: (batch * 2 + r, 0)),
                jax.ShapeDtypeStruct((MB * rows, 3 * width), bf16),
                True,
            ),
            (
                pl.BlockSpec((step, D), lambda r: (r, 0)),
                jax.ShapeDtypeStruct((rows, D), bf16),
                False,
            ),
        ],
        kept,
        (2,),
        [],
        pl.CostEstimate(flops=6 * rows * D * width, bytes_accessed=8 * rows * D, transcendentals=0),
        "unpack_heads",
    )


def nt(left, right):
    return lax.dot_general(left, right, (((1,), (1,)), ((), ())), preferred_element_type=f32)


def nn(left, right):
    return lax.dot_general(left, right, (((1,), (0,)), ((), ())), preferred_element_type=f32)


def key_query_iotas(keys):
    key_at = lax.broadcasted_iota(jnp.int32, (keys, PAIR), 0)
    query_at = lax.broadcasted_iota(jnp.int32, (keys, PAIR), 1)
    return key_at, query_at


def causal_mask():
    key_at, query_at = key_query_iotas(PAIR)
    return key_at <= query_at


def apart_mask(above):
    key_at, query_at = key_query_iotas(above + PAIR)
    key_at = key_at - above
    own = (key_at <= query_at) & ((key_at < BLK) == (query_at < BLK))
    return own | (key_at < 0)


def softmax_parts(queries, trunk_keys, near_keys, mask):
    near = jnp.where(mask, nt(near_keys, queries), -1e30)
    top = jnp.max(near, axis=0, keepdims=True)
    if trunk_keys is None:
        near = jnp.exp((near - top) * SCALING)
        scale = 1.0 / jnp.sum(near, axis=0, keepdims=True)
        return None, near * scale
    far = nt(trunk_keys, queries)
    top = jnp.maximum(top, jnp.max(far, axis=0, keepdims=True))
    near = jnp.exp((near - top) * SCALING)
    far = jnp.exp((far - top) * SCALING)
    scale = 1.0 / (jnp.sum(near, axis=0, keepdims=True) + jnp.sum(far, axis=0, keepdims=True))
    return far * scale, near * scale


def places(order_ref, tree):
    def at(within):
        slot = order_ref[tree * TREE_BLOCKS + within]
        return lax.div(slot, SEG_DEV), lax.rem(slot, SEG_DEV)

    return at


def load(ref, which, *spots):
    parts = [ref[group, which, row] for group, row in spots]
    return parts[0] if len(parts) == 1 else jnp.concatenate(parts, axis=0)


def across(values):
    return jnp.transpose(values.astype(f32)).astype(bf16)


def forward_kernel(trees, order_ref, x_ref, y_ref, k_ref, vt_ref):
    def one_tree(tree, carry):
        at = places(order_ref, tree)
        for within in range(TRUNK):
            rows = slice(within * BLK, (within + 1) * BLK)
            spot = at(within)
            k_ref[rows, :] = load(x_ref, 1, spot)
            vt_ref[:, rows] = across(load(x_ref, 2, spot))

        def attend(spots, far_rows, near_keys, near_values, mask):
            queries = load(x_ref, 0, *spots)
            far, near = softmax_parts(
                queries, k_ref[:far_rows, :] if far_rows else None, near_keys, mask
            )
            summed = nn(across(near_values), near.astype(bf16))
            if far_rows:
                summed = summed + nn(vt_ref[:, :far_rows], far.astype(bf16))
            rows = jnp.transpose(summed).astype(bf16)
            y_ref[spots[0][0], spots[0][1]] = rows[:BLK]
            y_ref[spots[1][0], spots[1][1]] = rows[BLK:]

        causal = causal_mask()
        for pair in range(TRUNK // 2):
            spots = (at(2 * pair), at(2 * pair + 1))
            attend(spots, pair * PAIR, load(x_ref, 1, *spots), load(x_ref, 2, *spots), causal)
        apart = apart_mask(0)
        for pair in range(BRANCHES // 2):
            spots = (at(TRUNK + 2 * pair), at(TRUNK + 2 * pair + 1))
            attend(spots, TRUNK_ROWS, load(x_ref, 1, *spots), load(x_ref, 2, *spots), apart)
        under = apart_mask(BLK)
        for branch in range(BRANCHES):
            first = TRUNK + BRANCHES + LEAVES * branch
            spots = (at(first), at(first + 1))
            near = (at(TRUNK + branch),) + spots
            attend(spots, TRUNK_ROWS, load(x_ref, 1, *near), load(x_ref, 2, *near), under)
        return carry

    lax.fori_loop(0, trees, one_tree, 0)


def attend_forward(order, packed):
    groups = packed.shape[0]
    blocks = packed.shape[2]
    trees = groups * blocks // TREE_BLOCKS
    pairs = trees * TREE_BLOCKS * BLK * 1100
    return pl.pallas_call(
        functools.partial(forward_kernel, trees),
        in_specs=[
            pl.BlockSpec(memory_space=pltpu.SMEM),
            pl.BlockSpec(memory_space=pltpu.VMEM),
        ],
        out_specs=pl.BlockSpec(memory_space=pltpu.VMEM),
        out_shape=jax.ShapeDtypeStruct((groups, blocks, BLK, HEAD), bf16),
        scratch_shapes=[
            pltpu.VMEM((TRUNK_ROWS, HEAD), bf16),
            pltpu.VMEM((HEAD, TRUNK_ROWS), bf16),
        ],
        compiler_params=pltpu.CompilerParams(vmem_limit_bytes=VMEM_LIMIT),
        cost_estimate=pl.CostEstimate(
            flops=pairs * HEAD * 4, bytes_accessed=packed.size * 3, transcendentals=pairs
        ),
        name="attend_forward",
    )(order, packed)


def backward_kernel(
    trees, order_ref, x_ref, dy_ref, out_ref, k_ref, kt_ref, v_ref, dk_ref, dv_ref, dkb_ref, dvb_ref
):
    def one_tree(tree, carry):
        at = places(order_ref, tree)
        for within in range(TRUNK):
            rows = slice(within * BLK, (within + 1) * BLK)
            spot = at(within)
            keys = load(x_ref, 1, spot)
            k_ref[rows, :] = keys
            kt_ref[:, rows] = across(keys)
            v_ref[rows, :] = load(x_ref, 2, spot)

        def attend(spots, far_rows, near_spots, mask, start):
            queries = load(x_ref, 0, *spots)
            grads = jnp.concatenate(
                [dy_ref[spots[0][0], spots[0][1]], dy_ref[spots[1][0], spots[1][1]]], axis=0
            )
            near_keys = load(x_ref, 1, *near_spots)
            near_values = load(x_ref, 2, *near_spots)
            far, near = softmax_parts(
                queries, k_ref[:far_rows, :] if far_rows else None, near_keys, mask
            )
            near_grad = nt(near_values, grads)
            inner = jnp.sum(near * near_grad, axis=0, keepdims=True)
            if far_rows:
                far_grad = nt(v_ref[:far_rows, :], grads)
                inner = inner + jnp.sum(far * far_grad, axis=0, keepdims=True)
                far_score = (far * (far_grad - inner)).astype(bf16)
                far_dk = nn(far_score, queries)
                far_dv = nn(far.astype(bf16), grads)
                if start:
                    dk_ref[:far_rows, :] = far_dk
                    dv_ref[:far_rows, :] = far_dv
                else:
                    dk_ref[:far_rows, :] += far_dk
                    dv_ref[:far_rows, :] += far_dv
            near_score = (near * (near_grad - inner)).astype(bf16)
            turned = nn(across(near_keys), near_score)
            if far_rows:
                turned = turned + nn(kt_ref[:, :far_rows], far_score)
            rows = (jnp.transpose(turned) * SCALING).astype(bf16)
            out_ref[spots[0][0], 0, spots[0][1]] = rows[:BLK]
            out_ref[spots[1][0], 0, spots[1][1]] = rows[BLK:]
            return nn(near_score, queries), nn(near.astype(bf16), grads)

        def store(spot, key_grad, value_grad):
            out_ref[spot[0], 1, spot[1]] = (key_grad * SCALING).astype(bf16)
            out_ref[spot[0], 2, spot[1]] = value_grad.astype(bf16)

        under = apart_mask(BLK)
        for branch in range(BRANCHES):
            first = TRUNK + BRANCHES + LEAVES * branch
            spots = (at(first), at(first + 1))
            key_grad, value_grad = attend(
                spots, TRUNK_ROWS, (at(TRUNK + branch),) + spots, under, branch == 0
            )
            dkb_ref[branch] = key_grad[:BLK]
            dvb_ref[branch] = value_grad[:BLK]
            store(spots[0], key_grad[BLK : 2 * BLK], value_grad[BLK : 2 * BLK])
            store(spots[1], key_grad[2 * BLK :], value_grad[2 * BLK :])
        apart = apart_mask(0)
        for pair in range(BRANCHES // 2):
            spots = (at(TRUNK + 2 * pair), at(TRUNK + 2 * pair + 1))
            key_grad, value_grad = attend(spots, TRUNK_ROWS, spots, apart, False)
            for half in range(2):
                rows = slice(half * BLK, (half + 1) * BLK)
                branch = 2 * pair + half
                store(
                    spots[half], key_grad[rows] + dkb_ref[branch], value_grad[rows] + dvb_ref[branch]
                )
        causal = causal_mask()
        for pair in reversed(range(TRUNK // 2)):
            spots = (at(2 * pair), at(2 * pair + 1))
            key_grad, value_grad = attend(spots, pair * PAIR, spots, causal, False)
            for half in range(2):
                rows = slice(half * BLK, (half + 1) * BLK)
                held = slice(pair * PAIR + half * BLK, pair * PAIR + (half + 1) * BLK)
                store(
                    spots[half],
                    key_grad[rows] + dk_ref[held, :],
                    value_grad[rows] + dv_ref[held, :],
                )
        return carry

    lax.fori_loop(0, trees, one_tree, 0)


def attend_backward(order, packed, grads):
    groups = packed.shape[0]
    blocks = packed.shape[2]
    trees = groups * blocks // TREE_BLOCKS
    pairs = trees * TREE_BLOCKS * BLK * 1100
    return pl.pallas_call(
        functools.partial(backward_kernel, trees),
        in_specs=[
            pl.BlockSpec(memory_space=pltpu.SMEM),
            pl.BlockSpec(memory_space=pltpu.VMEM),
            pl.BlockSpec(memory_space=pltpu.VMEM),
        ],
        out_specs=pl.BlockSpec(memory_space=pltpu.VMEM),
        out_shape=jax.ShapeDtypeStruct(packed.shape, bf16),
        scratch_shapes=[
            pltpu.VMEM((TRUNK_ROWS, HEAD), bf16),
            pltpu.VMEM((HEAD, TRUNK_ROWS), bf16),
            pltpu.VMEM((TRUNK_ROWS, HEAD), bf16),
            pltpu.VMEM((TRUNK_ROWS, HEAD), f32),
            pltpu.VMEM((TRUNK_ROWS, HEAD), f32),
            pltpu.VMEM((BRANCHES, BLK, HEAD), f32),
            pltpu.VMEM((BRANCHES, BLK, HEAD), f32),
        ],
        compiler_params=pltpu.CompilerParams(vmem_limit_bytes=VMEM_LIMIT),
        cost_estimate=pl.CostEstimate(
            flops=pairs * HEAD * 10, bytes_accessed=packed.size * 5, transcendentals=pairs
        ),
        name="attend_backward",
    )(order, packed, grads)


def mean_square(values):
    return jnp.mean(values * values, axis=-1, keepdims=True)


def norm_back(gradient, normed, inverse, gain_vec):
    weighted = gradient * gain_vec
    return inverse * (weighted - normed * jnp.mean(normed * weighted, axis=-1, keepdims=True))


def chunk_call(kernel, ins, outs, kept, grid, scratch, cost, name):
    count = len(ins)
    specs = [spec for spec, _ in ins]
    values = [value for _, value in ins]
    aliases = {}
    if kept is not None:
        whole = [at for at, out in enumerate(outs) if out[2]]
        for at, value in zip(whole, kept):
            aliases[len(values)] = at
            specs.append(pl.BlockSpec(memory_space=pl.ANY))
            values.append(value)
    extra = len(values) - count

    def body(*refs):
        kernel(*refs[:count], *refs[count + extra :])

    return pl.pallas_call(
        body,
        grid=grid,
        in_specs=specs,
        out_specs=[out[0] for out in outs],
        out_shape=[out[1] for out in outs],
        scratch_shapes=scratch,
        input_output_aliases=aliases,
        compiler_params=pltpu.CompilerParams(vmem_limit_bytes=VMEM_LIMIT),
        cost_estimate=cost,
        name=name,
    )(*values)


def forward_chunk_kernel(
    place,
    core_ref,
    gain_ref,
    y_hbm,
    x_hbm,
    woa_hbm,
    wob_hbm,
    wg_hbm,
    wr_hbm,
    proj_hbm,
    low_hbm,
    act_hbm,
    silu_hbm,
    slope_hbm,
    part_hbm,
    y_ref,
    x_ref,
    row_ref,
    gate_ref,
    up_ref,
    exact_ref,
    proj_ref,
    low_ref,
    act_ref,
    silu_ref,
    slope_ref,
    part_ref,
    y_sem,
    x_sem,
    row_sems,
    gate_sems,
    up_sems,
    out_sems,
    part_sems,
):
    at, batch, part = place
    rows = y_ref.shape[0]
    units = act_ref.shape[1]
    tiles = D // TILE
    half = tiles // 2
    unit_tiles = units // TILE
    here = pl.ds(at * rows, rows)

    def tile(index):
        return pl.ds(pl.multiple_of(index * TILE, TILE), TILE)

    def out_tile(source, index):
        slot = index if source is woa_hbm else index + half
        return pltpu.make_async_copy(
            source.at[tile(index), :], row_ref.at[slot], row_sems.at[slot]
        )

    def unit_copies(index):
        slot = lax.rem(index, 2)
        return (
            pltpu.make_async_copy(wg_hbm.at[0, :, tile(index)], gate_ref.at[slot], gate_sems.at[slot]),
            pltpu.make_async_copy(wr_hbm.at[0, :, tile(index)], up_ref.at[slot], up_sems.at[slot]),
        )

    def down_copy(index):
        return pltpu.make_async_copy(
            wr_hbm.at[1, tile(index), :], row_ref.at[index, :, pl.ds(0, units)], row_sems.at[index]
        )

    def row_wait(index, width):
        pltpu.make_async_copy(
            woa_hbm.at[pl.ds(0, TILE), pl.ds(0, width)],
            row_ref.at[index, :, pl.ds(0, width)],
            row_sems.at[index],
        ).wait()

    y_copy = pltpu.make_async_copy(y_hbm.at[pl.ds(part * rows, rows), :], y_ref, y_sem)
    x_copy = pltpu.make_async_copy(x_hbm.at[batch, pl.ds(part * rows, rows), :], x_ref, x_sem)
    y_copy.start()
    for index in range(half):
        out_tile(woa_hbm, index).start()
    x_copy.start()
    y_copy.wait()

    def project_tile(index, carry):
        row_wait(index, D)

        @pl.when(index < half)
        def _():
            out_tile(wob_hbm, index).start()

        @pl.when(index >= half)
        def _():
            for copy in unit_copies(index - half):
                copy.start()

        side = jnp.where(index < half, core_ref[0], 1 - core_ref[0])
        columns = tile(side * half + lax.rem(index, half))
        exact_ref[:, columns] = nt(y_ref[...], row_ref[index])
        return carry

    lax.fori_loop(0, tiles, project_tile, 0)
    x_copy.wait()
    proj = exact_ref[...]
    inverse = lax.rsqrt(mean_square(proj) + EPSILON)
    proj_ref[...] = proj.astype(bf16)
    low_ref[...] = (x_ref[...].astype(f32) + proj * inverse * gain_ref[...]).astype(bf16)
    outs = [
        pltpu.make_async_copy(proj_ref, proj_hbm.at[here, :], out_sems.at[0]),
        pltpu.make_async_copy(low_ref, low_hbm.at[here, :], out_sems.at[1]),
        pltpu.make_async_copy(act_ref, act_hbm.at[here, :], out_sems.at[2]),
        pltpu.make_async_copy(silu_ref, silu_hbm.at[here, :], out_sems.at[3]),
        pltpu.make_async_copy(slope_ref, slope_hbm.at[here, :], out_sems.at[4]),
    ]
    outs[0].start()
    outs[1].start()

    def unit_tile(index, carry):
        slot = lax.rem(index, 2)
        for copy in unit_copies(index):
            copy.wait()
        low = low_ref[...]
        gate = nn(low, gate_ref[slot])
        up = nn(low, up_ref[slot])

        @pl.when(index + 2 < unit_tiles)
        def _():
            for copy in unit_copies(index + 2):
                copy.start()

        @pl.when(index + 2 >= unit_tiles)
        def _():
            first = (index + 2 - unit_tiles) * half
            for more in range(half):
                down_copy(first + more).start()

        sigmoid = 1.0 / (1.0 + jnp.exp(-gate))
        silu = gate * sigmoid
        columns = tile(index)
        act_ref[:, columns] = (silu * up).astype(bf16)
        silu_ref[:, columns] = silu.astype(bf16)
        slope_ref[:, columns] = (up * sigmoid * (1.0 + gate * (1.0 - sigmoid))).astype(bf16)
        return carry

    lax.fori_loop(0, unit_tiles, unit_tile, 0)
    for copy in outs[2:]:
        copy.start()

    def part_copy(index):
        columns = tile(index)
        return pltpu.make_async_copy(
            part_ref.at[:, columns], part_hbm.at[:, columns], part_sems.at[index]
        )

    def down_tile(index, carry):
        row_wait(index, units)
        part_ref[:, tile(index)] = nt(act_ref[...], row_ref[index, :, :units]).astype(bf16)
        part_copy(index).start()
        return carry

    lax.fori_loop(0, tiles, down_tile, 0)
    for index in range(tiles):
        part_copy(index).wait()
    for copy in outs:
        copy.wait()


def forward_chunk(at, batch, part, rows, y_all, tokens, gain, w_out, w_mlp, kept):
    core, w_out_a, w_out_b = w_out
    w_gate, w_rest = w_mlp
    units = w_gate.shape[2]
    total = tokens.shape[0] * tokens.shape[1]
    tiles = D // TILE
    anywhere = pl.BlockSpec(memory_space=pl.ANY)
    wide = jax.ShapeDtypeStruct((total, units), bf16)
    narrow = jax.ShapeDtypeStruct((total, D), bf16)
    dma = pltpu.SemaphoreType.DMA
    return chunk_call(
        functools.partial(forward_chunk_kernel, (at, batch, part)),
        [
            (pl.BlockSpec(memory_space=pltpu.SMEM), core),
            (pl.BlockSpec(memory_space=pltpu.VMEM), gain),
            (anywhere, y_all),
            (anywhere, tokens),
            (anywhere, w_out_a),
            (anywhere, w_out_b),
            (anywhere, w_gate),
            (anywhere, w_rest),
        ],
        [
            (anywhere, narrow, True),
            (anywhere, narrow, True),
            (anywhere, wide, True),
            (anywhere, wide, True),
            (anywhere, wide, True),
            (anywhere, jax.ShapeDtypeStruct((rows, D), bf16), False),
        ],
        kept,
        (),
        [
            pltpu.VMEM((rows, D), bf16),
            pltpu.VMEM((rows, D), bf16),
            pltpu.VMEM((tiles, TILE, D), bf16),
            pltpu.VMEM((2, D, TILE), bf16),
            pltpu.VMEM((2, D, TILE), bf16),
            pltpu.VMEM((rows, D), f32),
            pltpu.VMEM((rows, D), bf16),
            pltpu.VMEM((rows, D), bf16),
            pltpu.VMEM((rows, units), bf16),
            pltpu.VMEM((rows, units), bf16),
            pltpu.VMEM((rows, units), bf16),
            pltpu.VMEM((rows, D), bf16),
            dma,
            dma,
            dma((tiles,)),
            dma((2,)),
            dma((2,)),
            dma((5,)),
            dma((tiles,)),
        ],
        pl.CostEstimate(
            flops=2 * rows * D * (D + 3 * units),
            bytes_accessed=2 * D * (D + 3 * units) + 16 * rows * D,
            transcendentals=rows * units,
        ),
        "forward_chunk",
    )


def middle_chunk_kernel(
    place,
    attn_gain_ref,
    gain_ref,
    sum_hbm,
    proj_hbm,
    x_hbm,
    grad_hbm,
    silu_hbm,
    slope_hbm,
    wg_hbm,
    wr_hbm,
    output_hbm,
    low_hbm,
    gate_hbm,
    up_hbm,
    gain_part_ref,
    part_hbm,
    sum_ref,
    proj_ref,
    x_ref,
    grad_ref,
    silu_ref,
    slope_ref,
    down_ref,
    wg_ref,
    wu_ref,
    output_ref,
    low_ref,
    gates_ref,
    ups_ref,
    part_ref,
    in_sems,
    down_sems,
    wg_sems,
    wu_sems,
    out_sems,
    part_sems,
):
    at, batch, part = place
    rows = sum_ref.shape[0]
    units = silu_ref.shape[1]
    tiles = D // TILE
    half = tiles // 2
    unit_tiles = units // TILE
    here = pl.ds(at * rows, rows)
    inside = pl.ds(part * rows, rows)

    def tile(index):
        return pl.ds(pl.multiple_of(index * TILE, TILE), TILE)

    def down_copy(index):
        slot = lax.rem(index, 2)
        return pltpu.make_async_copy(
            wr_hbm.at[1, :, tile(index)], down_ref.at[slot], down_sems.at[slot]
        )

    def row_copies(index):
        slot = lax.rem(index, half)
        return (
            pltpu.make_async_copy(wg_hbm.at[0, tile(index), :], wg_ref.at[slot], wg_sems.at[slot]),
            pltpu.make_async_copy(wr_hbm.at[0, tile(index), :], wu_ref.at[slot], wu_sems.at[slot]),
        )

    ins = [
        pltpu.make_async_copy(sum_hbm, sum_ref, in_sems.at[0]),
        pltpu.make_async_copy(grad_hbm.at[batch, inside, :], grad_ref, in_sems.at[1]),
        pltpu.make_async_copy(proj_hbm.at[here, :], proj_ref, in_sems.at[2]),
        pltpu.make_async_copy(x_hbm.at[batch, inside, :], x_ref, in_sems.at[3]),
        pltpu.make_async_copy(silu_hbm.at[here, :], silu_ref, in_sems.at[4]),
        pltpu.make_async_copy(slope_hbm.at[here, :], slope_ref, in_sems.at[5]),
    ]
    ins[0].start()
    ins[1].start()
    down_copy(0).start()
    ins[4].start()
    ins[5].start()
    down_copy(1).start()
    ins[2].start()
    ins[3].start()
    ins[0].wait()
    ins[1].wait()
    mlp = sum_ref[...].astype(f32)
    mlp_inverse = lax.rsqrt(mean_square(mlp) + EPSILON)
    normed = mlp * mlp_inverse
    grad = grad_ref[...]
    gain_part_ref[...] = jnp.sum(grad * normed, axis=0, keepdims=True)
    low_ref[...] = norm_back(grad, normed, mlp_inverse, gain_ref[...]).astype(bf16)
    outs = [
        pltpu.make_async_copy(output_ref, output_hbm.at[here, :], out_sems.at[0]),
        pltpu.make_async_copy(low_ref, low_hbm.at[here, :], out_sems.at[1]),
        pltpu.make_async_copy(gates_ref, gate_hbm.at[here, :], out_sems.at[2]),
        pltpu.make_async_copy(ups_ref, up_hbm.at[here, :], out_sems.at[3]),
    ]
    outs[1].start()
    ins[4].wait()
    ins[5].wait()

    def unit_tile(index, carry):
        down_copy(index).wait()
        act_grad = nn(low_ref[...], down_ref[lax.rem(index, 2)])

        @pl.when(index + 2 < unit_tiles)
        def _():
            down_copy(index + 2).start()

        @pl.when(index + 2 >= unit_tiles)
        def _():
            for copy in row_copies(index + 2 - unit_tiles):
                copy.start()

        columns = tile(index)
        ups_ref[:, columns] = (act_grad * silu_ref[:, columns].astype(f32)).astype(bf16)
        gates_ref[:, columns] = (act_grad * slope_ref[:, columns].astype(f32)).astype(bf16)
        return carry

    lax.fori_loop(0, unit_tiles, unit_tile, 0)
    outs[2].start()
    outs[3].start()
    ins[2].wait()
    ins[3].wait()
    proj = proj_ref[...].astype(f32)
    inverse = lax.rsqrt(mean_square(proj) + EPSILON)
    hidden = x_ref[...].astype(f32) + proj * inverse * attn_gain_ref[...]
    mlp = sum_ref[...].astype(f32)
    output_ref[...] = (hidden + mlp * mlp_inverse * gain_ref[...]).astype(bf16)
    outs[0].start()

    def part_copy(index):
        columns = tile(index)
        return pltpu.make_async_copy(
            part_ref.at[:, columns], part_hbm.at[:, columns], part_sems.at[index]
        )

    def row_tile(index, carry):
        slot = lax.rem(index, half)
        for copy in row_copies(index):
            copy.wait()
        part_ref[:, tile(index)] = (
            nt(gates_ref[...], wg_ref[slot]) + nt(ups_ref[...], wu_ref[slot])
        ).astype(bf16)
        part_copy(index).start()

        @pl.when(index + half < tiles)
        def _():
            for copy in row_copies(index + half):
                copy.start()

        return carry

    lax.fori_loop(0, tiles, row_tile, 0)
    for index in range(tiles):
        part_copy(index).wait()
    for copy in outs:
        copy.wait()


def middle_chunk(
    at, batch, part, rows, mlp_sum, proj, tokens, grad, attn_gain, gain, silu, slope, w_mlp, kept
):
    w_gate, w_rest = w_mlp
    units = w_gate.shape[2]
    total = proj.shape[0]
    tiles = D // TILE
    half = tiles // 2
    vmem = pl.BlockSpec(memory_space=pltpu.VMEM)
    anywhere = pl.BlockSpec(memory_space=pl.ANY)
    wide = jax.ShapeDtypeStruct((total, units), bf16)
    narrow = jax.ShapeDtypeStruct((total, D), bf16)
    dma = pltpu.SemaphoreType.DMA
    return chunk_call(
        functools.partial(middle_chunk_kernel, (at, batch, part)),
        [
            (vmem, attn_gain),
            (vmem, gain),
            (anywhere, mlp_sum),
            (anywhere, proj),
            (anywhere, tokens),
            (anywhere, grad),
            (anywhere, silu),
            (anywhere, slope),
            (anywhere, w_gate),
            (anywhere, w_rest),
        ],
        [
            (anywhere, narrow, True),
            (anywhere, narrow, True),
            (anywhere, wide, True),
            (anywhere, wide, True),
            (vmem, jax.ShapeDtypeStruct((1, D), f32), False),
            (anywhere, jax.ShapeDtypeStruct((rows, D), bf16), False),
        ],
        kept,
        (),
        [
            pltpu.VMEM((rows, D), bf16),
            pltpu.VMEM((rows, D), bf16),
            pltpu.VMEM((rows, D), bf16),
            pltpu.VMEM((rows, D), f32),
            pltpu.VMEM((rows, units), bf16),
            pltpu.VMEM((rows, units), bf16),
            pltpu.VMEM((2, D, TILE), bf16),
            pltpu.VMEM((half, TILE, units), bf16),
            pltpu.VMEM((half, TILE, units), bf16),
            pltpu.VMEM((rows, D), bf16),
            pltpu.VMEM((rows, D), bf16),
            pltpu.VMEM((rows, units), bf16),
            pltpu.VMEM((rows, units), bf16),
            pltpu.VMEM((rows, D), bf16),
            dma((6,)),
            dma((2,)),
            dma((half,)),
            dma((half,)),
            dma((4,)),
            dma((tiles,)),
        ],
        pl.CostEstimate(
            flops=2 * rows * D * 3 * units,
            bytes_accessed=2 * D * 3 * units + 24 * rows * D,
            transcendentals=rows,
        ),
        "middle_chunk",
    )


def backward_chunk_kernel(
    heads, sum_ref, grad_ref, proj_ref, gain_ref, wo_ref, hidden_ref, low_ref, dy_ref, gain_part_ref
):
    hidden_grad = grad_ref[...] + sum_ref[...].astype(f32)
    proj = proj_ref[...].astype(f32)
    inverse = lax.rsqrt(mean_square(proj) + EPSILON)
    normed = proj * inverse
    hidden_ref[...] = hidden_grad
    gain_part_ref[...] = jnp.sum(hidden_grad * normed, axis=0, keepdims=True)
    low = norm_back(hidden_grad, normed, inverse, gain_ref[...]).astype(bf16)
    low_ref[...] = low
    grad = nn(low, wo_ref[...])
    for head in range(heads):
        dy_ref[head] = grad[:, head_cols(head)].astype(bf16)


def backward_chunk(at, batch, part, rows, branch_sum, grad, proj, gain, w_attn, kept):
    total = proj.shape[0]
    width = w_attn.shape[2]
    heads = width // HEAD
    whole = pl.BlockSpec((rows, D), lambda s: (at, 0))
    line = pl.BlockSpec((1, D), lambda s: (0, 0))
    return chunk_call(
        functools.partial(backward_chunk_kernel, heads),
        [
            (pl.BlockSpec((rows, D), lambda s: (0, 0)), branch_sum),
            (pl.BlockSpec((None, rows, D), lambda s: (batch, part, 0)), grad),
            (whole, proj),
            (line, gain),
            (pl.BlockSpec((None, D, width), lambda s: (3, 0, 0)), w_attn),
        ],
        [
            (whole, jax.ShapeDtypeStruct((total, D), f32), True),
            (whole, jax.ShapeDtypeStruct((total, D), bf16), True),
            (
                pl.BlockSpec((heads, rows, HEAD), lambda s: (0, at, 0)),
                jax.ShapeDtypeStruct((heads, total, HEAD), bf16),
                True,
            ),
            (line, jax.ShapeDtypeStruct((1, D), f32), False),
        ],
        kept,
        (1,),
        [],
        pl.CostEstimate(
            flops=2 * rows * D * width, bytes_accessed=16 * rows * D, transcendentals=rows
        ),
        "backward_chunk",
    )


def weight_sum_kernel(left_ref, right_ref, out_ref):
    out_ref[...] = lax.dot_general(
        left_ref[...], right_ref[...], (((0,), (0,)), ((), ())), preferred_element_type=f32
    ).astype(bf16)


def weight_sum(slots, count, left, right, units, kept):
    rows, depth = left.shape
    first = slots[0]
    return chunk_call(
        weight_sum_kernel,
        [
            (pl.BlockSpec((rows, TILE), lambda w, s: (0, s)), left),
            (pl.BlockSpec((rows, units), lambda w, s: (0, w)), right),
        ],
        [
            (
                pl.BlockSpec((None, TILE, units), lambda w, s: (first + w, s, 0)),
                jax.ShapeDtypeStruct((count, depth, units), bf16),
                True,
            )
        ],
        kept,
        (len(slots), depth // TILE),
        [],
        pl.CostEstimate(
            flops=2 * rows * depth * units * len(slots),
            bytes_accessed=2 * len(slots) * (rows * depth + rows * units + depth * units),
            transcendentals=0,
        ),
        "weight_sum",
    )


def shards(
    layer_input,
    cotangent,
    w_query,
    w_key,
    w_value,
    w_output,
    w_gate,
    w_up,
    w_down,
    query_gain,
    key_gain,
    attn_gain,
    mlp_gain,
    slot_parent,
    slot_depth,
):
    dp_index = lax.axis_index("dp")
    tp_index = lax.axis_index("tensor")
    dp_count = lax.axis_size("dp")
    tp_count = lax.axis_size("tensor")
    rows = layer_input.shape[1]
    share = rows // tp_count
    width = w_query.shape[1]
    heads = width // HEAD
    hidden_width = w_gate.shape[1]
    items = heads * MB
    copies = dp_count // items

    def gather_stack(*pieces):
        return lax.all_gather(jnp.stack(pieces), "dp", axis=1, tiled=True)

    def scatter_rows(total, dimension=0):
        return lax.psum_scatter(
            total.astype(bf16), "dp", scatter_dimension=dimension, tiled=True
        )

    def exchange(pieces):
        flat = pieces.reshape((items, -1, HEAD))
        if copies > 1:
            flat = jnp.tile(flat, (copies, 1, 1))
        return lax.all_to_all(flat, "dp", split_axis=0, concat_axis=0, tiled=True)

    def give_back(pieces):
        flat = pieces.reshape((dp_count, -1, HEAD))
        return lax.all_to_all(flat, "dp", split_axis=0, concat_axis=0, tiled=True)[:items]

    w_attn = gather_stack(w_query, w_key, w_value, jnp.transpose(w_output))
    w_gate_all = gather_stack(w_gate)

    order = tree_order(slot_parent, slot_depth)
    my_batch = lax.rem(lax.rem(dp_index, items), MB)
    my_order = lax.dynamic_index_in_dim(order, my_batch, 0, keepdims=False)
    my_depth = lax.dynamic_slice_in_dim(slot_depth, dp_index * SEG_DEV, SEG_DEV, 1)
    cosines, sines = rope_tables(my_depth)

    q_raw, k_raw, squares = project(layer_input, w_attn, (0, 1), True)
    squares = jnp.transpose(squares.reshape(MB * rows, 2))
    (v_raw,) = project(layer_input, w_attn, (2,), False)
    squares = small_sum(squares, "tensor", tp_count)
    inverse = jnp.transpose(lax.rsqrt(squares / D + EPSILON)).reshape(MB, rows, 2)
    gains = jnp.concatenate([query_gain, key_gain])[None, :]
    packed = pack_heads(q_raw, k_raw, v_raw, inverse, gains, cosines, sines, heads)
    w_out_begun = begin_output_weight(w_attn[3], packed, dp_index, dp_count, tp_count)
    packed = follow(exchange(packed), w_out_begun[1:]).reshape(dp_count, 3, SEG_DEV, BLK, HEAD)
    w_out = end_output_weight(w_out_begun, packed, dp_index, dp_count, tp_count)
    w_mlp = (w_gate_all, gather_stack(*follow((w_up, jnp.transpose(w_down)), packed)))

    attended = give_back(attend_forward(my_order, packed))
    attended = attended.reshape(heads, MB, rows, HEAD).transpose(1, 2, 0, 3)
    attended = attended.reshape(MB, rows, width)

    parts = 2
    step = rows // parts
    spots = [(batch, part) for batch in range(MB) for part in range(parts)]
    begun = go_on_all_gather(begin_all_gather(attended[0], tp_count), tp_count)
    gathered, hop = end_all_gather(begun, tp_count)
    everything = [gathered]
    begun = [begun]
    for batch in range(1, MB):
        begun.append(begin_all_gather(follow(attended[batch], hop), tp_count))
    sums = SumLine(tp_count)
    attn_gain_row = attn_gain[None, :]
    mlp_gain_row = mlp_gain[None, :]
    chunks = len(spots)
    state = dict(forward=None, middle=None, backward=None)
    mlp_gain_parts = []
    attn_gain_parts = []

    def forward(at, after):
        batch, part = spots[at]
        if batch == len(everything):
            early = sums.terms[0] if sums.terms else None
            going = go_on_all_gather(begun[batch], tp_count)
            everything.append(end_all_gather(going, tp_count, early)[0])
        *state["forward"], term = forward_chunk(
            at,
            batch,
            part,
            step,
            follow(everything[batch], after),
            layer_input,
            attn_gain_row,
            w_out,
            w_mlp,
            state["forward"],
        )
        return term

    def middle(at, after):
        batch, part = spots[at]
        proj, _, _, silu, slope = state["forward"]
        *kept, gain_part, term = middle_chunk(
            at,
            batch,
            part,
            step,
            follow(sums.sums[at], after),
            proj,
            layer_input,
            cotangent,
            attn_gain_row,
            mlp_gain_row,
            silu,
            slope,
            w_mlp,
            state["middle"],
        )
        state["middle"] = kept
        mlp_gain_parts.append(gain_part)
        return term

    def backward(at, after):
        batch, part = spots[at]
        *kept, gain_part = backward_chunk(
            at,
            batch,
            part,
            step,
            follow(sums.sums[chunks + at], after),
            cotangent,
            state["forward"][0],
            attn_gain_row,
            w_attn,
            state["backward"],
        )
        state["backward"] = kept
        attn_gain_parts.append(gain_part)
        return gain_part

    sums.enter(forward(0, None))
    sums.enter(forward(1, None))
    last = None
    mlp_total = None
    for at in range(2 * chunks + 2):
        after = sums.terms[-1] if last is None and tp_count == 4 else last
        moved = tuple(sums.advance(after)) or None
        coming = at + 2
        if coming < chunks:
            last = forward(coming, moved)
            sums.enter(last)
        elif coming < 2 * chunks:
            last = middle(coming - chunks, moved)
            sums.enter(last)
        else:
            last = backward(coming - 2 * chunks, moved)
            turn_at = coming - 2 * chunks
            output, mlp_grad, gate_grad, up_grad = state["middle"]
            hidden_low, act = state["forward"][1:3]
            left, right = (
                (hidden_low, gate_grad),
                (hidden_low, up_grad),
                (mlp_grad, act),
                (None, None),
            )[turn_at]
            if left is not None:
                mlp_total = weight_sum(
                    (turn_at,), 3, follow(left, last), right, hidden_width, mlp_total
                )
                last = mlp_total[0]
        if coming == 3 * chunks - 1:
            break
    hidden_grad, proj_grad, attn_grad = state["backward"]
    mlp_weight_grad = scatter_rows(mlp_total[0], 1)
    attended = attended.reshape(MB * rows, width)
    attn_total = weight_sum((3,), 4, proj_grad, follow(attended, attn_grad), width, None)

    attn_grad = follow(exchange(attn_grad), attn_total)
    attn_grad = attn_grad.reshape(dp_count, SEG_DEV, BLK, HEAD)
    back = give_back(attend_backward(my_order, packed, attn_grad))
    back = back.reshape(heads, MB, 3, rows, HEAD)
    inner, gain_part = inner_sums(back, q_raw, k_raw, inverse, gains, cosines, sines, heads)
    means = small_sum(jnp.transpose(inner.reshape(-1, 2)), "tensor", tp_count) / D
    means = jnp.transpose(means).reshape(MB, rows, 2)
    qkv_grad = None
    terms = []
    for batch in range(MB):
        *qkv_grad, term = unpack_heads(
            batch, back, q_raw, k_raw, inverse, means, gains, cosines, sines, w_attn, heads, qkv_grad
        )
        terms.append(term)
    mlp_weight_grads = [mlp_weight_grad[at].astype(f32) for at in range(3)]
    mlp_weight_grads[2] = jnp.transpose(mlp_weight_grads[2])
    parts, second_operands, last_operands = line_reduce_scatter(terms, tp_count, mlp_weight_grads)
    tokens = layer_input.reshape(MB * rows, D)
    qkv_grad = follow(qkv_grad[0], (mlp_weight_grad, second_operands))
    attn_total = weight_sum((0, 1, 2), 4, tokens, qkv_grad, width, attn_total)
    attn_weight_grad = scatter_rows(attn_total[0], 1)
    input_parts = [
        lax.dynamic_slice_in_dim(hidden_grad, batch * rows + tp_index * share, share, 0) + part
        for batch, part in enumerate(parts)
    ]

    gain_sums = jnp.concatenate(
        [
            gain_part[0],
            sum(attn_gain_parts)[0],
            sum(mlp_gain_parts)[0],
        ]
    )
    gain_sums = follow(gain_sums.reshape(-1, HEAD), last_operands)
    gain_sums = small_sum(gain_sums, "dp", dp_count).reshape(-1)
    return (
        output.reshape(MB, rows, D),
        jnp.stack(input_parts),
        attn_weight_grad[0].astype(f32),
        attn_weight_grad[1].astype(f32),
        attn_weight_grad[2].astype(f32),
        jnp.transpose(attn_weight_grad[3].astype(f32)),
        *mlp_weight_grads,
        gain_sums[:width],
        gain_sums[width : 2 * width],
        gain_sums[2 * width : 2 * width + D],
        gain_sums[2 * width + D :],
    )


def solution(mesh):
    in_specs = (
        P(None, "dp", None),
        P(None, "dp", None),
        P("dp", "tensor"),
        P("dp", "tensor"),
        P("dp", "tensor"),
        P("tensor", "dp"),
        P("dp", "tensor"),
        P("dp", "tensor"),
        P("tensor", "dp"),
        P("tensor"),
        P("tensor"),
        P(),
        P(),
        P(),
        P(),
    )
    out_specs = (
        P(None, "dp", None),
        P(None, ("dp", "tensor"), None),
        P("dp", "tensor"),
        P("dp", "tensor"),
        P("dp", "tensor"),
        P("tensor", "dp"),
        P("dp", "tensor"),
        P("dp", "tensor"),
        P("tensor", "dp"),
        P("tensor"),
        P("tensor"),
        P(),
        P(),
    )
    return jax.shard_map(shards, mesh=mesh, in_specs=in_specs, out_specs=out_specs, check_vma=False)
```

```python
import functools

import jax
import jax.numpy as jnp
from jax import lax
from jax.experimental import pallas as pl
from jax.experimental.pallas import tpu as pltpu
from jax.sharding import PartitionSpec as P

D = 2048
HEADS = 16
HEAD = D // HEADS
BLK = 128
TRUNK = 8
BRANCHES = 4
LEAVES = 2
TREE_BLOCKS = 20
MB = 2
SEG_DEV = 5
PAIR = 2 * BLK
TRUNK_ROWS = TRUNK * BLK
TILE = 512

EPSILON = 1e-06
ROPE_BASE = 500000.0
SCALING = HEAD ** (-0.5)
VMEM_LIMIT = 50 * 1024 * 1024

f32 = jnp.float32
bf16 = jnp.bfloat16


def tree_order(parents, depths):
    blocks = parents.shape[1]
    ids = jnp.arange(blocks, dtype=jnp.int32)

    def follow(table, index):
        hot = index[:, :, None] == ids[None, None, :]
        return jnp.sum(jnp.where(hot, table[:, None, :], 0), axis=-1)

    up2 = follow(parents, parents)
    up4 = follow(up2, up2)
    up8 = follow(up4, up4)
    root = follow(up8, up8)
    is_leaf = depths == TRUNK + 1
    above = jnp.where(is_leaf, parents, 0)
    key = ((root * (TRUNK + 2) + depths) * blocks + above) * blocks + ids[None, :]
    rank = jnp.sum((key[:, None, :] < key[:, :, None]).astype(jnp.int32), axis=-1)
    return jnp.sum(
        jnp.where(rank[:, None, :] == ids[None, :, None], ids[None, None, :], 0), axis=-1
    ).astype(jnp.int32)


def rope_tables(depths):
    half = HEAD // 2
    offsets = jnp.arange(BLK, dtype=jnp.int32)
    places = (depths[:, :, None] * BLK + offsets).reshape(depths.shape[0], -1).astype(f32)
    frequency = ROPE_BASE ** (-2.0 * jnp.arange(half, dtype=f32) / HEAD)
    angles = places[:, :, None] * frequency
    cosines = jnp.cos(angles)
    sines = jnp.sin(angles)
    return (
        jnp.concatenate([cosines, cosines], -1),
        jnp.concatenate([-sines, sines], -1),
    )


def low_sum(*parts):
    total = parts[0].astype(f32)
    for part in parts[1:]:
        total = total + part.astype(f32)
    return total.astype(bf16)


def follow(values, after):
    if after is None:
        return values
    return lax.optimization_barrier((values, after))[0]


def small_sum(values, axis, count):
    step = 1
    while step < count:
        values = values + lax.ppermute(values, axis, [(i, i ^ step) for i in range(count)])
        step *= 2
    return values


class SumLine:
    def __init__(self, count):
        self.count = count
        index = lax.axis_index("tensor")
        self.inner = (index == 1) | (index == 2)
        self.terms = []
        self.inward = []
        self.sides = []
        self.across = []
        self.totals = []
        self.outward = []
        self.sums = []

    def enter(self, term):
        if self.count != 4:
            self.sums.append(lax.psum(term, "tensor"))
            return
        self.terms.append(term)
        self.inward.append(lax.ppermute(term, "tensor", [(0, 1), (3, 2)]))

    def advance(self, after):
        if self.count != 4:
            return []
        moved = []
        if len(self.sides) < len(self.terms):
            at = len(self.sides)
            side = low_sum(follow(self.terms[at], after), self.inward[at])
            self.sides.append(side)
            moved.append(side)
        at = len(self.totals)
        if at < len(self.sides) - 1 or (at < len(self.sides) and not moved):
            total = low_sum(follow(self.sides[at], after), self.across[at])
            self.totals.append(total)
            moved.append(total)
        at = len(self.sums)
        if at < len(self.outward):
            self.sums.append(
                jnp.where(self.inner, follow(self.totals[at], after), self.outward[at])
            )
        if len(self.across) < len(self.sides):
            self.across.append(lax.ppermute(self.sides[-1], "tensor", [(1, 2), (2, 1)]))
        if len(self.outward) < len(self.totals):
            self.outward.append(lax.ppermute(self.totals[-1], "tensor", [(1, 0), (2, 3)]))
        return moved


def line_reduce_scatter(batches, count, late):
    if count != 4:
        return [
            (lax.psum_scatter(values, "tensor", scatter_dimension=0, tiled=True),)
            for values in batches
        ], (None, None), None
    index = lax.axis_index("tensor")
    rights = []
    lefts = []
    blocks = [item.reshape(count, item.shape[0] // count, item.shape[1]) for item in batches]

    def block(item, at):
        return lax.dynamic_index_in_dim(item, lax.rem(at + 2 * count, count), 0, keepdims=False)

    operands = []
    for stage in range(count - 1):
        to_right = [(i, i + 1) for i in range(stage + 1)]
        to_left = [(count - 1 - i, count - 2 - i) for i in range(stage + 1)]
        for at, item in enumerate(blocks):
            right = block(item, index + count - 1 - stage)
            left = block(item, index - count + 1 + stage)
            if stage == 1 and at == 0:
                right, left = follow((right, left), batches[-1])
            if stage:
                right = low_sum(right, rights[at])
                left = low_sum(left, lefts[at])
                if stage == count - 2 and at == len(blocks) - 1:
                    right, left = follow((right, left), late)
                rights[at] = lax.ppermute(right, "tensor", to_right)
                lefts[at] = lax.ppermute(left, "tensor", to_left)
            else:
                rights.append(lax.ppermute(right, "tensor", to_right))
                lefts.append(lax.ppermute(left, "tensor", to_left))
            operands.append((right, left))
    sums = [
        (block(item, index), right, left) for item, right, left in zip(blocks, rights, lefts)
    ]
    return sums, operands[1 : len(blocks) + 1], operands[-1]


def begin_all_gather(values, count):
    if count != 4:
        return values, None
    right = lax.ppermute(values, "tensor", [(0, 1), (1, 2), (2, 3)])
    left = lax.ppermute(values, "tensor", [(3, 2), (2, 1), (1, 0)])
    return values, (right, left)


def go_on_all_gather(begun, count):
    values, first = begun
    if count != 4:
        return values, None, None
    right = lax.ppermute(first[0], "tensor", [(1, 2), (2, 3)])
    left = lax.ppermute(first[1], "tensor", [(2, 1), (1, 0)])
    return values, first, (right, left)


def end_all_gather(begun, count, after=None):
    values, first, second = begun
    if count != 4:
        return lax.all_gather(values, "tensor", axis=1, tiled=True), None
    index = lax.axis_index("tensor")
    width = values.shape[1]
    right, left = follow(second, after)
    right = lax.ppermute(right, "tensor", [(2, 3)])
    left = lax.ppermute(left, "tensor", [(1, 0)])
    whole = jnp.zeros((values.shape[0], count * width), values.dtype)
    pieces = (
        values,
        jnp.where(index >= 1, first[0], left),
        jnp.where(index >= 2, second[0], second[1]),
        jnp.where(index >= 3, right, first[1]),
    )
    for back, piece in enumerate(pieces):
        place = lax.rem(index - back + count, count) * width
        whole = lax.dynamic_update_slice(whole, piece, (0, place))
    return whole, (right, left)


def begin_output_weight(own, after, dp_index, dp_count, count):
    if count != 4 or dp_count % 2:
        return own, None, None
    half = own.shape[0] // 2
    mine = lax.dynamic_slice_in_dim(follow(own, after), lax.rem(dp_index, 2) * half, half, 0)
    return go_on_all_gather(begin_all_gather(mine, count), count)


def end_output_weight(begun, after, dp_index, dp_count, count):
    if count != 4 or dp_count % 2:
        whole = lax.all_gather(begun[0], "tensor", axis=1, tiled=True)
        half = whole.shape[0] // 2
        return jnp.zeros((1,), jnp.int32), whole[:half], whole[half:]
    mine, _ = end_all_gather(begun, count, after)
    other = lax.ppermute(mine, "dp", [(i, i ^ 1) for i in range(dp_count)])
    return lax.rem(dp_index, 2).astype(jnp.int32).reshape(1), mine, other


def turn(values, cosines, sines):
    return values * cosines + pltpu.roll(values, HEAD // 2, 1) * sines


def head_cols(head, group=0, heads=0):
    start = (group * heads + head) * HEAD
    return slice(start, start + HEAD)


def project_kernel(x_ref, *refs):
    count = len(refs) // 2 if len(refs) > 2 else 1
    weights, outs = refs[:count], refs[count:]
    for at in range(count):
        raw = jnp.dot(x_ref[0], weights[at][0], preferred_element_type=f32)
        outs[at][0] = raw.astype(outs[at].dtype)
        if len(outs) > count:
            outs[count][0, :, at : at + 1] = jnp.sum(raw * raw, axis=1, keepdims=True)


def project(tokens, weights, which, squares):
    batches, rows, _ = tokens.shape
    width = weights.shape[2]
    step = rows // 2
    dtype = f32 if squares else bf16
    out_specs = [pl.BlockSpec((1, step, width), lambda b, r: (b, r, 0))] * len(which)
    out_shape = [jax.ShapeDtypeStruct((batches, rows, width), dtype)] * len(which)
    if squares:
        out_specs.append(pl.BlockSpec((1, step, len(which)), lambda b, r: (b, r, 0)))
        out_shape.append(jax.ShapeDtypeStruct((batches, rows, len(which)), f32))
    return pl.pallas_call(
        project_kernel,
        grid=(batches, rows // step),
        in_specs=[pl.BlockSpec((1, step, D), lambda b, r: (b, r, 0))]
        + [pl.BlockSpec((1, D, width), lambda b, r, at=at: (at, 0, 0)) for at in which],
        out_specs=out_specs,
        out_shape=out_shape,
        compiler_params=pltpu.CompilerParams(vmem_limit_bytes=VMEM_LIMIT),
        cost_estimate=pl.CostEstimate(
            flops=2 * batches * rows * D * width * len(which),
            bytes_accessed=2 * batches * rows * D + 2 * D * width * len(which),
            transcendentals=0,
        ),
        name="project",
    )(tokens, *([weights] * len(which)))


def pack_kernel(heads, q_ref, k_ref, v_ref, inv_ref, gain_ref, cos_ref, sin_ref, out_ref):
    cosines = cos_ref[0]
    sines = sin_ref[0]
    for head in range(heads):
        for which in range(2):
            cols = head_cols(head, which, heads)
            raw_ref = (q_ref, k_ref)[which]
            normed = raw_ref[0, :, head_cols(head)] * inv_ref[0, :, which : which + 1] * gain_ref[:, cols]
            out_ref[head, 0, which] = turn(normed, cosines, sines).astype(bf16)
        out_ref[head, 0, 2] = v_ref[0, :, head_cols(head)]


def pack_heads(q_raw, k_raw, v_raw, inverse, gains, cosines, sines, heads):
    rows = q_raw.shape[1]
    step = rows // 2
    width = heads * HEAD
    return pl.pallas_call(
        functools.partial(pack_kernel, heads),
        grid=(MB, rows // step),
        in_specs=[
            pl.BlockSpec((1, step, width), lambda b, r: (b, r, 0)),
            pl.BlockSpec((1, step, width), lambda b, r: (b, r, 0)),
            pl.BlockSpec((1, step, width), lambda b, r: (b, r, 0)),
            pl.BlockSpec((1, step, 2), lambda b, r: (b, r, 0)),
            pl.BlockSpec((1, 2 * width), lambda b, r: (0, 0)),
            pl.BlockSpec((1, step, HEAD), lambda b, r: (b, r, 0)),
            pl.BlockSpec((1, step, HEAD), lambda b, r: (b, r, 0)),
        ],
        out_specs=pl.BlockSpec((heads, 1, 3, step, HEAD), lambda b, r: (0, b, 0, r, 0)),
        out_shape=jax.ShapeDtypeStruct((heads, MB, 3, rows, HEAD), bf16),
        name="pack_heads",
    )(q_raw, k_raw, v_raw, inverse, gains, cosines, sines)


def inner_kernel(heads, back_ref, q_ref, k_ref, inv_ref, gain_ref, cos_ref, sin_ref, inner_ref, part_ref):
    cosines = cos_ref[0]
    sines = -sin_ref[0]

    @pl.when((pl.program_id(0) == 0) & (pl.program_id(1) == 0))
    def _():
        part_ref[...] = jnp.zeros_like(part_ref)

    for which in range(2):
        total = None
        for head in range(heads):
            cols = head_cols(head, which, heads)
            straight = turn(back_ref[head, 0, which].astype(f32), cosines, sines)
            hat = (q_ref, k_ref)[which][0, :, head_cols(head)] * inv_ref[0, :, which : which + 1]
            product = straight * hat
            part_ref[:, cols] += jnp.sum(product, axis=0, keepdims=True)
            weighted = product * gain_ref[:, cols]
            total = weighted if total is None else total + weighted
        inner_ref[0, :, which : which + 1] = jnp.sum(total, axis=1, keepdims=True)


def inner_sums(back, q_raw, k_raw, inverse, gains, cosines, sines, heads):
    rows = q_raw.shape[1]
    step = rows // 2
    width = heads * HEAD
    return pl.pallas_call(
        functools.partial(inner_kernel, heads),
        grid=(MB, rows // step),
        in_specs=[
            pl.BlockSpec((heads, 1, 2, step, HEAD), lambda b, r: (0, b, 0, r, 0)),
            pl.BlockSpec((1, step, width), lambda b, r: (b, r, 0)),
            pl.BlockSpec((1, step, width), lambda b, r: (b, r, 0)),
            pl.BlockSpec((1, step, 2), lambda b, r: (b, r, 0)),
            pl.BlockSpec((1, 2 * width), lambda b, r: (0, 0)),
            pl.BlockSpec((1, step, HEAD), lambda b, r: (b, r, 0)),
            pl.BlockSpec((1, step, HEAD), lambda b, r: (b, r, 0)),
        ],
        out_specs=[
            pl.BlockSpec((1, step, 2), lambda b, r: (b, r, 0)),
            pl.BlockSpec((1, 2 * width), lambda b, r: (0, 0)),
        ],
        out_shape=[
            jax.ShapeDtypeStruct((MB, rows, 2), f32),
            jax.ShapeDtypeStruct((1, 2 * width), f32),
        ],
        name="inner_sums",
    )(back, q_raw, k_raw, inverse, gains, cosines, sines)


def unpack_kernel(
    heads,
    back_ref,
    q_ref,
    k_ref,
    inv_ref,
    mean_ref,
    gain_ref,
    cos_ref,
    sin_ref,
    wq_ref,
    wk_ref,
    wv_ref,
    grad_ref,
    term_ref,
):
    cosines = cos_ref[0]
    sines = -sin_ref[0]
    width = heads * HEAD
    for head in range(heads):
        for which in range(2):
            cols = head_cols(head, which, heads)
            inverse = inv_ref[0, :, which : which + 1]
            straight = turn(back_ref[head, 0, which].astype(f32), cosines, sines)
            hat = (q_ref, k_ref)[which][0, :, head_cols(head)] * inverse
            grad = inverse * (straight * gain_ref[:, cols] - hat * mean_ref[0, :, which : which + 1])
            grad_ref[:, cols] = grad.astype(bf16)
        grad_ref[:, head_cols(head, 2, heads)] = back_ref[head, 0, 2]
    term = nt(grad_ref[:, :width], wq_ref[0])
    term = term + nt(grad_ref[:, width : 2 * width], wk_ref[0])
    term = term + nt(grad_ref[:, 2 * width :], wv_ref[0])
    term_ref[...] = term.astype(bf16)


def unpack_heads(
    batch, back, q_raw, k_raw, inverse, means, gains, cosines, sines, weights, heads, kept
):
    rows = q_raw.shape[1]
    step = rows // 2
    width = heads * HEAD
    row_spec = lambda cols: pl.BlockSpec((1, step, cols), lambda r: (batch, r, 0))
    return chunk_call(
        functools.partial(unpack_kernel, heads),
        [
            (pl.BlockSpec((heads, 1, 3, step, HEAD), lambda r: (0, batch, 0, r, 0)), back),
            (row_spec(width), q_raw),
            (row_spec(width), k_raw),
            (row_spec(2), inverse),
            (row_spec(2), means),
            (pl.BlockSpec((1, 2 * width), lambda r: (0, 0)), gains),
            (row_spec(HEAD), cosines),
            (row_spec(HEAD), sines),
        ]
        + [(pl.BlockSpec((1, D, width), lambda r, at=at: (at, 0, 0)), weights) for at in range(3)],
        [
            (
                pl.BlockSpec((step, 3 * width), lambda r: (batch * 2 + r, 0)),
                jax.ShapeDtypeStruct((MB * rows, 3 * width), bf16),
                True,
            ),
            (
                pl.BlockSpec((step, D), lambda r: (r, 0)),
                jax.ShapeDtypeStruct((rows, D), bf16),
                False,
            ),
        ],
        kept,
        (2,),
        [],
        pl.CostEstimate(flops=6 * rows * D * width, bytes_accessed=8 * rows * D, transcendentals=0),
        "unpack_heads",
    )


def nt(left, right):
    return lax.dot_general(left, right, (((1,), (1,)), ((), ())), preferred_element_type=f32)


def nn(left, right):
    return lax.dot_general(left, right, (((1,), (0,)), ((), ())), preferred_element_type=f32)


def key_query_iotas(keys):
    key_at = lax.broadcasted_iota(jnp.int32, (keys, PAIR), 0)
    query_at = lax.broadcasted_iota(jnp.int32, (keys, PAIR), 1)
    return key_at, query_at


def causal_mask():
    key_at, query_at = key_query_iotas(PAIR)
    return key_at <= query_at


def apart_mask(above):
    key_at, query_at = key_query_iotas(above + PAIR)
    key_at = key_at - above
    own = (key_at <= query_at) & ((key_at < BLK) == (query_at < BLK))
    return own | (key_at < 0)


def softmax_parts(queries, trunk_keys, near_keys, mask):
    near = jnp.where(mask, nt(near_keys, queries), -1e30)
    top = jnp.max(near, axis=0, keepdims=True)
    if trunk_keys is None:
        near = jnp.exp((near - top) * SCALING)
        scale = 1.0 / jnp.sum(near, axis=0, keepdims=True)
        return None, near * scale
    far = nt(trunk_keys, queries)
    top = jnp.maximum(top, jnp.max(far, axis=0, keepdims=True))
    near = jnp.exp((near - top) * SCALING)
    far = jnp.exp((far - top) * SCALING)
    scale = 1.0 / (jnp.sum(near, axis=0, keepdims=True) + jnp.sum(far, axis=0, keepdims=True))
    return far * scale, near * scale


def places(order_ref, tree):
    def at(within):
        slot = order_ref[tree * TREE_BLOCKS + within]
        return lax.div(slot, SEG_DEV), lax.rem(slot, SEG_DEV)

    return at


def load(ref, which, *spots):
    parts = [ref[group, which, row] for group, row in spots]
    return parts[0] if len(parts) == 1 else jnp.concatenate(parts, axis=0)


def across(values):
    return jnp.transpose(values.astype(f32)).astype(bf16)


def forward_kernel(trees, order_ref, x_ref, y_ref, k_ref, vt_ref):
    def one_tree(tree, carry):
        at = places(order_ref, tree)
        for within in range(TRUNK):
            rows = slice(within * BLK, (within + 1) * BLK)
            spot = at(within)
            k_ref[rows, :] = load(x_ref, 1, spot)
            vt_ref[:, rows] = across(load(x_ref, 2, spot))

        def attend(spots, far_rows, near_keys, near_values, mask):
            queries = load(x_ref, 0, *spots)
            far, near = softmax_parts(
                queries, k_ref[:far_rows, :] if far_rows else None, near_keys, mask
            )
            summed = nn(across(near_values), near.astype(bf16))
            if far_rows:
                summed = summed + nn(vt_ref[:, :far_rows], far.astype(bf16))
            rows = jnp.transpose(summed).astype(bf16)
            y_ref[spots[0][0], spots[0][1]] = rows[:BLK]
            y_ref[spots[1][0], spots[1][1]] = rows[BLK:]

        causal = causal_mask()
        for pair in range(TRUNK // 2):
            spots = (at(2 * pair), at(2 * pair + 1))
            attend(spots, pair * PAIR, load(x_ref, 1, *spots), load(x_ref, 2, *spots), causal)
        apart = apart_mask(0)
        for pair in range(BRANCHES // 2):
            spots = (at(TRUNK + 2 * pair), at(TRUNK + 2 * pair + 1))
            attend(spots, TRUNK_ROWS, load(x_ref, 1, *spots), load(x_ref, 2, *spots), apart)
        under = apart_mask(BLK)
        for branch in range(BRANCHES):
            first = TRUNK + BRANCHES + LEAVES * branch
            spots = (at(first), at(first + 1))
            near = (at(TRUNK + branch),) + spots
            attend(spots, TRUNK_ROWS, load(x_ref, 1, *near), load(x_ref, 2, *near), under)
        return carry

    lax.fori_loop(0, trees, one_tree, 0)


def attend_forward(order, packed):
    groups = packed.shape[0]
    blocks = packed.shape[2]
    trees = groups * blocks // TREE_BLOCKS
    pairs = trees * TREE_BLOCKS * BLK * 1100
    return pl.pallas_call(
        functools.partial(forward_kernel, trees),
        in_specs=[
            pl.BlockSpec(memory_space=pltpu.SMEM),
            pl.BlockSpec(memory_space=pltpu.VMEM),
        ],
        out_specs=pl.BlockSpec(memory_space=pltpu.VMEM),
        out_shape=jax.ShapeDtypeStruct((groups, blocks, BLK, HEAD), bf16),
        scratch_shapes=[
            pltpu.VMEM((TRUNK_ROWS, HEAD), bf16),
            pltpu.VMEM((HEAD, TRUNK_ROWS), bf16),
        ],
        compiler_params=pltpu.CompilerParams(vmem_limit_bytes=VMEM_LIMIT),
        cost_estimate=pl.CostEstimate(
            flops=pairs * HEAD * 4, bytes_accessed=packed.size * 3, transcendentals=pairs
        ),
        name="attend_forward",
    )(order, packed)


def backward_kernel(
    trees, order_ref, x_ref, dy_ref, out_ref, k_ref, kt_ref, v_ref, dk_ref, dv_ref, dkb_ref, dvb_ref
):
    def one_tree(tree, carry):
        at = places(order_ref, tree)
        for within in range(TRUNK):
            rows = slice(within * BLK, (within + 1) * BLK)
            spot = at(within)
            keys = load(x_ref, 1, spot)
            k_ref[rows, :] = keys
            kt_ref[:, rows] = across(keys)
            v_ref[rows, :] = load(x_ref, 2, spot)

        def attend(spots, far_rows, near_spots, mask, start):
            queries = load(x_ref, 0, *spots)
            grads = jnp.concatenate(
                [dy_ref[spots[0][0], spots[0][1]], dy_ref[spots[1][0], spots[1][1]]], axis=0
            )
            near_keys = load(x_ref, 1, *near_spots)
            near_values = load(x_ref, 2, *near_spots)
            far, near = softmax_parts(
                queries, k_ref[:far_rows, :] if far_rows else None, near_keys, mask
            )
            near_grad = nt(near_values, grads)
            inner = jnp.sum(near * near_grad, axis=0, keepdims=True)
            if far_rows:
                far_grad = nt(v_ref[:far_rows, :], grads)
                inner = inner + jnp.sum(far * far_grad, axis=0, keepdims=True)
                far_score = (far * (far_grad - inner)).astype(bf16)
                far_dk = nn(far_score, queries)
                far_dv = nn(far.astype(bf16), grads)
                if start:
                    dk_ref[:far_rows, :] = far_dk
                    dv_ref[:far_rows, :] = far_dv
                else:
                    dk_ref[:far_rows, :] += far_dk
                    dv_ref[:far_rows, :] += far_dv
            near_score = (near * (near_grad - inner)).astype(bf16)
            turned = nn(across(near_keys), near_score)
            if far_rows:
                turned = turned + nn(kt_ref[:, :far_rows], far_score)
            rows = (jnp.transpose(turned) * SCALING).astype(bf16)
            out_ref[spots[0][0], 0, spots[0][1]] = rows[:BLK]
            out_ref[spots[1][0], 0, spots[1][1]] = rows[BLK:]
            return nn(near_score, queries), nn(near.astype(bf16), grads)

        def store(spot, key_grad, value_grad):
            out_ref[spot[0], 1, spot[1]] = (key_grad * SCALING).astype(bf16)
            out_ref[spot[0], 2, spot[1]] = value_grad.astype(bf16)

        under = apart_mask(BLK)
        for branch in range(BRANCHES):
            first = TRUNK + BRANCHES + LEAVES * branch
            spots = (at(first), at(first + 1))
            key_grad, value_grad = attend(
                spots, TRUNK_ROWS, (at(TRUNK + branch),) + spots, under, branch == 0
            )
            dkb_ref[branch] = key_grad[:BLK]
            dvb_ref[branch] = value_grad[:BLK]
            store(spots[0], key_grad[BLK : 2 * BLK], value_grad[BLK : 2 * BLK])
            store(spots[1], key_grad[2 * BLK :], value_grad[2 * BLK :])
        apart = apart_mask(0)
        for pair in range(BRANCHES // 2):
            spots = (at(TRUNK + 2 * pair), at(TRUNK + 2 * pair + 1))
            key_grad, value_grad = attend(spots, TRUNK_ROWS, spots, apart, False)
            for half in range(2):
                rows = slice(half * BLK, (half + 1) * BLK)
                branch = 2 * pair + half
                store(
                    spots[half], key_grad[rows] + dkb_ref[branch], value_grad[rows] + dvb_ref[branch]
                )
        causal = causal_mask()
        for pair in reversed(range(TRUNK // 2)):
            spots = (at(2 * pair), at(2 * pair + 1))
            key_grad, value_grad = attend(spots, pair * PAIR, spots, causal, False)
            for half in range(2):
                rows = slice(half * BLK, (half + 1) * BLK)
                held = slice(pair * PAIR + half * BLK, pair * PAIR + (half + 1) * BLK)
                store(
                    spots[half],
                    key_grad[rows] + dk_ref[held, :],
                    value_grad[rows] + dv_ref[held, :],
                )
        return carry

    lax.fori_loop(0, trees, one_tree, 0)


def attend_backward(order, packed, grads):
    groups = packed.shape[0]
    blocks = packed.shape[2]
    trees = groups * blocks // TREE_BLOCKS
    pairs = trees * TREE_BLOCKS * BLK * 1100
    return pl.pallas_call(
        functools.partial(backward_kernel, trees),
        in_specs=[
            pl.BlockSpec(memory_space=pltpu.SMEM),
            pl.BlockSpec(memory_space=pltpu.VMEM),
            pl.BlockSpec(memory_space=pltpu.VMEM),
        ],
        out_specs=pl.BlockSpec(memory_space=pltpu.VMEM),
        out_shape=jax.ShapeDtypeStruct(packed.shape, bf16),
        scratch_shapes=[
            pltpu.VMEM((TRUNK_ROWS, HEAD), bf16),
            pltpu.VMEM((HEAD, TRUNK_ROWS), bf16),
            pltpu.VMEM((TRUNK_ROWS, HEAD), bf16),
            pltpu.VMEM((TRUNK_ROWS, HEAD), f32),
            pltpu.VMEM((TRUNK_ROWS, HEAD), f32),
            pltpu.VMEM((BRANCHES, BLK, HEAD), f32),
            pltpu.VMEM((BRANCHES, BLK, HEAD), f32),
        ],
        compiler_params=pltpu.CompilerParams(vmem_limit_bytes=VMEM_LIMIT),
        cost_estimate=pl.CostEstimate(
            flops=pairs * HEAD * 10, bytes_accessed=packed.size * 5, transcendentals=pairs
        ),
        name="attend_backward",
    )(order, packed, grads)


def mean_square(values):
    return jnp.mean(values * values, axis=-1, keepdims=True)


def norm_back(gradient, normed, inverse, gain_vec):
    weighted = gradient * gain_vec
    return inverse * (weighted - normed * jnp.mean(normed * weighted, axis=-1, keepdims=True))


def chunk_call(kernel, ins, outs, kept, grid, scratch, cost, name):
    count = len(ins)
    specs = [spec for spec, _ in ins]
    values = [value for _, value in ins]
    aliases = {}
    if kept is not None:
        whole = [at for at, out in enumerate(outs) if out[2]]
        for at, value in zip(whole, kept):
            aliases[len(values)] = at
            specs.append(pl.BlockSpec(memory_space=pl.ANY))
            values.append(value)
    extra = len(values) - count

    def body(*refs):
        kernel(*refs[:count], *refs[count + extra :])

    return pl.pallas_call(
        body,
        grid=grid,
        in_specs=specs,
        out_specs=[out[0] for out in outs],
        out_shape=[out[1] for out in outs],
        scratch_shapes=scratch,
        input_output_aliases=aliases,
        compiler_params=pltpu.CompilerParams(vmem_limit_bytes=VMEM_LIMIT),
        cost_estimate=cost,
        name=name,
    )(*values)


def forward_chunk_kernel(
    place,
    core_ref,
    gain_ref,
    y_hbm,
    x_hbm,
    woa_hbm,
    wob_hbm,
    wg_hbm,
    wr_hbm,
    proj_hbm,
    low_hbm,
    act_hbm,
    silu_hbm,
    slope_hbm,
    part_hbm,
    y_ref,
    x_ref,
    row_ref,
    gate_ref,
    up_ref,
    exact_ref,
    proj_ref,
    low_ref,
    act_ref,
    silu_ref,
    slope_ref,
    part_ref,
    y_sem,
    x_sem,
    row_sems,
    gate_sems,
    up_sems,
    out_sems,
    part_sems,
):
    at, batch, part = place
    rows = y_ref.shape[0]
    units = act_ref.shape[1]
    tiles = D // TILE
    half = tiles // 2
    unit_tiles = units // TILE
    here = pl.ds(at * rows, rows)

    def tile(index):
        return pl.ds(pl.multiple_of(index * TILE, TILE), TILE)

    def out_tile(source, index):
        slot = index if source is woa_hbm else index + half
        return pltpu.make_async_copy(
            source.at[tile(index), :], row_ref.at[slot], row_sems.at[slot]
        )

    def unit_copies(index):
        slot = lax.rem(index, 2)
        return (
            pltpu.make_async_copy(wg_hbm.at[0, :, tile(index)], gate_ref.at[slot], gate_sems.at[slot]),
            pltpu.make_async_copy(wr_hbm.at[0, :, tile(index)], up_ref.at[slot], up_sems.at[slot]),
        )

    def down_copy(index):
        return pltpu.make_async_copy(
            wr_hbm.at[1, tile(index), :], row_ref.at[index, :, pl.ds(0, units)], row_sems.at[index]
        )

    def row_wait(index, width):
        pltpu.make_async_copy(
            woa_hbm.at[pl.ds(0, TILE), pl.ds(0, width)],
            row_ref.at[index, :, pl.ds(0, width)],
            row_sems.at[index],
        ).wait()

    y_copy = pltpu.make_async_copy(y_hbm.at[pl.ds(part * rows, rows), :], y_ref, y_sem)
    x_copy = pltpu.make_async_copy(x_hbm.at[batch, pl.ds(part * rows, rows), :], x_ref, x_sem)
    y_copy.start()
    for index in range(half):
        out_tile(woa_hbm, index).start()
    x_copy.start()
    y_copy.wait()

    def project_tile(index, carry):
        row_wait(index, D)

        @pl.when(index < half)
        def _():
            out_tile(wob_hbm, index).start()

        @pl.when(index >= half)
        def _():
            for copy in unit_copies(index - half):
                copy.start()

        side = jnp.where(index < half, core_ref[0], 1 - core_ref[0])
        columns = tile(side * half + lax.rem(index, half))
        exact_ref[:, columns] = nt(y_ref[...], row_ref[index])
        return carry

    lax.fori_loop(0, tiles, project_tile, 0)
    x_copy.wait()
    proj = exact_ref[...]
    inverse = lax.rsqrt(mean_square(proj) + EPSILON)
    proj_ref[...] = proj.astype(bf16)
    low_ref[...] = (x_ref[...].astype(f32) + proj * inverse * gain_ref[...]).astype(bf16)
    outs = [
        pltpu.make_async_copy(proj_ref, proj_hbm.at[here, :], out_sems.at[0]),
        pltpu.make_async_copy(low_ref, low_hbm.at[here, :], out_sems.at[1]),
        pltpu.make_async_copy(act_ref, act_hbm.at[here, :], out_sems.at[2]),
        pltpu.make_async_copy(silu_ref, silu_hbm.at[here, :], out_sems.at[3]),
        pltpu.make_async_copy(slope_ref, slope_hbm.at[here, :], out_sems.at[4]),
    ]
    outs[0].start()
    outs[1].start()

    def unit_tile(index, carry):
        slot = lax.rem(index, 2)
        for copy in unit_copies(index):
            copy.wait()
        low = low_ref[...]
        gate = nn(low, gate_ref[slot])
        up = nn(low, up_ref[slot])

        @pl.when(index + 2 < unit_tiles)
        def _():
            for copy in unit_copies(index + 2):
                copy.start()

        @pl.when(index + 2 >= unit_tiles)
        def _():
            first = (index + 2 - unit_tiles) * half
            for more in range(half):
                down_copy(first + more).start()

        sigmoid = 1.0 / (1.0 + jnp.exp(-gate))
        silu = gate * sigmoid
        columns = tile(index)
        act_ref[:, columns] = (silu * up).astype(bf16)
        silu_ref[:, columns] = silu.astype(bf16)
        slope_ref[:, columns] = (up * sigmoid * (1.0 + gate * (1.0 - sigmoid))).astype(bf16)
        return carry

    lax.fori_loop(0, unit_tiles, unit_tile, 0)
    for copy in outs[2:]:
        copy.start()

    def part_copy(index):
        columns = tile(index)
        return pltpu.make_async_copy(
            part_ref.at[:, columns], part_hbm.at[:, columns], part_sems.at[index]
        )

    def down_tile(index, carry):
        row_wait(index, units)
        part_ref[:, tile(index)] = nt(act_ref[...], row_ref[index, :, :units]).astype(bf16)
        part_copy(index).start()
        return carry

    lax.fori_loop(0, tiles, down_tile, 0)
    for index in range(tiles):
        part_copy(index).wait()
    for copy in outs:
        copy.wait()


def forward_chunk(at, batch, part, rows, y_all, tokens, gain, w_out, w_mlp, kept):
    core, w_out_a, w_out_b = w_out
    w_gate, w_rest = w_mlp
    units = w_gate.shape[2]
    total = tokens.shape[0] * tokens.shape[1]
    tiles = D // TILE
    anywhere = pl.BlockSpec(memory_space=pl.ANY)
    wide = jax.ShapeDtypeStruct((total, units), bf16)
    narrow = jax.ShapeDtypeStruct((total, D), bf16)
    dma = pltpu.SemaphoreType.DMA
    return chunk_call(
        functools.partial(forward_chunk_kernel, (at, batch, part)),
        [
            (pl.BlockSpec(memory_space=pltpu.SMEM), core),
            (pl.BlockSpec(memory_space=pltpu.VMEM), gain),
            (anywhere, y_all),
            (anywhere, tokens),
            (anywhere, w_out_a),
            (anywhere, w_out_b),
            (anywhere, w_gate),
            (anywhere, w_rest),
        ],
        [
            (anywhere, narrow, True),
            (anywhere, narrow, True),
            (anywhere, wide, True),
            (anywhere, wide, True),
            (anywhere, wide, True),
            (anywhere, jax.ShapeDtypeStruct((rows, D), bf16), False),
        ],
        kept,
        (),
        [
            pltpu.VMEM((rows, D), bf16),
            pltpu.VMEM((rows, D), bf16),
            pltpu.VMEM((tiles, TILE, D), bf16),
            pltpu.VMEM((2, D, TILE), bf16),
            pltpu.VMEM((2, D, TILE), bf16),
            pltpu.VMEM((rows, D), f32),
            pltpu.VMEM((rows, D), bf16),
            pltpu.VMEM((rows, D), bf16),
            pltpu.VMEM((rows, units), bf16),
            pltpu.VMEM((rows, units), bf16),
            pltpu.VMEM((rows, units), bf16),
            pltpu.VMEM((rows, D), bf16),
            dma,
            dma,
            dma((tiles,)),
            dma((2,)),
            dma((2,)),
            dma((5,)),
            dma((tiles,)),
        ],
        pl.CostEstimate(
            flops=2 * rows * D * (D + 3 * units),
            bytes_accessed=2 * D * (D + 3 * units) + 16 * rows * D,
            transcendentals=rows * units,
        ),
        "forward_chunk",
    )


def middle_chunk_kernel(
    place,
    attn_gain_ref,
    gain_ref,
    sum_hbm,
    proj_hbm,
    x_hbm,
    grad_hbm,
    silu_hbm,
    slope_hbm,
    wg_hbm,
    wr_hbm,
    output_hbm,
    low_hbm,
    gate_hbm,
    up_hbm,
    gain_part_ref,
    part_hbm,
    sum_ref,
    proj_ref,
    x_ref,
    grad_ref,
    silu_ref,
    slope_ref,
    down_ref,
    wg_ref,
    wu_ref,
    output_ref,
    low_ref,
    gates_ref,
    ups_ref,
    part_ref,
    in_sems,
    down_sems,
    wg_sems,
    wu_sems,
    out_sems,
    part_sems,
):
    at, batch, part = place
    rows = sum_ref.shape[0]
    units = silu_ref.shape[1]
    tiles = D // TILE
    half = tiles // 2
    unit_tiles = units // TILE
    here = pl.ds(at * rows, rows)
    inside = pl.ds(part * rows, rows)

    def tile(index):
        return pl.ds(pl.multiple_of(index * TILE, TILE), TILE)

    def down_copy(index):
        slot = lax.rem(index, 2)
        return pltpu.make_async_copy(
            wr_hbm.at[1, :, tile(index)], down_ref.at[slot], down_sems.at[slot]
        )

    def row_copies(index):
        slot = lax.rem(index, half)
        return (
            pltpu.make_async_copy(wg_hbm.at[0, tile(index), :], wg_ref.at[slot], wg_sems.at[slot]),
            pltpu.make_async_copy(wr_hbm.at[0, tile(index), :], wu_ref.at[slot], wu_sems.at[slot]),
        )

    ins = [
        pltpu.make_async_copy(sum_hbm, sum_ref, in_sems.at[0]),
        pltpu.make_async_copy(grad_hbm.at[batch, inside, :], grad_ref, in_sems.at[1]),
        pltpu.make_async_copy(proj_hbm.at[here, :], proj_ref, in_sems.at[2]),
        pltpu.make_async_copy(x_hbm.at[batch, inside, :], x_ref, in_sems.at[3]),
        pltpu.make_async_copy(silu_hbm.at[here, :], silu_ref, in_sems.at[4]),
        pltpu.make_async_copy(slope_hbm.at[here, :], slope_ref, in_sems.at[5]),
    ]
    ins[0].start()
    ins[1].start()
    down_copy(0).start()
    ins[4].start()
    ins[5].start()
    down_copy(1).start()
    ins[2].start()
    ins[3].start()
    ins[0].wait()
    ins[1].wait()
    mlp = sum_ref[...].astype(f32)
    mlp_inverse = lax.rsqrt(mean_square(mlp) + EPSILON)
    normed = mlp * mlp_inverse
    grad = grad_ref[...]
    gain_part_ref[...] = jnp.sum(grad * normed, axis=0, keepdims=True)
    low_ref[...] = norm_back(grad, normed, mlp_inverse, gain_ref[...]).astype(bf16)
    outs = [
        pltpu.make_async_copy(output_ref, output_hbm.at[here, :], out_sems.at[0]),
        pltpu.make_async_copy(low_ref, low_hbm.at[here, :], out_sems.at[1]),
        pltpu.make_async_copy(gates_ref, gate_hbm.at[here, :], out_sems.at[2]),
        pltpu.make_async_copy(ups_ref, up_hbm.at[here, :], out_sems.at[3]),
    ]
    outs[1].start()
    ins[4].wait()
    ins[5].wait()

    def unit_tile(index, carry):
        down_copy(index).wait()
        act_grad = nn(low_ref[...], down_ref[lax.rem(index, 2)])

        @pl.when(index + 2 < unit_tiles)
        def _():
            down_copy(index + 2).start()

        @pl.when(index + 2 >= unit_tiles)
        def _():
            for copy in row_copies(index + 2 - unit_tiles):
                copy.start()

        columns = tile(index)
        ups_ref[:, columns] = (act_grad * silu_ref[:, columns].astype(f32)).astype(bf16)
        gates_ref[:, columns] = (act_grad * slope_ref[:, columns].astype(f32)).astype(bf16)
        return carry

    lax.fori_loop(0, unit_tiles, unit_tile, 0)
    outs[2].start()
    outs[3].start()
    ins[2].wait()
    ins[3].wait()
    proj = proj_ref[...].astype(f32)
    inverse = lax.rsqrt(mean_square(proj) + EPSILON)
    hidden = x_ref[...].astype(f32) + proj * inverse * attn_gain_ref[...]
    mlp = sum_ref[...].astype(f32)
    output_ref[...] = (hidden + mlp * mlp_inverse * gain_ref[...]).astype(bf16)
    outs[0].start()

    def part_copy(index):
        columns = tile(index)
        return pltpu.make_async_copy(
            part_ref.at[:, columns], part_hbm.at[:, columns], part_sems.at[index]
        )

    def row_tile(index, carry):
        slot = lax.rem(index, half)
        for copy in row_copies(index):
            copy.wait()
        part_ref[:, tile(index)] = (
            nt(gates_ref[...], wg_ref[slot]) + nt(ups_ref[...], wu_ref[slot])
        ).astype(bf16)
        part_copy(index).start()

        @pl.when(index + half < tiles)
        def _():
            for copy in row_copies(index + half):
                copy.start()

        return carry

    lax.fori_loop(0, tiles, row_tile, 0)
    for index in range(tiles):
        part_copy(index).wait()
    for copy in outs:
        copy.wait()


def middle_chunk(
    at, batch, part, rows, mlp_sum, proj, tokens, grad, attn_gain, gain, silu, slope, w_mlp, kept
):
    w_gate, w_rest = w_mlp
    units = w_gate.shape[2]
    total = proj.shape[0]
    tiles = D // TILE
    half = tiles // 2
    vmem = pl.BlockSpec(memory_space=pltpu.VMEM)
    anywhere = pl.BlockSpec(memory_space=pl.ANY)
    wide = jax.ShapeDtypeStruct((total, units), bf16)
    narrow = jax.ShapeDtypeStruct((total, D), bf16)
    dma = pltpu.SemaphoreType.DMA
    return chunk_call(
        functools.partial(middle_chunk_kernel, (at, batch, part)),
        [
            (vmem, attn_gain),
            (vmem, gain),
            (anywhere, mlp_sum),
            (anywhere, proj),
            (anywhere, tokens),
            (anywhere, grad),
            (anywhere, silu),
            (anywhere, slope),
            (anywhere, w_gate),
            (anywhere, w_rest),
        ],
        [
            (anywhere, narrow, True),
            (anywhere, narrow, True),
            (anywhere, wide, True),
            (anywhere, wide, True),
            (vmem, jax.ShapeDtypeStruct((1, D), f32), False),
            (anywhere, jax.ShapeDtypeStruct((rows, D), bf16), False),
        ],
        kept,
        (),
        [
            pltpu.VMEM((rows, D), bf16),
            pltpu.VMEM((rows, D), bf16),
            pltpu.VMEM((rows, D), bf16),
            pltpu.VMEM((rows, D), f32),
            pltpu.VMEM((rows, units), bf16),
            pltpu.VMEM((rows, units), bf16),
            pltpu.VMEM((2, D, TILE), bf16),
            pltpu.VMEM((half, TILE, units), bf16),
            pltpu.VMEM((half, TILE, units), bf16),
            pltpu.VMEM((rows, D), bf16),
            pltpu.VMEM((rows, D), bf16),
            pltpu.VMEM((rows, units), bf16),
            pltpu.VMEM((rows, units), bf16),
            pltpu.VMEM((rows, D), bf16),
            dma((6,)),
            dma((2,)),
            dma((half,)),
            dma((half,)),
            dma((4,)),
            dma((tiles,)),
        ],
        pl.CostEstimate(
            flops=2 * rows * D * 3 * units,
            bytes_accessed=2 * D * 3 * units + 24 * rows * D,
            transcendentals=rows,
        ),
        "middle_chunk",
    )


def backward_chunk_kernel(
    heads, sum_ref, grad_ref, proj_ref, gain_ref, wo_ref, hidden_ref, low_ref, dy_ref, gain_part_ref
):
    hidden_grad = grad_ref[...] + sum_ref[...].astype(f32)
    proj = proj_ref[...].astype(f32)
    inverse = lax.rsqrt(mean_square(proj) + EPSILON)
    normed = proj * inverse
    hidden_ref[...] = hidden_grad
    gain_part_ref[...] = jnp.sum(hidden_grad * normed, axis=0, keepdims=True)
    low = norm_back(hidden_grad, normed, inverse, gain_ref[...]).astype(bf16)
    low_ref[...] = low
    grad = nn(low, wo_ref[...])
    for head in range(heads):
        dy_ref[head] = grad[:, head_cols(head)].astype(bf16)


def backward_chunk(at, batch, part, rows, branch_sum, grad, proj, gain, w_attn, kept):
    total = proj.shape[0]
    width = w_attn.shape[2]
    heads = width // HEAD
    whole = pl.BlockSpec((rows, D), lambda s: (at, 0))
    line = pl.BlockSpec((1, D), lambda s: (0, 0))
    return chunk_call(
        functools.partial(backward_chunk_kernel, heads),
        [
            (pl.BlockSpec((rows, D), lambda s: (0, 0)), branch_sum),
            (pl.BlockSpec((None, rows, D), lambda s: (batch, part, 0)), grad),
            (whole, proj),
            (line, gain),
            (pl.BlockSpec((None, D, width), lambda s: (3, 0, 0)), w_attn),
        ],
        [
            (whole, jax.ShapeDtypeStruct((total, D), f32), True),
            (whole, jax.ShapeDtypeStruct((total, D), bf16), True),
            (
                pl.BlockSpec((heads, rows, HEAD), lambda s: (0, at, 0)),
                jax.ShapeDtypeStruct((heads, total, HEAD), bf16),
                True,
            ),
            (line, jax.ShapeDtypeStruct((1, D), f32), False),
        ],
        kept,
        (1,),
        [],
        pl.CostEstimate(
            flops=2 * rows * D * width, bytes_accessed=16 * rows * D, transcendentals=rows
        ),
        "backward_chunk",
    )


def weight_sum_kernel(count, left_ref, right_ref, out_ref):
    units = out_ref.shape[2]
    for at in range(count):
        out_ref[at] = lax.dot_general(
            left_ref[...],
            right_ref[:, at * units : (at + 1) * units],
            (((0,), (0,)), ((), ())),
            preferred_element_type=f32,
        ).astype(bf16)


def weight_sum(first, slots, count, left, right, kept):
    rows, depth = left.shape
    units = right.shape[1] // slots
    return chunk_call(
        functools.partial(weight_sum_kernel, slots),
        [
            (pl.BlockSpec((rows, TILE), lambda s: (0, s)), left),
            (pl.BlockSpec((rows, slots * units), lambda s: (0, 0)), right),
        ],
        [
            (
                pl.BlockSpec((slots, TILE, units), lambda s: (first // slots, s, 0)),
                jax.ShapeDtypeStruct((count, depth, units), bf16),
                True,
            )
        ],
        kept,
        (depth // TILE,),
        [],
        pl.CostEstimate(
            flops=2 * rows * depth * units * slots,
            bytes_accessed=2 * slots * (rows * depth + rows * units + depth * units),
            transcendentals=0,
        ),
        "weight_sum",
    )


def shards(
    layer_input,
    cotangent,
    w_query,
    w_key,
    w_value,
    w_output,
    w_gate,
    w_up,
    w_down,
    query_gain,
    key_gain,
    attn_gain,
    mlp_gain,
    slot_parent,
    slot_depth,
):
    dp_index = lax.axis_index("dp")
    tp_index = lax.axis_index("tensor")
    dp_count = lax.axis_size("dp")
    tp_count = lax.axis_size("tensor")
    rows = layer_input.shape[1]
    share = rows // tp_count
    width = w_query.shape[1]
    heads = width // HEAD
    hidden_width = w_gate.shape[1]
    items = heads * MB
    copies = dp_count // items

    def gather_stack(*pieces):
        return lax.all_gather(jnp.stack(pieces), "dp", axis=1, tiled=True)

    def scatter_rows(total, dimension=0):
        return lax.psum_scatter(
            total.astype(bf16), "dp", scatter_dimension=dimension, tiled=True
        )

    def exchange(pieces):
        flat = pieces.reshape((items, -1, HEAD))
        if copies > 1:
            flat = jnp.tile(flat, (copies, 1, 1))
        return lax.all_to_all(flat, "dp", split_axis=0, concat_axis=0, tiled=True)

    def give_back(pieces):
        flat = pieces.reshape((dp_count, -1, HEAD))
        return lax.all_to_all(flat, "dp", split_axis=0, concat_axis=0, tiled=True)[:items]

    w_attn = gather_stack(w_query, w_key, w_value, jnp.transpose(w_output))
    w_gate_all = gather_stack(w_gate)

    order = tree_order(slot_parent, slot_depth)
    my_batch = lax.rem(lax.rem(dp_index, items), MB)
    my_order = lax.dynamic_index_in_dim(order, my_batch, 0, keepdims=False)
    my_depth = lax.dynamic_slice_in_dim(slot_depth, dp_index * SEG_DEV, SEG_DEV, 1)
    cosines, sines = rope_tables(my_depth)

    q_raw, k_raw, squares = project(layer_input, w_attn, (0, 1), True)
    squares = jnp.transpose(squares.reshape(MB * rows, 2))
    (v_raw,) = project(layer_input, w_attn, (2,), False)
    squares = small_sum(squares, "tensor", tp_count)
    inverse = jnp.transpose(lax.rsqrt(squares / D + EPSILON)).reshape(MB, rows, 2)
    gains = jnp.concatenate([query_gain, key_gain])[None, :]
    packed = pack_heads(q_raw, k_raw, v_raw, inverse, gains, cosines, sines, heads)
    w_out_begun = begin_output_weight(w_attn[3], packed, dp_index, dp_count, tp_count)
    packed = follow(exchange(packed), w_out_begun[1:]).reshape(dp_count, 3, SEG_DEV, BLK, HEAD)
    w_out = end_output_weight(w_out_begun, packed, dp_index, dp_count, tp_count)
    w_mlp = (w_gate_all, gather_stack(*follow((w_up, jnp.transpose(w_down)), packed)))

    attended = give_back(attend_forward(my_order, packed))
    attended = attended.reshape(heads, MB, rows, HEAD).transpose(1, 2, 0, 3)
    attended = attended.reshape(MB, rows, width)

    parts = 2
    step = rows // parts
    spots = [(batch, part) for batch in range(MB) for part in range(parts)]
    begun = go_on_all_gather(begin_all_gather(attended[0], tp_count), tp_count)
    gathered, hop = end_all_gather(begun, tp_count)
    everything = [gathered]
    begun = [begun]
    for batch in range(1, MB):
        begun.append(begin_all_gather(follow(attended[batch], hop), tp_count))
    sums = SumLine(tp_count)
    attn_gain_row = attn_gain[None, :]
    mlp_gain_row = mlp_gain[None, :]
    chunks = len(spots)
    state = dict(forward=None, middle=None, backward=None)
    mlp_gain_parts = []
    attn_gain_parts = []

    def forward(at, after):
        batch, part = spots[at]
        if batch == len(everything):
            early = sums.terms[0] if sums.terms else None
            going = go_on_all_gather(begun[batch], tp_count)
            everything.append(end_all_gather(going, tp_count, early)[0])
        *state["forward"], term = forward_chunk(
            at,
            batch,
            part,
            step,
            follow(everything[batch], after),
            layer_input,
            attn_gain_row,
            w_out,
            w_mlp,
            state["forward"],
        )
        return term

    def middle(at, after):
        batch, part = spots[at]
        proj, _, _, silu, slope = state["forward"]
        *kept, gain_part, term = middle_chunk(
            at,
            batch,
            part,
            step,
            follow(sums.sums[at], after),
            proj,
            layer_input,
            cotangent,
            attn_gain_row,
            mlp_gain_row,
            silu,
            slope,
            w_mlp,
            state["middle"],
        )
        state["middle"] = kept
        mlp_gain_parts.append(gain_part)
        return term

    def backward(at, after):
        batch, part = spots[at]
        *kept, gain_part = backward_chunk(
            at,
            batch,
            part,
            step,
            follow(sums.sums[chunks + at], after),
            cotangent,
            state["forward"][0],
            attn_gain_row,
            w_attn,
            state["backward"],
        )
        state["backward"] = kept
        attn_gain_parts.append(gain_part)
        return gain_part

    sums.enter(forward(0, None))
    sums.enter(forward(1, None))
    last = None
    mlp_total = None
    for at in range(2 * chunks + 2):
        after = sums.terms[-1] if last is None and tp_count == 4 else last
        moved = tuple(sums.advance(after)) or None
        coming = at + 2
        if coming < chunks:
            last = forward(coming, moved)
            sums.enter(last)
        elif coming < 2 * chunks:
            last = middle(coming - chunks, moved)
            sums.enter(last)
        else:
            last = backward(coming - 2 * chunks, moved)
            turn_at = coming - 2 * chunks
            output, mlp_grad, gate_grad, up_grad = state["middle"]
            hidden_low, act = state["forward"][1:3]
            left, right = (
                (hidden_low, gate_grad),
                (hidden_low, up_grad),
                (mlp_grad, act),
                (None, None),
            )[turn_at]
            if left is not None:
                mlp_total = weight_sum(turn_at, 1, 3, follow(left, last), right, mlp_total)
                last = mlp_total[0]
        if coming == 3 * chunks - 1:
            break
    hidden_grad, proj_grad, attn_grad = state["backward"]
    mlp_weight_grad = scatter_rows(follow(mlp_total[0], attn_grad), 1)
    attended = attended.reshape(MB * rows, width)
    attn_total = weight_sum(3, 1, 4, proj_grad, follow(attended, attn_grad), None)

    attn_grad = follow(exchange(attn_grad), attn_total)
    attn_grad = attn_grad.reshape(dp_count, SEG_DEV, BLK, HEAD)
    back = give_back(attend_backward(my_order, packed, attn_grad))
    back = back.reshape(heads, MB, 3, rows, HEAD)
    inner, gain_part = inner_sums(back, q_raw, k_raw, inverse, gains, cosines, sines, heads)
    means = small_sum(jnp.transpose(inner.reshape(-1, 2)), "tensor", tp_count) / D
    means = jnp.transpose(means).reshape(MB, rows, 2)
    qkv_grad = None
    terms = []
    for batch in range(MB):
        *qkv_grad, term = unpack_heads(
            batch, back, q_raw, k_raw, inverse, means, gains, cosines, sines, w_attn, heads, qkv_grad
        )
        terms.append(term)
    mlp_weight_grads = [
        mlp_weight_grad[0].astype(f32),
        mlp_weight_grad[1].astype(f32),
        jnp.transpose(mlp_weight_grad[2].astype(f32)),
    ]
    parts, early_operands, last_operands = line_reduce_scatter(terms, tp_count, mlp_weight_grads)
    tokens = layer_input.reshape(MB * rows, D)
    qkv_grad = follow(qkv_grad[0], early_operands[0])
    attn_total = weight_sum(0, 3, 4, tokens, qkv_grad, attn_total)
    attn_total = follow(attn_total[0], (mlp_weight_grad, early_operands[1]))
    attn_weight_grad = scatter_rows(attn_total, 1)
    attn_weight_grads = [attn_weight_grad[at].astype(f32) for at in range(4)]
    attn_weight_grads[3] = jnp.transpose(attn_weight_grads[3])
    parts[-1] = (follow(parts[-1][0], attn_weight_grads),) + parts[-1][1:]
    input_parts = [
        lax.dynamic_slice_in_dim(hidden_grad, batch * rows + tp_index * share, share, 0)
        + sum(piece.astype(f32) for piece in part)
        for batch, part in enumerate(parts)
    ]

    gain_sums = jnp.concatenate(
        [
            gain_part[0],
            sum(attn_gain_parts)[0],
            sum(mlp_gain_parts)[0],
        ]
    )
    gain_sums = follow(gain_sums.reshape(-1, HEAD), last_operands)
    gain_sums = small_sum(gain_sums, "dp", dp_count).reshape(-1)
    return (
        output.reshape(MB, rows, D),
        jnp.stack(input_parts),
        *attn_weight_grads,
        *mlp_weight_grads,
        gain_sums[:width],
        gain_sums[width : 2 * width],
        gain_sums[2 * width : 2 * width + D],
        gain_sums[2 * width + D :],
    )


def solution(mesh):
    in_specs = (
        P(None, "dp", None),
        P(None, "dp", None),
        P("dp", "tensor"),
        P("dp", "tensor"),
        P("dp", "tensor"),
        P("tensor", "dp"),
        P("dp", "tensor"),
        P("dp", "tensor"),
        P("tensor", "dp"),
        P("tensor"),
        P("tensor"),
        P(),
        P(),
        P(),
        P(),
    )
    out_specs = (
        P(None, "dp", None),
        P(None, ("dp", "tensor"), None),
        P("dp", "tensor"),
        P("dp", "tensor"),
        P("dp", "tensor"),
        P("tensor", "dp"),
        P("dp", "tensor"),
        P("dp", "tensor"),
        P("tensor", "dp"),
        P("tensor"),
        P("tensor"),
        P(),
        P(),
    )
    return jax.shard_map(shards, mesh=mesh, in_specs=in_specs, out_specs=out_specs, check_vma=False)
```

```python
import functools

import jax
import jax.numpy as jnp
from jax import lax
from jax.experimental import pallas as pl
from jax.experimental.pallas import tpu as pltpu
from jax.sharding import PartitionSpec as P

D = 2048
HEADS = 16
HEAD = D // HEADS
BLK = 128
TRUNK = 8
BRANCHES = 4
LEAVES = 2
TREE_BLOCKS = 20
MB = 2
SEG_DEV = 5
PAIR = 2 * BLK
TRUNK_ROWS = TRUNK * BLK
TILE = 512

EPSILON = 1e-06
ROPE_BASE = 500000.0
SCALING = HEAD ** (-0.5)
VMEM_LIMIT = 50 * 1024 * 1024

f32 = jnp.float32
bf16 = jnp.bfloat16


def tree_order(parents, depths):
    blocks = parents.shape[1]
    ids = jnp.arange(blocks, dtype=jnp.int32)

    def follow(table, index):
        hot = index[:, :, None] == ids[None, None, :]
        return jnp.sum(jnp.where(hot, table[:, None, :], 0), axis=-1)

    up2 = follow(parents, parents)
    up4 = follow(up2, up2)
    up8 = follow(up4, up4)
    root = follow(up8, up8)
    is_leaf = depths == TRUNK + 1
    above = jnp.where(is_leaf, parents, 0)
    key = ((root * (TRUNK + 2) + depths) * blocks + above) * blocks + ids[None, :]
    rank = jnp.sum((key[:, None, :] < key[:, :, None]).astype(jnp.int32), axis=-1)
    return jnp.sum(
        jnp.where(rank[:, None, :] == ids[None, :, None], ids[None, None, :], 0), axis=-1
    ).astype(jnp.int32)


def rope_tables(depths):
    half = HEAD // 2
    offsets = jnp.arange(BLK, dtype=jnp.int32)
    places = (depths[:, :, None] * BLK + offsets).reshape(depths.shape[0], -1).astype(f32)
    frequency = ROPE_BASE ** (-2.0 * jnp.arange(half, dtype=f32) / HEAD)
    angles = places[:, :, None] * frequency
    cosines = jnp.cos(angles)
    sines = jnp.sin(angles)
    return (
        jnp.concatenate([cosines, cosines], -1),
        jnp.concatenate([-sines, sines], -1),
    )


def low_sum(*parts):
    total = parts[0].astype(f32)
    for part in parts[1:]:
        total = total + part.astype(f32)
    return total.astype(bf16)


def follow(values, after):
    if after is None:
        return values
    return lax.optimization_barrier((values, after))[0]


def small_sum(values, axis, count):
    step = 1
    while step < count:
        values = values + lax.ppermute(values, axis, [(i, i ^ step) for i in range(count)])
        step *= 2
    return values


class SumLine:
    def __init__(self, count):
        self.count = count
        index = lax.axis_index("tensor")
        self.inner = (index == 1) | (index == 2)
        self.terms = []
        self.inward = []
        self.sides = []
        self.across = []
        self.totals = []
        self.outward = []
        self.sums = []

    def enter(self, term):
        if self.count != 4:
            self.sums.append(lax.psum(term, "tensor"))
            return
        self.terms.append(term)
        self.inward.append(lax.ppermute(term, "tensor", [(0, 1), (3, 2)]))

    def advance(self, after):
        if self.count != 4:
            return []
        moved = []
        if len(self.sides) < len(self.terms):
            at = len(self.sides)
            side = low_sum(follow(self.terms[at], after), self.inward[at])
            self.sides.append(side)
            moved.append(side)
        at = len(self.totals)
        if at < len(self.sides) - 1 or (at < len(self.sides) and not moved):
            total = low_sum(follow(self.sides[at], after), self.across[at])
            self.totals.append(total)
            moved.append(total)
        at = len(self.sums)
        if at < len(self.outward):
            self.sums.append(
                jnp.where(self.inner, follow(self.totals[at], after), self.outward[at])
            )
        if len(self.across) < len(self.sides):
            self.across.append(lax.ppermute(self.sides[-1], "tensor", [(1, 2), (2, 1)]))
        if len(self.outward) < len(self.totals):
            self.outward.append(lax.ppermute(self.totals[-1], "tensor", [(1, 0), (2, 3)]))
        return moved


def line_reduce_scatter(batches, count, late):
    if count != 4:
        return [
            (lax.psum_scatter(values, "tensor", scatter_dimension=0, tiled=True),)
            for values in batches
        ], None, None
    index = lax.axis_index("tensor")
    rights = []
    lefts = []
    blocks = [item.reshape(count, item.shape[0] // count, item.shape[1]) for item in batches]

    def block(item, at):
        return lax.dynamic_index_in_dim(item, lax.rem(at + 2 * count, count), 0, keepdims=False)

    operands = []
    for stage in range(count - 1):
        to_right = [(i, i + 1) for i in range(stage + 1)]
        to_left = [(count - 1 - i, count - 2 - i) for i in range(stage + 1)]
        for at, item in enumerate(blocks):
            right = block(item, index + count - 1 - stage)
            left = block(item, index - count + 1 + stage)
            if at or stage:
                before = max(at - 1, 0)
                right, left = follow((right, left), (rights[before], lefts[before]))
            if stage:
                right = low_sum(right, rights[at])
                left = low_sum(left, lefts[at])
                if stage == 1 and at == len(blocks) - 1:
                    right, left = follow((right, left), late)
                rights[at] = lax.ppermute(right, "tensor", to_right)
                lefts[at] = lax.ppermute(left, "tensor", to_left)
            else:
                rights.append(lax.ppermute(right, "tensor", to_right))
                lefts.append(lax.ppermute(left, "tensor", to_left))
            operands.append((right, left))
    sums = [
        (block(item, index), right, left) for item, right, left in zip(blocks, rights, lefts)
    ]
    return sums, operands[1], operands[len(blocks)]


def begin_all_gather(values, count):
    if count != 4:
        return values, None
    right = lax.ppermute(values, "tensor", [(0, 1), (1, 2), (2, 3)])
    left = lax.ppermute(values, "tensor", [(3, 2), (2, 1), (1, 0)])
    return values, (right, left)


def go_on_all_gather(begun, count):
    values, first = begun
    if count != 4:
        return values, None, None
    right = lax.ppermute(first[0], "tensor", [(1, 2), (2, 3)])
    left = lax.ppermute(first[1], "tensor", [(2, 1), (1, 0)])
    return values, first, (right, left)


def end_all_gather(begun, count, after=None):
    values, first, second = begun
    if count != 4:
        return lax.all_gather(values, "tensor", axis=1, tiled=True), None
    index = lax.axis_index("tensor")
    width = values.shape[1]
    right, left = follow(second, after)
    right = lax.ppermute(right, "tensor", [(2, 3)])
    left = lax.ppermute(left, "tensor", [(1, 0)])
    whole = jnp.zeros((values.shape[0], count * width), values.dtype)
    pieces = (
        values,
        jnp.where(index >= 1, first[0], left),
        jnp.where(index >= 2, second[0], second[1]),
        jnp.where(index >= 3, right, first[1]),
    )
    for back, piece in enumerate(pieces):
        place = lax.rem(index - back + count, count) * width
        whole = lax.dynamic_update_slice(whole, piece, (0, place))
    return whole, (right, left)


def begin_output_weight(own, after, dp_index, dp_count, count):
    if count != 4 or dp_count % 2:
        return own, None, None
    half = own.shape[0] // 2
    mine = lax.dynamic_slice_in_dim(follow(own, after), lax.rem(dp_index, 2) * half, half, 0)
    return go_on_all_gather(begin_all_gather(mine, count), count)


def end_output_weight(begun, after, dp_index, dp_count, count):
    if count != 4 or dp_count % 2:
        whole = lax.all_gather(begun[0], "tensor", axis=1, tiled=True)
        half = whole.shape[0] // 2
        return jnp.zeros((1,), jnp.int32), whole[:half], whole[half:]
    mine, _ = end_all_gather(begun, count, after)
    other = lax.ppermute(mine, "dp", [(i, i ^ 1) for i in range(dp_count)])
    return lax.rem(dp_index, 2).astype(jnp.int32).reshape(1), mine, other


def turn(values, cosines, sines):
    return values * cosines + pltpu.roll(values, HEAD // 2, 1) * sines


def head_cols(head, group=0, heads=0):
    start = (group * heads + head) * HEAD
    return slice(start, start + HEAD)


def project_kernel(x_ref, *refs):
    count = len(refs) // 2 if len(refs) > 2 else 1
    weights, outs = refs[:count], refs[count:]
    for at in range(count):
        raw = jnp.dot(x_ref[0], weights[at][0], preferred_element_type=f32)
        outs[at][0] = raw.astype(outs[at].dtype)
        if len(outs) > count:
            outs[count][0, :, at : at + 1] = jnp.sum(raw * raw, axis=1, keepdims=True)


def project(tokens, weights, which, squares):
    batches, rows, _ = tokens.shape
    width = weights.shape[2]
    step = rows // 2
    dtype = f32 if squares else bf16
    out_specs = [pl.BlockSpec((1, step, width), lambda b, r: (b, r, 0))] * len(which)
    out_shape = [jax.ShapeDtypeStruct((batches, rows, width), dtype)] * len(which)
    if squares:
        out_specs.append(pl.BlockSpec((1, step, len(which)), lambda b, r: (b, r, 0)))
        out_shape.append(jax.ShapeDtypeStruct((batches, rows, len(which)), f32))
    return pl.pallas_call(
        project_kernel,
        grid=(batches, rows // step),
        in_specs=[pl.BlockSpec((1, step, D), lambda b, r: (b, r, 0))]
        + [pl.BlockSpec((1, D, width), lambda b, r, at=at: (at, 0, 0)) for at in which],
        out_specs=out_specs,
        out_shape=out_shape,
        compiler_params=pltpu.CompilerParams(vmem_limit_bytes=VMEM_LIMIT),
        cost_estimate=pl.CostEstimate(
            flops=2 * batches * rows * D * width * len(which),
            bytes_accessed=2 * batches * rows * D + 2 * D * width * len(which),
            transcendentals=0,
        ),
        name="project",
    )(tokens, *([weights] * len(which)))


def pack_kernel(heads, q_ref, k_ref, v_ref, inv_ref, gain_ref, cos_ref, sin_ref, out_ref):
    cosines = cos_ref[0]
    sines = sin_ref[0]
    for head in range(heads):
        for which in range(2):
            cols = head_cols(head, which, heads)
            raw_ref = (q_ref, k_ref)[which]
            normed = raw_ref[0, :, head_cols(head)] * inv_ref[0, :, which : which + 1] * gain_ref[:, cols]
            out_ref[head, 0, which] = turn(normed, cosines, sines).astype(bf16)
        out_ref[head, 0, 2] = v_ref[0, :, head_cols(head)]


def pack_heads(q_raw, k_raw, v_raw, inverse, gains, cosines, sines, heads):
    rows = q_raw.shape[1]
    step = rows // 2
    width = heads * HEAD
    return pl.pallas_call(
        functools.partial(pack_kernel, heads),
        grid=(MB, rows // step),
        in_specs=[
            pl.BlockSpec((1, step, width), lambda b, r: (b, r, 0)),
            pl.BlockSpec((1, step, width), lambda b, r: (b, r, 0)),
            pl.BlockSpec((1, step, width), lambda b, r: (b, r, 0)),
            pl.BlockSpec((1, step, 2), lambda b, r: (b, r, 0)),
            pl.BlockSpec((1, 2 * width), lambda b, r: (0, 0)),
            pl.BlockSpec((1, step, HEAD), lambda b, r: (b, r, 0)),
            pl.BlockSpec((1, step, HEAD), lambda b, r: (b, r, 0)),
        ],
        out_specs=pl.BlockSpec((heads, 1, 3, step, HEAD), lambda b, r: (0, b, 0, r, 0)),
        out_shape=jax.ShapeDtypeStruct((heads, MB, 3, rows, HEAD), bf16),
        name="pack_heads",
    )(q_raw, k_raw, v_raw, inverse, gains, cosines, sines)


def inner_kernel(heads, back_ref, q_ref, k_ref, inv_ref, gain_ref, cos_ref, sin_ref, inner_ref, part_ref):
    cosines = cos_ref[0]
    sines = -sin_ref[0]

    @pl.when((pl.program_id(0) == 0) & (pl.program_id(1) == 0))
    def _():
        part_ref[...] = jnp.zeros_like(part_ref)

    for which in range(2):
        total = None
        for head in range(heads):
            cols = head_cols(head, which, heads)
            straight = turn(back_ref[head, 0, which].astype(f32), cosines, sines)
            hat = (q_ref, k_ref)[which][0, :, head_cols(head)] * inv_ref[0, :, which : which + 1]
            product = straight * hat
            part_ref[:, cols] += jnp.sum(product, axis=0, keepdims=True)
            weighted = product * gain_ref[:, cols]
            total = weighted if total is None else total + weighted
        inner_ref[0, :, which : which + 1] = jnp.sum(total, axis=1, keepdims=True)


def inner_sums(back, q_raw, k_raw, inverse, gains, cosines, sines, heads):
    rows = q_raw.shape[1]
    step = rows // 2
    width = heads * HEAD
    return pl.pallas_call(
        functools.partial(inner_kernel, heads),
        grid=(MB, rows // step),
        in_specs=[
            pl.BlockSpec((heads, 1, 2, step, HEAD), lambda b, r: (0, b, 0, r, 0)),
            pl.BlockSpec((1, step, width), lambda b, r: (b, r, 0)),
            pl.BlockSpec((1, step, width), lambda b, r: (b, r, 0)),
            pl.BlockSpec((1, step, 2), lambda b, r: (b, r, 0)),
            pl.BlockSpec((1, 2 * width), lambda b, r: (0, 0)),
            pl.BlockSpec((1, step, HEAD), lambda b, r: (b, r, 0)),
            pl.BlockSpec((1, step, HEAD), lambda b, r: (b, r, 0)),
        ],
        out_specs=[
            pl.BlockSpec((1, step, 2), lambda b, r: (b, r, 0)),
            pl.BlockSpec((1, 2 * width), lambda b, r: (0, 0)),
        ],
        out_shape=[
            jax.ShapeDtypeStruct((MB, rows, 2), f32),
            jax.ShapeDtypeStruct((1, 2 * width), f32),
        ],
        name="inner_sums",
    )(back, q_raw, k_raw, inverse, gains, cosines, sines)


def unpack_kernel(
    heads,
    back_ref,
    q_ref,
    k_ref,
    inv_ref,
    mean_ref,
    gain_ref,
    cos_ref,
    sin_ref,
    wq_ref,
    wk_ref,
    wv_ref,
    grad_ref,
    term_ref,
):
    cosines = cos_ref[0]
    sines = -sin_ref[0]
    width = heads * HEAD
    for head in range(heads):
        for which in range(2):
            cols = head_cols(head, which, heads)
            inverse = inv_ref[0, :, which : which + 1]
            straight = turn(back_ref[head, 0, which].astype(f32), cosines, sines)
            hat = (q_ref, k_ref)[which][0, :, head_cols(head)] * inverse
            grad = inverse * (straight * gain_ref[:, cols] - hat * mean_ref[0, :, which : which + 1])
            grad_ref[:, cols] = grad.astype(bf16)
        grad_ref[:, head_cols(head, 2, heads)] = back_ref[head, 0, 2]
    term = nt(grad_ref[:, :width], wq_ref[0])
    term = term + nt(grad_ref[:, width : 2 * width], wk_ref[0])
    term = term + nt(grad_ref[:, 2 * width :], wv_ref[0])
    term_ref[...] = term.astype(bf16)


def unpack_heads(
    batch, back, q_raw, k_raw, inverse, means, gains, cosines, sines, weights, heads, kept
):
    rows = q_raw.shape[1]
    step = rows // 2
    width = heads * HEAD
    row_spec = lambda cols: pl.BlockSpec((1, step, cols), lambda r: (batch, r, 0))
    return chunk_call(
        functools.partial(unpack_kernel, heads),
        [
            (pl.BlockSpec((heads, 1, 3, step, HEAD), lambda r: (0, batch, 0, r, 0)), back),
            (row_spec(width), q_raw),
            (row_spec(width), k_raw),
            (row_spec(2), inverse),
            (row_spec(2), means),
            (pl.BlockSpec((1, 2 * width), lambda r: (0, 0)), gains),
            (row_spec(HEAD), cosines),
            (row_spec(HEAD), sines),
        ]
        + [(pl.BlockSpec((1, D, width), lambda r, at=at: (at, 0, 0)), weights) for at in range(3)],
        [
            (
                pl.BlockSpec((step, 3 * width), lambda r: (batch * 2 + r, 0)),
                jax.ShapeDtypeStruct((MB * rows, 3 * width), bf16),
                True,
            ),
            (
                pl.BlockSpec((step, D), lambda r: (r, 0)),
                jax.ShapeDtypeStruct((rows, D), bf16),
                False,
            ),
        ],
        kept,
        (2,),
        [],
        pl.CostEstimate(flops=6 * rows * D * width, bytes_accessed=8 * rows * D, transcendentals=0),
        "unpack_heads",
    )


def nt(left, right):
    return lax.dot_general(left, right, (((1,), (1,)), ((), ())), preferred_element_type=f32)


def nn(left, right):
    return lax.dot_general(left, right, (((1,), (0,)), ((), ())), preferred_element_type=f32)


def key_query_iotas(keys):
    key_at = lax.broadcasted_iota(jnp.int32, (keys, PAIR), 0)
    query_at = lax.broadcasted_iota(jnp.int32, (keys, PAIR), 1)
    return key_at, query_at


def causal_mask():
    key_at, query_at = key_query_iotas(PAIR)
    return key_at <= query_at


def apart_mask(above):
    key_at, query_at = key_query_iotas(above + PAIR)
    key_at = key_at - above
    own = (key_at <= query_at) & ((key_at < BLK) == (query_at < BLK))
    return own | (key_at < 0)


def softmax_parts(queries, trunk_keys, near_keys, mask):
    near = jnp.where(mask, nt(near_keys, queries), -1e30)
    top = jnp.max(near, axis=0, keepdims=True)
    if trunk_keys is None:
        near = jnp.exp((near - top) * SCALING)
        scale = 1.0 / jnp.sum(near, axis=0, keepdims=True)
        return None, near * scale
    far = nt(trunk_keys, queries)
    top = jnp.maximum(top, jnp.max(far, axis=0, keepdims=True))
    near = jnp.exp((near - top) * SCALING)
    far = jnp.exp((far - top) * SCALING)
    scale = 1.0 / (jnp.sum(near, axis=0, keepdims=True) + jnp.sum(far, axis=0, keepdims=True))
    return far * scale, near * scale


def places(order_ref, tree):
    def at(within):
        slot = order_ref[tree * TREE_BLOCKS + within]
        return lax.div(slot, SEG_DEV), lax.rem(slot, SEG_DEV)

    return at


def load(ref, which, *spots):
    parts = [ref[group, which, row] for group, row in spots]
    return parts[0] if len(parts) == 1 else jnp.concatenate(parts, axis=0)


def across(values):
    return jnp.transpose(values.astype(f32)).astype(bf16)


def forward_kernel(trees, order_ref, x_ref, y_ref, k_ref, vt_ref):
    def one_tree(tree, carry):
        at = places(order_ref, tree)
        for within in range(TRUNK):
            rows = slice(within * BLK, (within + 1) * BLK)
            spot = at(within)
            k_ref[rows, :] = load(x_ref, 1, spot)
            vt_ref[:, rows] = across(load(x_ref, 2, spot))

        def attend(spots, far_rows, near_keys, near_values, mask):
            queries = load(x_ref, 0, *spots)
            far, near = softmax_parts(
                queries, k_ref[:far_rows, :] if far_rows else None, near_keys, mask
            )
            summed = nn(across(near_values), near.astype(bf16))
            if far_rows:
                summed = summed + nn(vt_ref[:, :far_rows], far.astype(bf16))
            rows = jnp.transpose(summed).astype(bf16)
            y_ref[spots[0][0], spots[0][1]] = rows[:BLK]
            y_ref[spots[1][0], spots[1][1]] = rows[BLK:]

        causal = causal_mask()
        for pair in range(TRUNK // 2):
            spots = (at(2 * pair), at(2 * pair + 1))
            attend(spots, pair * PAIR, load(x_ref, 1, *spots), load(x_ref, 2, *spots), causal)
        apart = apart_mask(0)
        for pair in range(BRANCHES // 2):
            spots = (at(TRUNK + 2 * pair), at(TRUNK + 2 * pair + 1))
            attend(spots, TRUNK_ROWS, load(x_ref, 1, *spots), load(x_ref, 2, *spots), apart)
        under = apart_mask(BLK)
        for branch in range(BRANCHES):
            first = TRUNK + BRANCHES + LEAVES * branch
            spots = (at(first), at(first + 1))
            near = (at(TRUNK + branch),) + spots
            attend(spots, TRUNK_ROWS, load(x_ref, 1, *near), load(x_ref, 2, *near), under)
        return carry

    lax.fori_loop(0, trees, one_tree, 0)


def attend_forward(order, packed):
    groups = packed.shape[0]
    blocks = packed.shape[2]
    trees = groups * blocks // TREE_BLOCKS
    pairs = trees * TREE_BLOCKS * BLK * 1100
    return pl.pallas_call(
        functools.partial(forward_kernel, trees),
        in_specs=[
            pl.BlockSpec(memory_space=pltpu.SMEM),
            pl.BlockSpec(memory_space=pltpu.VMEM),
        ],
        out_specs=pl.BlockSpec(memory_space=pltpu.VMEM),
        out_shape=jax.ShapeDtypeStruct((groups, blocks, BLK, HEAD), bf16),
        scratch_shapes=[
            pltpu.VMEM((TRUNK_ROWS, HEAD), bf16),
            pltpu.VMEM((HEAD, TRUNK_ROWS), bf16),
        ],
        compiler_params=pltpu.CompilerParams(vmem_limit_bytes=VMEM_LIMIT),
        cost_estimate=pl.CostEstimate(
            flops=pairs * HEAD * 4, bytes_accessed=packed.size * 3, transcendentals=pairs
        ),
        name="attend_forward",
    )(order, packed)


def backward_kernel(
    trees, order_ref, x_ref, dy_ref, out_ref, k_ref, kt_ref, v_ref, dk_ref, dv_ref, dkb_ref, dvb_ref
):
    def one_tree(tree, carry):
        at = places(order_ref, tree)
        for within in range(TRUNK):
            rows = slice(within * BLK, (within + 1) * BLK)
            spot = at(within)
            keys = load(x_ref, 1, spot)
            k_ref[rows, :] = keys
            kt_ref[:, rows] = across(keys)
            v_ref[rows, :] = load(x_ref, 2, spot)

        def attend(spots, far_rows, near_spots, mask, start):
            queries = load(x_ref, 0, *spots)
            grads = jnp.concatenate(
                [dy_ref[spots[0][0], spots[0][1]], dy_ref[spots[1][0], spots[1][1]]], axis=0
            )
            near_keys = load(x_ref, 1, *near_spots)
            near_values = load(x_ref, 2, *near_spots)
            far, near = softmax_parts(
                queries, k_ref[:far_rows, :] if far_rows else None, near_keys, mask
            )
            near_grad = nt(near_values, grads)
            inner = jnp.sum(near * near_grad, axis=0, keepdims=True)
            if far_rows:
                far_grad = nt(v_ref[:far_rows, :], grads)
                inner = inner + jnp.sum(far * far_grad, axis=0, keepdims=True)
                far_score = (far * (far_grad - inner)).astype(bf16)
                far_dk = nn(far_score, queries)
                far_dv = nn(far.astype(bf16), grads)
                if start:
                    dk_ref[:far_rows, :] = far_dk
                    dv_ref[:far_rows, :] = far_dv
                else:
                    dk_ref[:far_rows, :] += far_dk
                    dv_ref[:far_rows, :] += far_dv
            near_score = (near * (near_grad - inner)).astype(bf16)
            turned = nn(across(near_keys), near_score)
            if far_rows:
                turned = turned + nn(kt_ref[:, :far_rows], far_score)
            rows = (jnp.transpose(turned) * SCALING).astype(bf16)
            out_ref[spots[0][0], 0, spots[0][1]] = rows[:BLK]
            out_ref[spots[1][0], 0, spots[1][1]] = rows[BLK:]
            return nn(near_score, queries), nn(near.astype(bf16), grads)

        def store(spot, key_grad, value_grad):
            out_ref[spot[0], 1, spot[1]] = (key_grad * SCALING).astype(bf16)
            out_ref[spot[0], 2, spot[1]] = value_grad.astype(bf16)

        under = apart_mask(BLK)
        for branch in range(BRANCHES):
            first = TRUNK + BRANCHES + LEAVES * branch
            spots = (at(first), at(first + 1))
            key_grad, value_grad = attend(
                spots, TRUNK_ROWS, (at(TRUNK + branch),) + spots, under, branch == 0
            )
            dkb_ref[branch] = key_grad[:BLK]
            dvb_ref[branch] = value_grad[:BLK]
            store(spots[0], key_grad[BLK : 2 * BLK], value_grad[BLK : 2 * BLK])
            store(spots[1], key_grad[2 * BLK :], value_grad[2 * BLK :])
        apart = apart_mask(0)
        for pair in range(BRANCHES // 2):
            spots = (at(TRUNK + 2 * pair), at(TRUNK + 2 * pair + 1))
            key_grad, value_grad = attend(spots, TRUNK_ROWS, spots, apart, False)
            for half in range(2):
                rows = slice(half * BLK, (half + 1) * BLK)
                branch = 2 * pair + half
                store(
                    spots[half], key_grad[rows] + dkb_ref[branch], value_grad[rows] + dvb_ref[branch]
                )
        causal = causal_mask()
        for pair in reversed(range(TRUNK // 2)):
            spots = (at(2 * pair), at(2 * pair + 1))
            key_grad, value_grad = attend(spots, pair * PAIR, spots, causal, False)
            for half in range(2):
                rows = slice(half * BLK, (half + 1) * BLK)
                held = slice(pair * PAIR + half * BLK, pair * PAIR + (half + 1) * BLK)
                store(
                    spots[half],
                    key_grad[rows] + dk_ref[held, :],
                    value_grad[rows] + dv_ref[held, :],
                )
        return carry

    lax.fori_loop(0, trees, one_tree, 0)


def attend_backward(order, packed, grads):
    groups = packed.shape[0]
    blocks = packed.shape[2]
    trees = groups * blocks // TREE_BLOCKS
    pairs = trees * TREE_BLOCKS * BLK * 1100
    return pl.pallas_call(
        functools.partial(backward_kernel, trees),
        in_specs=[
            pl.BlockSpec(memory_space=pltpu.SMEM),
            pl.BlockSpec(memory_space=pltpu.VMEM),
            pl.BlockSpec(memory_space=pltpu.VMEM),
        ],
        out_specs=pl.BlockSpec(memory_space=pltpu.VMEM),
        out_shape=jax.ShapeDtypeStruct(packed.shape, bf16),
        scratch_shapes=[
            pltpu.VMEM((TRUNK_ROWS, HEAD), bf16),
            pltpu.VMEM((HEAD, TRUNK_ROWS), bf16),
            pltpu.VMEM((TRUNK_ROWS, HEAD), bf16),
            pltpu.VMEM((TRUNK_ROWS, HEAD), f32),
            pltpu.VMEM((TRUNK_ROWS, HEAD), f32),
            pltpu.VMEM((BRANCHES, BLK, HEAD), f32),
            pltpu.VMEM((BRANCHES, BLK, HEAD), f32),
        ],
        compiler_params=pltpu.CompilerParams(vmem_limit_bytes=VMEM_LIMIT),
        cost_estimate=pl.CostEstimate(
            flops=pairs * HEAD * 10, bytes_accessed=packed.size * 5, transcendentals=pairs
        ),
        name="attend_backward",
    )(order, packed, grads)


def mean_square(values):
    return jnp.mean(values * values, axis=-1, keepdims=True)


def norm_back(gradient, normed, inverse, gain_vec):
    weighted = gradient * gain_vec
    return inverse * (weighted - normed * jnp.mean(normed * weighted, axis=-1, keepdims=True))


def chunk_call(kernel, ins, outs, kept, grid, scratch, cost, name):
    count = len(ins)
    specs = [spec for spec, _ in ins]
    values = [value for _, value in ins]
    aliases = {}
    if kept is not None:
        whole = [at for at, out in enumerate(outs) if out[2]]
        for at, value in zip(whole, kept):
            aliases[len(values)] = at
            specs.append(pl.BlockSpec(memory_space=pl.ANY))
            values.append(value)
    extra = len(values) - count

    def body(*refs):
        kernel(*refs[:count], *refs[count + extra :])

    return pl.pallas_call(
        body,
        grid=grid,
        in_specs=specs,
        out_specs=[out[0] for out in outs],
        out_shape=[out[1] for out in outs],
        scratch_shapes=scratch,
        input_output_aliases=aliases,
        compiler_params=pltpu.CompilerParams(vmem_limit_bytes=VMEM_LIMIT),
        cost_estimate=cost,
        name=name,
    )(*values)


def forward_chunk_kernel(
    place,
    core_ref,
    gain_ref,
    y_hbm,
    x_hbm,
    woa_hbm,
    wob_hbm,
    wg_hbm,
    wr_hbm,
    proj_hbm,
    low_hbm,
    act_hbm,
    silu_hbm,
    slope_hbm,
    part_hbm,
    y_ref,
    x_ref,
    row_ref,
    gate_ref,
    up_ref,
    exact_ref,
    proj_ref,
    low_ref,
    act_ref,
    silu_ref,
    slope_ref,
    part_ref,
    y_sem,
    x_sem,
    row_sems,
    gate_sems,
    up_sems,
    out_sems,
    part_sems,
):
    at, batch, part = place
    rows = y_ref.shape[0]
    units = act_ref.shape[1]
    tiles = D // TILE
    half = tiles // 2
    unit_tiles = units // TILE
    here = pl.ds(at * rows, rows)

    def tile(index):
        return pl.ds(pl.multiple_of(index * TILE, TILE), TILE)

    def out_tile(source, index):
        slot = index if source is woa_hbm else index + half
        return pltpu.make_async_copy(
            source.at[tile(index), :], row_ref.at[slot], row_sems.at[slot]
        )

    def unit_copies(index):
        slot = lax.rem(index, 2)
        return (
            pltpu.make_async_copy(wg_hbm.at[0, :, tile(index)], gate_ref.at[slot], gate_sems.at[slot]),
            pltpu.make_async_copy(wr_hbm.at[0, :, tile(index)], up_ref.at[slot], up_sems.at[slot]),
        )

    def down_copy(index):
        return pltpu.make_async_copy(
            wr_hbm.at[1, tile(index), :], row_ref.at[index, :, pl.ds(0, units)], row_sems.at[index]
        )

    def row_wait(index, width):
        pltpu.make_async_copy(
            woa_hbm.at[pl.ds(0, TILE), pl.ds(0, width)],
            row_ref.at[index, :, pl.ds(0, width)],
            row_sems.at[index],
        ).wait()

    y_copy = pltpu.make_async_copy(y_hbm.at[pl.ds(part * rows, rows), :], y_ref, y_sem)
    x_copy = pltpu.make_async_copy(x_hbm.at[batch, pl.ds(part * rows, rows), :], x_ref, x_sem)
    y_copy.start()
    for index in range(half):
        out_tile(woa_hbm, index).start()
    x_copy.start()
    y_copy.wait()

    def project_tile(index, carry):
        row_wait(index, D)

        @pl.when(index < half)
        def _():
            out_tile(wob_hbm, index).start()

        @pl.when(index >= half)
        def _():
            for copy in unit_copies(index - half):
                copy.start()

        side = jnp.where(index < half, core_ref[0], 1 - core_ref[0])
        columns = tile(side * half + lax.rem(index, half))
        exact_ref[:, columns] = nt(y_ref[...], row_ref[index])
        return carry

    lax.fori_loop(0, tiles, project_tile, 0)
    x_copy.wait()
    proj = exact_ref[...]
    inverse = lax.rsqrt(mean_square(proj) + EPSILON)
    proj_ref[...] = proj.astype(bf16)
    low_ref[...] = (x_ref[...].astype(f32) + proj * inverse * gain_ref[...]).astype(bf16)
    outs = [
        pltpu.make_async_copy(proj_ref, proj_hbm.at[here, :], out_sems.at[0]),
        pltpu.make_async_copy(low_ref, low_hbm.at[here, :], out_sems.at[1]),
        pltpu.make_async_copy(act_ref, act_hbm.at[here, :], out_sems.at[2]),
        pltpu.make_async_copy(silu_ref, silu_hbm.at[here, :], out_sems.at[3]),
        pltpu.make_async_copy(slope_ref, slope_hbm.at[here, :], out_sems.at[4]),
    ]
    outs[0].start()
    outs[1].start()

    def unit_tile(index, carry):
        slot = lax.rem(index, 2)
        for copy in unit_copies(index):
            copy.wait()
        low = low_ref[...]
        gate = nn(low, gate_ref[slot])
        up = nn(low, up_ref[slot])

        @pl.when(index + 2 < unit_tiles)
        def _():
            for copy in unit_copies(index + 2):
                copy.start()

        @pl.when(index + 2 >= unit_tiles)
        def _():
            first = (index + 2 - unit_tiles) * half
            for more in range(half):
                down_copy(first + more).start()

        sigmoid = 1.0 / (1.0 + jnp.exp(-gate))
        silu = gate * sigmoid
        columns = tile(index)
        act_ref[:, columns] = (silu * up).astype(bf16)
        silu_ref[:, columns] = silu.astype(bf16)
        slope_ref[:, columns] = (up * sigmoid * (1.0 + gate * (1.0 - sigmoid))).astype(bf16)
        return carry

    lax.fori_loop(0, unit_tiles, unit_tile, 0)
    for copy in outs[2:]:
        copy.start()

    def part_copy(index):
        columns = tile(index)
        return pltpu.make_async_copy(
            part_ref.at[:, columns], part_hbm.at[:, columns], part_sems.at[index]
        )

    def down_tile(index, carry):
        row_wait(index, units)
        part_ref[:, tile(index)] = nt(act_ref[...], row_ref[index, :, :units]).astype(bf16)
        part_copy(index).start()
        return carry

    lax.fori_loop(0, tiles, down_tile, 0)
    for index in range(tiles):
        part_copy(index).wait()
    for copy in outs:
        copy.wait()


def forward_chunk(at, batch, part, rows, y_all, tokens, gain, w_out, w_mlp, kept):
    core, w_out_a, w_out_b = w_out
    w_gate, w_rest = w_mlp
    units = w_gate.shape[2]
    total = tokens.shape[0] * tokens.shape[1]
    tiles = D // TILE
    anywhere = pl.BlockSpec(memory_space=pl.ANY)
    wide = jax.ShapeDtypeStruct((total, units), bf16)
    narrow = jax.ShapeDtypeStruct((total, D), bf16)
    dma = pltpu.SemaphoreType.DMA
    return chunk_call(
        functools.partial(forward_chunk_kernel, (at, batch, part)),
        [
            (pl.BlockSpec(memory_space=pltpu.SMEM), core),
            (pl.BlockSpec(memory_space=pltpu.VMEM), gain),
            (anywhere, y_all),
            (anywhere, tokens),
            (anywhere, w_out_a),
            (anywhere, w_out_b),
            (anywhere, w_gate),
            (anywhere, w_rest),
        ],
        [
            (anywhere, narrow, True),
            (anywhere, narrow, True),
            (anywhere, wide, True),
            (anywhere, wide, True),
            (anywhere, wide, True),
            (anywhere, jax.ShapeDtypeStruct((rows, D), bf16), False),
        ],
        kept,
        (),
        [
            pltpu.VMEM((rows, D), bf16),
            pltpu.VMEM((rows, D), bf16),
            pltpu.VMEM((tiles, TILE, D), bf16),
            pltpu.VMEM((2, D, TILE), bf16),
            pltpu.VMEM((2, D, TILE), bf16),
            pltpu.VMEM((rows, D), f32),
            pltpu.VMEM((rows, D), bf16),
            pltpu.VMEM((rows, D), bf16),
            pltpu.VMEM((rows, units), bf16),
            pltpu.VMEM((rows, units), bf16),
            pltpu.VMEM((rows, units), bf16),
            pltpu.VMEM((rows, D), bf16),
            dma,
            dma,
            dma((tiles,)),
            dma((2,)),
            dma((2,)),
            dma((5,)),
            dma((tiles,)),
        ],
        pl.CostEstimate(
            flops=2 * rows * D * (D + 3 * units),
            bytes_accessed=2 * D * (D + 3 * units) + 16 * rows * D,
            transcendentals=rows * units,
        ),
        "forward_chunk",
    )


def middle_chunk_kernel(
    place,
    attn_gain_ref,
    gain_ref,
    sum_hbm,
    proj_hbm,
    x_hbm,
    grad_hbm,
    silu_hbm,
    slope_hbm,
    wg_hbm,
    wr_hbm,
    output_hbm,
    low_hbm,
    gate_hbm,
    up_hbm,
    gain_part_ref,
    part_hbm,
    sum_ref,
    proj_ref,
    x_ref,
    grad_ref,
    silu_ref,
    slope_ref,
    down_ref,
    wg_ref,
    wu_ref,
    output_ref,
    low_ref,
    gates_ref,
    ups_ref,
    part_ref,
    in_sems,
    down_sems,
    wg_sems,
    wu_sems,
    out_sems,
    part_sems,
):
    at, batch, part = place
    rows = sum_ref.shape[0]
    units = silu_ref.shape[1]
    tiles = D // TILE
    half = tiles // 2
    unit_tiles = units // TILE
    here = pl.ds(at * rows, rows)
    inside = pl.ds(part * rows, rows)

    def tile(index):
        return pl.ds(pl.multiple_of(index * TILE, TILE), TILE)

    def down_copy(index):
        slot = lax.rem(index, 2)
        return pltpu.make_async_copy(
            wr_hbm.at[1, :, tile(index)], down_ref.at[slot], down_sems.at[slot]
        )

    def row_copies(index):
        slot = lax.rem(index, half)
        return (
            pltpu.make_async_copy(wg_hbm.at[0, tile(index), :], wg_ref.at[slot], wg_sems.at[slot]),
            pltpu.make_async_copy(wr_hbm.at[0, tile(index), :], wu_ref.at[slot], wu_sems.at[slot]),
        )

    ins = [
        pltpu.make_async_copy(sum_hbm, sum_ref, in_sems.at[0]),
        pltpu.make_async_copy(grad_hbm.at[batch, inside, :], grad_ref, in_sems.at[1]),
        pltpu.make_async_copy(proj_hbm.at[here, :], proj_ref, in_sems.at[2]),
        pltpu.make_async_copy(x_hbm.at[batch, inside, :], x_ref, in_sems.at[3]),
        pltpu.make_async_copy(silu_hbm.at[here, :], silu_ref, in_sems.at[4]),
        pltpu.make_async_copy(slope_hbm.at[here, :], slope_ref, in_sems.at[5]),
    ]
    ins[0].start()
    ins[1].start()
    down_copy(0).start()
    ins[4].start()
    ins[5].start()
    down_copy(1).start()
    ins[2].start()
    ins[3].start()
    ins[0].wait()
    ins[1].wait()
    mlp = sum_ref[...].astype(f32)
    mlp_inverse = lax.rsqrt(mean_square(mlp) + EPSILON)
    normed = mlp * mlp_inverse
    grad = grad_ref[...]
    gain_part_ref[...] = jnp.sum(grad * normed, axis=0, keepdims=True)
    low_ref[...] = norm_back(grad, normed, mlp_inverse, gain_ref[...]).astype(bf16)
    outs = [
        pltpu.make_async_copy(output_ref, output_hbm.at[here, :], out_sems.at[0]),
        pltpu.make_async_copy(low_ref, low_hbm.at[here, :], out_sems.at[1]),
        pltpu.make_async_copy(gates_ref, gate_hbm.at[here, :], out_sems.at[2]),
        pltpu.make_async_copy(ups_ref, up_hbm.at[here, :], out_sems.at[3]),
    ]
    outs[1].start()
    ins[4].wait()
    ins[5].wait()

    def unit_tile(index, carry):
        down_copy(index).wait()
        act_grad = nn(low_ref[...], down_ref[lax.rem(index, 2)])

        @pl.when(index + 2 < unit_tiles)
        def _():
            down_copy(index + 2).start()

        @pl.when(index + 2 >= unit_tiles)
        def _():
            for copy in row_copies(index + 2 - unit_tiles):
                copy.start()

        columns = tile(index)
        ups_ref[:, columns] = (act_grad * silu_ref[:, columns].astype(f32)).astype(bf16)
        gates_ref[:, columns] = (act_grad * slope_ref[:, columns].astype(f32)).astype(bf16)
        return carry

    lax.fori_loop(0, unit_tiles, unit_tile, 0)
    outs[2].start()
    outs[3].start()
    ins[2].wait()
    ins[3].wait()
    proj = proj_ref[...].astype(f32)
    inverse = lax.rsqrt(mean_square(proj) + EPSILON)
    hidden = x_ref[...].astype(f32) + proj * inverse * attn_gain_ref[...]
    mlp = sum_ref[...].astype(f32)
    output_ref[...] = (hidden + mlp * mlp_inverse * gain_ref[...]).astype(bf16)
    outs[0].start()

    def part_copy(index):
        columns = tile(index)
        return pltpu.make_async_copy(
            part_ref.at[:, columns], part_hbm.at[:, columns], part_sems.at[index]
        )

    def row_tile(index, carry):
        slot = lax.rem(index, half)
        for copy in row_copies(index):
            copy.wait()
        part_ref[:, tile(index)] = (
            nt(gates_ref[...], wg_ref[slot]) + nt(ups_ref[...], wu_ref[slot])
        ).astype(bf16)
        part_copy(index).start()

        @pl.when(index + half < tiles)
        def _():
            for copy in row_copies(index + half):
                copy.start()

        return carry

    lax.fori_loop(0, tiles, row_tile, 0)
    for index in range(tiles):
        part_copy(index).wait()
    for copy in outs:
        copy.wait()


def middle_chunk(
    at, batch, part, rows, mlp_sum, proj, tokens, grad, attn_gain, gain, silu, slope, w_mlp, kept
):
    w_gate, w_rest = w_mlp
    units = w_gate.shape[2]
    total = proj.shape[0]
    tiles = D // TILE
    half = tiles // 2
    vmem = pl.BlockSpec(memory_space=pltpu.VMEM)
    anywhere = pl.BlockSpec(memory_space=pl.ANY)
    wide = jax.ShapeDtypeStruct((total, units), bf16)
    narrow = jax.ShapeDtypeStruct((total, D), bf16)
    dma = pltpu.SemaphoreType.DMA
    return chunk_call(
        functools.partial(middle_chunk_kernel, (at, batch, part)),
        [
            (vmem, attn_gain),
            (vmem, gain),
            (anywhere, mlp_sum),
            (anywhere, proj),
            (anywhere, tokens),
            (anywhere, grad),
            (anywhere, silu),
            (anywhere, slope),
            (anywhere, w_gate),
            (anywhere, w_rest),
        ],
        [
            (anywhere, narrow, True),
            (anywhere, narrow, True),
            (anywhere, wide, True),
            (anywhere, wide, True),
            (vmem, jax.ShapeDtypeStruct((1, D), f32), False),
            (anywhere, jax.ShapeDtypeStruct((rows, D), bf16), False),
        ],
        kept,
        (),
        [
            pltpu.VMEM((rows, D), bf16),
            pltpu.VMEM((rows, D), bf16),
            pltpu.VMEM((rows, D), bf16),
            pltpu.VMEM((rows, D), f32),
            pltpu.VMEM((rows, units), bf16),
            pltpu.VMEM((rows, units), bf16),
            pltpu.VMEM((2, D, TILE), bf16),
            pltpu.VMEM((half, TILE, units), bf16),
            pltpu.VMEM((half, TILE, units), bf16),
            pltpu.VMEM((rows, D), bf16),
            pltpu.VMEM((rows, D), bf16),
            pltpu.VMEM((rows, units), bf16),
            pltpu.VMEM((rows, units), bf16),
            pltpu.VMEM((rows, D), bf16),
            dma((6,)),
            dma((2,)),
            dma((half,)),
            dma((half,)),
            dma((4,)),
            dma((tiles,)),
        ],
        pl.CostEstimate(
            flops=2 * rows * D * 3 * units,
            bytes_accessed=2 * D * 3 * units + 24 * rows * D,
            transcendentals=rows,
        ),
        "middle_chunk",
    )


def backward_chunk_kernel(
    heads, sum_ref, grad_ref, proj_ref, gain_ref, wo_ref, hidden_ref, low_ref, dy_ref, gain_part_ref
):
    hidden_grad = grad_ref[...] + sum_ref[...].astype(f32)
    proj = proj_ref[...].astype(f32)
    inverse = lax.rsqrt(mean_square(proj) + EPSILON)
    normed = proj * inverse
    hidden_ref[...] = hidden_grad
    gain_part_ref[...] = jnp.sum(hidden_grad * normed, axis=0, keepdims=True)
    low = norm_back(hidden_grad, normed, inverse, gain_ref[...]).astype(bf16)
    low_ref[...] = low
    grad = nn(low, wo_ref[...])
    for head in range(heads):
        dy_ref[head] = grad[:, head_cols(head)].astype(bf16)


def backward_chunk(at, batch, part, rows, branch_sum, grad, proj, gain, w_attn, kept):
    total = proj.shape[0]
    width = w_attn.shape[2]
    heads = width // HEAD
    whole = pl.BlockSpec((rows, D), lambda s: (at, 0))
    line = pl.BlockSpec((1, D), lambda s: (0, 0))
    return chunk_call(
        functools.partial(backward_chunk_kernel, heads),
        [
            (pl.BlockSpec((rows, D), lambda s: (0, 0)), branch_sum),
            (pl.BlockSpec((None, rows, D), lambda s: (batch, part, 0)), grad),
            (whole, proj),
            (line, gain),
            (pl.BlockSpec((None, D, width), lambda s: (3, 0, 0)), w_attn),
        ],
        [
            (whole, jax.ShapeDtypeStruct((total, D), f32), True),
            (whole, jax.ShapeDtypeStruct((total, D), bf16), True),
            (
                pl.BlockSpec((heads, rows, HEAD), lambda s: (0, at, 0)),
                jax.ShapeDtypeStruct((heads, total, HEAD), bf16),
                True,
            ),
            (line, jax.ShapeDtypeStruct((1, D), f32), False),
        ],
        kept,
        (1,),
        [],
        pl.CostEstimate(
            flops=2 * rows * D * width, bytes_accessed=16 * rows * D, transcendentals=rows
        ),
        "backward_chunk",
    )


def weight_sum_kernel(count, left_ref, right_ref, out_ref):
    units = out_ref.shape[2]
    for at in range(count):
        out_ref[at] = lax.dot_general(
            left_ref[...],
            right_ref[:, at * units : (at + 1) * units],
            (((0,), (0,)), ((), ())),
            preferred_element_type=f32,
        ).astype(bf16)


def weight_sum(first, slots, count, left, right, kept):
    rows, depth = left.shape
    units = right.shape[1] // slots
    return chunk_call(
        functools.partial(weight_sum_kernel, slots),
        [
            (pl.BlockSpec((rows, TILE), lambda s: (0, s)), left),
            (pl.BlockSpec((rows, slots * units), lambda s: (0, 0)), right),
        ],
        [
            (
                pl.BlockSpec((slots, TILE, units), lambda s: (first // slots, s, 0)),
                jax.ShapeDtypeStruct((count, depth, units), bf16),
                True,
            )
        ],
        kept,
        (depth // TILE,),
        [],
        pl.CostEstimate(
            flops=2 * rows * depth * units * slots,
            bytes_accessed=2 * slots * (rows * depth + rows * units + depth * units),
            transcendentals=0,
        ),
        "weight_sum",
    )


def shards(
    layer_input,
    cotangent,
    w_query,
    w_key,
    w_value,
    w_output,
    w_gate,
    w_up,
    w_down,
    query_gain,
    key_gain,
    attn_gain,
    mlp_gain,
    slot_parent,
    slot_depth,
):
    dp_index = lax.axis_index("dp")
    tp_index = lax.axis_index("tensor")
    dp_count = lax.axis_size("dp")
    tp_count = lax.axis_size("tensor")
    rows = layer_input.shape[1]
    share = rows // tp_count
    width = w_query.shape[1]
    heads = width // HEAD
    hidden_width = w_gate.shape[1]
    items = heads * MB
    copies = dp_count // items

    def gather_stack(*pieces):
        return lax.all_gather(jnp.stack(pieces), "dp", axis=1, tiled=True)

    def scatter_rows(total, dimension=0):
        return lax.psum_scatter(
            total.astype(bf16), "dp", scatter_dimension=dimension, tiled=True
        )

    def exchange(pieces):
        flat = pieces.reshape((items, -1, HEAD))
        if copies > 1:
            flat = jnp.tile(flat, (copies, 1, 1))
        return lax.all_to_all(flat, "dp", split_axis=0, concat_axis=0, tiled=True)

    def give_back(pieces):
        flat = pieces.reshape((dp_count, -1, HEAD))
        return lax.all_to_all(flat, "dp", split_axis=0, concat_axis=0, tiled=True)[:items]

    w_attn = gather_stack(w_query, w_key, w_value, jnp.transpose(w_output))
    w_gate_all = gather_stack(w_gate)

    order = tree_order(slot_parent, slot_depth)
    my_batch = lax.rem(lax.rem(dp_index, items), MB)
    my_order = lax.dynamic_index_in_dim(order, my_batch, 0, keepdims=False)
    my_depth = lax.dynamic_slice_in_dim(slot_depth, dp_index * SEG_DEV, SEG_DEV, 1)
    cosines, sines = rope_tables(my_depth)

    q_raw, k_raw, squares = project(layer_input, w_attn, (0, 1), True)
    squares = jnp.transpose(squares.reshape(MB * rows, 2))
    (v_raw,) = project(layer_input, w_attn, (2,), False)
    squares = small_sum(squares, "tensor", tp_count)
    inverse = jnp.transpose(lax.rsqrt(squares / D + EPSILON)).reshape(MB, rows, 2)
    gains = jnp.concatenate([query_gain, key_gain])[None, :]
    packed = pack_heads(q_raw, k_raw, v_raw, inverse, gains, cosines, sines, heads)
    w_out_begun = begin_output_weight(w_attn[3], packed, dp_index, dp_count, tp_count)
    packed = follow(exchange(packed), w_out_begun[1:]).reshape(dp_count, 3, SEG_DEV, BLK, HEAD)
    w_out = end_output_weight(w_out_begun, packed, dp_index, dp_count, tp_count)
    w_mlp = (w_gate_all, gather_stack(*follow((w_up, jnp.transpose(w_down)), packed)))

    attended = give_back(attend_forward(my_order, packed))
    attended = attended.reshape(heads, MB, rows, HEAD).transpose(1, 2, 0, 3)
    attended = attended.reshape(MB, rows, width)

    parts = 2
    step = rows // parts
    spots = [(batch, part) for batch in range(MB) for part in range(parts)]
    begun = go_on_all_gather(begin_all_gather(attended[0], tp_count), tp_count)
    gathered, hop = end_all_gather(begun, tp_count)
    everything = [gathered]
    begun = [begun]
    for batch in range(1, MB):
        begun.append(begin_all_gather(follow(attended[batch], hop), tp_count))
    sums = SumLine(tp_count)
    attn_gain_row = attn_gain[None, :]
    mlp_gain_row = mlp_gain[None, :]
    chunks = len(spots)
    state = dict(forward=None, middle=None, backward=None)
    mlp_gain_parts = []
    attn_gain_parts = []

    def forward(at, after):
        batch, part = spots[at]
        if batch == len(everything):
            early = sums.terms[0] if sums.terms else None
            going = go_on_all_gather(begun[batch], tp_count)
            everything.append(end_all_gather(going, tp_count, early)[0])
        *state["forward"], term = forward_chunk(
            at,
            batch,
            part,
            step,
            follow(everything[batch], after),
            layer_input,
            attn_gain_row,
            w_out,
            w_mlp,
            state["forward"],
        )
        return term

    def middle(at, after):
        batch, part = spots[at]
        proj, _, _, silu, slope = state["forward"]
        *kept, gain_part, term = middle_chunk(
            at,
            batch,
            part,
            step,
            follow(sums.sums[at], after),
            proj,
            layer_input,
            cotangent,
            attn_gain_row,
            mlp_gain_row,
            silu,
            slope,
            w_mlp,
            state["middle"],
        )
        state["middle"] = kept
        mlp_gain_parts.append(gain_part)
        return term

    def backward(at, after):
        batch, part = spots[at]
        *kept, gain_part = backward_chunk(
            at,
            batch,
            part,
            step,
            follow(sums.sums[chunks + at], after),
            cotangent,
            state["forward"][0],
            attn_gain_row,
            w_attn,
            state["backward"],
        )
        state["backward"] = kept
        attn_gain_parts.append(gain_part)
        return gain_part

    sums.enter(forward(0, None))
    sums.enter(forward(1, None))
    last = None
    mlp_total = None
    for at in range(2 * chunks + 2):
        after = sums.terms[-1] if last is None and tp_count == 4 else last
        moved = tuple(sums.advance(after)) or None
        coming = at + 2
        if coming < chunks:
            last = forward(coming, moved)
            sums.enter(last)
        elif coming < 2 * chunks:
            last = middle(coming - chunks, moved)
            sums.enter(last)
        else:
            last = backward(coming - 2 * chunks, moved)
            turn_at = coming - 2 * chunks
            output, mlp_grad, gate_grad, up_grad = state["middle"]
            hidden_low, act = state["forward"][1:3]
            left, right = (
                (hidden_low, gate_grad),
                (hidden_low, up_grad),
                (mlp_grad, act),
                (None, None),
            )[turn_at]
            if left is not None:
                mlp_total = weight_sum(turn_at, 1, 3, follow(left, last), right, mlp_total)
                last = mlp_total[0]
        if coming == 3 * chunks - 1:
            break
    hidden_grad, proj_grad, attn_grad = state["backward"]
    mlp_weight_grad = scatter_rows(follow(mlp_total[0], attn_grad), 1)
    attended = attended.reshape(MB * rows, width)
    attn_total = weight_sum(3, 1, 4, proj_grad, follow(attended, attn_grad), None)

    attn_grad = follow(exchange(attn_grad), attn_total)
    attn_grad = attn_grad.reshape(dp_count, SEG_DEV, BLK, HEAD)
    back = give_back(attend_backward(my_order, packed, attn_grad))
    back = back.reshape(heads, MB, 3, rows, HEAD)
    inner, gain_part = inner_sums(back, q_raw, k_raw, inverse, gains, cosines, sines, heads)
    means = small_sum(jnp.transpose(inner.reshape(-1, 2)), "tensor", tp_count) / D
    means = jnp.transpose(means).reshape(MB, rows, 2)
    qkv_grad = None
    terms = []
    for batch in range(MB):
        *qkv_grad, term = unpack_heads(
            batch, back, q_raw, k_raw, inverse, means, gains, cosines, sines, w_attn, heads, qkv_grad
        )
        terms.append(term)
    mlp_weight_grads = [
        mlp_weight_grad[0].astype(f32),
        mlp_weight_grad[1].astype(f32),
        jnp.transpose(mlp_weight_grad[2].astype(f32)),
    ]
    parts, first_operands, second_operands = line_reduce_scatter(terms, tp_count, mlp_weight_grads)
    tokens = layer_input.reshape(MB * rows, D)
    qkv_grad = qkv_grad[0]
    attn_total = weight_sum(0, 3, 4, tokens, qkv_grad, attn_total)
    attn_total = follow(attn_total[0], (mlp_weight_grad, first_operands))
    attn_weight_grad = scatter_rows(attn_total, 1)
    attn_weight_grads = [attn_weight_grad[at].astype(f32) for at in range(4)]
    attn_weight_grads[3] = jnp.transpose(attn_weight_grads[3])
    parts[-1] = (follow(parts[-1][0], attn_weight_grads),) + parts[-1][1:]
    input_parts = [
        lax.dynamic_slice_in_dim(hidden_grad, batch * rows + tp_index * share, share, 0)
        + sum(piece.astype(f32) for piece in part)
        for batch, part in enumerate(parts)
    ]

    gain_sums = jnp.concatenate(
        [
            gain_part[0],
            sum(attn_gain_parts)[0],
            sum(mlp_gain_parts)[0],
        ]
    )
    gain_sums = follow(gain_sums.reshape(-1, HEAD), second_operands)
    gain_sums = small_sum(gain_sums, "dp", dp_count).reshape(-1)
    return (
        output.reshape(MB, rows, D),
        jnp.stack(input_parts),
        *attn_weight_grads,
        *mlp_weight_grads,
        gain_sums[:width],
        gain_sums[width : 2 * width],
        gain_sums[2 * width : 2 * width + D],
        gain_sums[2 * width + D :],
    )


def solution(mesh):
    in_specs = (
        P(None, "dp", None),
        P(None, "dp", None),
        P("dp", "tensor"),
        P("dp", "tensor"),
        P("dp", "tensor"),
        P("tensor", "dp"),
        P("dp", "tensor"),
        P("dp", "tensor"),
        P("tensor", "dp"),
        P("tensor"),
        P("tensor"),
        P(),
        P(),
        P(),
        P(),
    )
    out_specs = (
        P(None, "dp", None),
        P(None, ("dp", "tensor"), None),
        P("dp", "tensor"),
        P("dp", "tensor"),
        P("dp", "tensor"),
        P("tensor", "dp"),
        P("dp", "tensor"),
        P("dp", "tensor"),
        P("tensor", "dp"),
        P("tensor"),
        P("tensor"),
        P(),
        P(),
    )
    return jax.shard_map(shards, mesh=mesh, in_specs=in_specs, out_specs=out_specs, check_vma=False)
```

```python
import functools

import jax
import jax.numpy as jnp
from jax import lax
from jax.experimental import pallas as pl
from jax.experimental.pallas import tpu as pltpu
from jax.sharding import PartitionSpec as P

D = 2048
HEADS = 16
HEAD = D // HEADS
BLK = 128
TRUNK = 8
BRANCHES = 4
LEAVES = 2
TREE_BLOCKS = 20
MB = 2
SEG_DEV = 5
PAIR = 2 * BLK
TRUNK_ROWS = TRUNK * BLK
TILE = 512

EPSILON = 1e-06
ROPE_BASE = 500000.0
SCALING = HEAD ** (-0.5)
VMEM_LIMIT = 50 * 1024 * 1024

f32 = jnp.float32
bf16 = jnp.bfloat16


def tree_order(parents, depths):
    blocks = parents.shape[1]
    ids = jnp.arange(blocks, dtype=jnp.int32)

    def follow(table, index):
        hot = index[:, :, None] == ids[None, None, :]
        return jnp.sum(jnp.where(hot, table[:, None, :], 0), axis=-1)

    up2 = follow(parents, parents)
    up4 = follow(up2, up2)
    up8 = follow(up4, up4)
    root = follow(up8, up8)
    is_leaf = depths == TRUNK + 1
    above = jnp.where(is_leaf, parents, 0)
    key = ((root * (TRUNK + 2) + depths) * blocks + above) * blocks + ids[None, :]
    rank = jnp.sum((key[:, None, :] < key[:, :, None]).astype(jnp.int32), axis=-1)
    return jnp.sum(
        jnp.where(rank[:, None, :] == ids[None, :, None], ids[None, None, :], 0), axis=-1
    ).astype(jnp.int32)


def rope_tables(depths):
    half = HEAD // 2
    offsets = jnp.arange(BLK, dtype=jnp.int32)
    places = (depths[:, :, None] * BLK + offsets).reshape(depths.shape[0], -1).astype(f32)
    frequency = ROPE_BASE ** (-2.0 * jnp.arange(half, dtype=f32) / HEAD)
    angles = places[:, :, None] * frequency
    cosines = jnp.cos(angles)
    sines = jnp.sin(angles)
    return (
        jnp.concatenate([cosines, cosines], -1),
        jnp.concatenate([-sines, sines], -1),
    )


def low_sum(*parts):
    total = parts[0].astype(f32)
    for part in parts[1:]:
        total = total + part.astype(f32)
    return total.astype(bf16)


def follow(values, after):
    if after is None:
        return values
    return lax.optimization_barrier((values, after))[0]


def small_sum(values, axis, count):
    step = 1
    while step < count:
        values = values + lax.ppermute(values, axis, [(i, i ^ step) for i in range(count)])
        step *= 2
    return values


class SumLine:
    def __init__(self, count):
        self.count = count
        index = lax.axis_index("tensor")
        self.inner = (index == 1) | (index == 2)
        self.terms = []
        self.inward = []
        self.sides = []
        self.across = []
        self.totals = []
        self.outward = []
        self.sums = []

    def enter(self, term):
        if self.count != 4:
            self.sums.append(lax.psum(term, "tensor"))
            return
        self.terms.append(term)
        self.inward.append(lax.ppermute(term, "tensor", [(0, 1), (3, 2)]))

    def advance(self, after):
        if self.count != 4:
            return []
        moved = []
        if len(self.sides) < len(self.terms):
            at = len(self.sides)
            side = low_sum(follow(self.terms[at], after), self.inward[at])
            self.sides.append(side)
            moved.append(side)
        at = len(self.totals)
        if at < len(self.sides) - 1 or (at < len(self.sides) and not moved):
            total = low_sum(follow(self.sides[at], after), self.across[at])
            self.totals.append(total)
            moved.append(total)
        at = len(self.sums)
        if at < len(self.outward):
            self.sums.append(
                jnp.where(self.inner, follow(self.totals[at], after), self.outward[at])
            )
        if len(self.across) < len(self.sides):
            self.across.append(lax.ppermute(self.sides[-1], "tensor", [(1, 2), (2, 1)]))
        if len(self.outward) < len(self.totals):
            self.outward.append(lax.ppermute(self.totals[-1], "tensor", [(1, 0), (2, 3)]))
        return moved


def line_reduce_scatter(batches, count, late):
    if count != 4:
        return [
            (lax.psum_scatter(values, "tensor", scatter_dimension=0, tiled=True),)
            for values in batches
        ], None, None
    index = lax.axis_index("tensor")
    rights = []
    lefts = []
    blocks = [item.reshape(count, item.shape[0] // count, item.shape[1]) for item in batches]

    def block(item, at):
        return lax.dynamic_index_in_dim(item, lax.rem(at + 2 * count, count), 0, keepdims=False)

    operands = []
    for stage in range(count - 1):
        to_right = [(i, i + 1) for i in range(stage + 1)]
        to_left = [(count - 1 - i, count - 2 - i) for i in range(stage + 1)]
        for at, item in enumerate(blocks):
            right = block(item, index + count - 1 - stage)
            left = block(item, index - count + 1 + stage)
            before = max(at - 1, 0)
            if stage:
                arrived = follow((rights[at], lefts[at]), (rights[before], lefts[before]))
                right = low_sum(right, arrived[0])
                left = low_sum(left, arrived[1])
            elif at:
                right, left = follow((right, left), (rights[before], lefts[before]))
            if stage:
                if stage == 1 and at == len(blocks) - 1:
                    right, left = follow((right, left), late)
                rights[at] = lax.ppermute(right, "tensor", to_right)
                lefts[at] = lax.ppermute(left, "tensor", to_left)
            else:
                rights.append(lax.ppermute(right, "tensor", to_right))
                lefts.append(lax.ppermute(left, "tensor", to_left))
            operands.append((right, left))
    sums = [
        (block(item, index), right, left) for item, right, left in zip(blocks, rights, lefts)
    ]
    return sums, operands[1], operands[len(blocks)]


def begin_all_gather(values, count):
    if count != 4:
        return values, None
    right = lax.ppermute(values, "tensor", [(0, 1), (1, 2), (2, 3)])
    left = lax.ppermute(values, "tensor", [(3, 2), (2, 1), (1, 0)])
    return values, (right, left)


def go_on_all_gather(begun, count):
    values, first = begun
    if count != 4:
        return values, None, None
    right = lax.ppermute(first[0], "tensor", [(1, 2), (2, 3)])
    left = lax.ppermute(first[1], "tensor", [(2, 1), (1, 0)])
    return values, first, (right, left)


def end_all_gather(begun, count, after=None):
    values, first, second = begun
    if count != 4:
        return lax.all_gather(values, "tensor", axis=1, tiled=True), None
    index = lax.axis_index("tensor")
    width = values.shape[1]
    right, left = follow(second, after)
    right = lax.ppermute(right, "tensor", [(2, 3)])
    left = lax.ppermute(left, "tensor", [(1, 0)])
    whole = jnp.zeros((values.shape[0], count * width), values.dtype)
    pieces = (
        values,
        jnp.where(index >= 1, first[0], left),
        jnp.where(index >= 2, second[0], second[1]),
        jnp.where(index >= 3, right, first[1]),
    )
    for back, piece in enumerate(pieces):
        place = lax.rem(index - back + count, count) * width
        whole = lax.dynamic_update_slice(whole, piece, (0, place))
    return whole, (right, left)


def begin_output_weight(own, after, dp_index, dp_count, count):
    if count != 4 or dp_count % 2:
        return own, None, None
    half = own.shape[0] // 2
    mine = lax.dynamic_slice_in_dim(follow(own, after), lax.rem(dp_index, 2) * half, half, 0)
    return go_on_all_gather(begin_all_gather(mine, count), count)


def end_output_weight(begun, after, dp_index, dp_count, count):
    if count != 4 or dp_count % 2:
        whole = lax.all_gather(begun[0], "tensor", axis=1, tiled=True)
        half = whole.shape[0] // 2
        return jnp.zeros((1,), jnp.int32), whole[:half], whole[half:]
    mine, _ = end_all_gather(begun, count, after)
    other = lax.ppermute(mine, "dp", [(i, i ^ 1) for i in range(dp_count)])
    return lax.rem(dp_index, 2).astype(jnp.int32).reshape(1), mine, other


def turn(values, cosines, sines):
    return values * cosines + pltpu.roll(values, HEAD // 2, 1) * sines


def head_cols(head, group=0, heads=0):
    start = (group * heads + head) * HEAD
    return slice(start, start + HEAD)


def project_kernel(x_ref, *refs):
    count = len(refs) // 2 if len(refs) > 2 else 1
    weights, outs = refs[:count], refs[count:]
    for at in range(count):
        raw = jnp.dot(x_ref[0], weights[at][0], preferred_element_type=f32)
        outs[at][0] = raw.astype(outs[at].dtype)
        if len(outs) > count:
            outs[count][0, :, at : at + 1] = jnp.sum(raw * raw, axis=1, keepdims=True)


def project(tokens, weights, which, squares):
    batches, rows, _ = tokens.shape
    width = weights.shape[2]
    step = rows // 2
    dtype = f32 if squares else bf16
    out_specs = [pl.BlockSpec((1, step, width), lambda b, r: (b, r, 0))] * len(which)
    out_shape = [jax.ShapeDtypeStruct((batches, rows, width), dtype)] * len(which)
    if squares:
        out_specs.append(pl.BlockSpec((1, step, len(which)), lambda b, r: (b, r, 0)))
        out_shape.append(jax.ShapeDtypeStruct((batches, rows, len(which)), f32))
    return pl.pallas_call(
        project_kernel,
        grid=(batches, rows // step),
        in_specs=[pl.BlockSpec((1, step, D), lambda b, r: (b, r, 0))]
        + [pl.BlockSpec((1, D, width), lambda b, r, at=at: (at, 0, 0)) for at in which],
        out_specs=out_specs,
        out_shape=out_shape,
        compiler_params=pltpu.CompilerParams(vmem_limit_bytes=VMEM_LIMIT),
        cost_estimate=pl.CostEstimate(
            flops=2 * batches * rows * D * width * len(which),
            bytes_accessed=2 * batches * rows * D + 2 * D * width * len(which),
            transcendentals=0,
        ),
        name="project",
    )(tokens, *([weights] * len(which)))


def pack_kernel(heads, q_ref, k_ref, v_ref, inv_ref, gain_ref, cos_ref, sin_ref, out_ref):
    cosines = cos_ref[0]
    sines = sin_ref[0]
    for head in range(heads):
        for which in range(2):
            cols = head_cols(head, which, heads)
            raw_ref = (q_ref, k_ref)[which]
            normed = raw_ref[0, :, head_cols(head)] * inv_ref[0, :, which : which + 1] * gain_ref[:, cols]
            out_ref[head, 0, which] = turn(normed, cosines, sines).astype(bf16)
        out_ref[head, 0, 2] = v_ref[0, :, head_cols(head)]


def pack_heads(q_raw, k_raw, v_raw, inverse, gains, cosines, sines, heads):
    rows = q_raw.shape[1]
    step = rows // 2
    width = heads * HEAD
    return pl.pallas_call(
        functools.partial(pack_kernel, heads),
        grid=(MB, rows // step),
        in_specs=[
            pl.BlockSpec((1, step, width), lambda b, r: (b, r, 0)),
            pl.BlockSpec((1, step, width), lambda b, r: (b, r, 0)),
            pl.BlockSpec((1, step, width), lambda b, r: (b, r, 0)),
            pl.BlockSpec((1, step, 2), lambda b, r: (b, r, 0)),
            pl.BlockSpec((1, 2 * width), lambda b, r: (0, 0)),
            pl.BlockSpec((1, step, HEAD), lambda b, r: (b, r, 0)),
            pl.BlockSpec((1, step, HEAD), lambda b, r: (b, r, 0)),
        ],
        out_specs=pl.BlockSpec((heads, 1, 3, step, HEAD), lambda b, r: (0, b, 0, r, 0)),
        out_shape=jax.ShapeDtypeStruct((heads, MB, 3, rows, HEAD), bf16),
        name="pack_heads",
    )(q_raw, k_raw, v_raw, inverse, gains, cosines, sines)


def inner_kernel(heads, back_ref, q_ref, k_ref, inv_ref, gain_ref, cos_ref, sin_ref, inner_ref, part_ref):
    cosines = cos_ref[0]
    sines = -sin_ref[0]

    @pl.when((pl.program_id(0) == 0) & (pl.program_id(1) == 0))
    def _():
        part_ref[...] = jnp.zeros_like(part_ref)

    for which in range(2):
        total = None
        for head in range(heads):
            cols = head_cols(head, which, heads)
            straight = turn(back_ref[head, 0, which].astype(f32), cosines, sines)
            hat = (q_ref, k_ref)[which][0, :, head_cols(head)] * inv_ref[0, :, which : which + 1]
            product = straight * hat
            part_ref[:, cols] += jnp.sum(product, axis=0, keepdims=True)
            weighted = product * gain_ref[:, cols]
            total = weighted if total is None else total + weighted
        inner_ref[0, :, which : which + 1] = jnp.sum(total, axis=1, keepdims=True)


def inner_sums(back, q_raw, k_raw, inverse, gains, cosines, sines, heads):
    rows = q_raw.shape[1]
    step = rows // 2
    width = heads * HEAD
    return pl.pallas_call(
        functools.partial(inner_kernel, heads),
        grid=(MB, rows // step),
        in_specs=[
            pl.BlockSpec((heads, 1, 2, step, HEAD), lambda b, r: (0, b, 0, r, 0)),
            pl.BlockSpec((1, step, width), lambda b, r: (b, r, 0)),
            pl.BlockSpec((1, step, width), lambda b, r: (b, r, 0)),
            pl.BlockSpec((1, step, 2), lambda b, r: (b, r, 0)),
            pl.BlockSpec((1, 2 * width), lambda b, r: (0, 0)),
            pl.BlockSpec((1, step, HEAD), lambda b, r: (b, r, 0)),
            pl.BlockSpec((1, step, HEAD), lambda b, r: (b, r, 0)),
        ],
        out_specs=[
            pl.BlockSpec((1, step, 2), lambda b, r: (b, r, 0)),
            pl.BlockSpec((1, 2 * width), lambda b, r: (0, 0)),
        ],
        out_shape=[
            jax.ShapeDtypeStruct((MB, rows, 2), f32),
            jax.ShapeDtypeStruct((1, 2 * width), f32),
        ],
        name="inner_sums",
    )(back, q_raw, k_raw, inverse, gains, cosines, sines)


def unpack_kernel(
    heads,
    back_ref,
    q_ref,
    k_ref,
    inv_ref,
    mean_ref,
    gain_ref,
    cos_ref,
    sin_ref,
    wq_ref,
    wk_ref,
    wv_ref,
    grad_ref,
    term_ref,
):
    cosines = cos_ref[0]
    sines = -sin_ref[0]
    width = heads * HEAD
    for head in range(heads):
        for which in range(2):
            cols = head_cols(head, which, heads)
            inverse = inv_ref[0, :, which : which + 1]
            straight = turn(back_ref[head, 0, which].astype(f32), cosines, sines)
            hat = (q_ref, k_ref)[which][0, :, head_cols(head)] * inverse
            grad = inverse * (straight * gain_ref[:, cols] - hat * mean_ref[0, :, which : which + 1])
            grad_ref[:, cols] = grad.astype(bf16)
        grad_ref[:, head_cols(head, 2, heads)] = back_ref[head, 0, 2]
    term = nt(grad_ref[:, :width], wq_ref[0])
    term = term + nt(grad_ref[:, width : 2 * width], wk_ref[0])
    term = term + nt(grad_ref[:, 2 * width :], wv_ref[0])
    term_ref[...] = term.astype(bf16)


def unpack_heads(
    batch, back, q_raw, k_raw, inverse, means, gains, cosines, sines, weights, heads, kept
):
    rows = q_raw.shape[1]
    step = rows // 2
    width = heads * HEAD
    row_spec = lambda cols: pl.BlockSpec((1, step, cols), lambda r: (batch, r, 0))
    return chunk_call(
        functools.partial(unpack_kernel, heads),
        [
            (pl.BlockSpec((heads, 1, 3, step, HEAD), lambda r: (0, batch, 0, r, 0)), back),
            (row_spec(width), q_raw),
            (row_spec(width), k_raw),
            (row_spec(2), inverse),
            (row_spec(2), means),
            (pl.BlockSpec((1, 2 * width), lambda r: (0, 0)), gains),
            (row_spec(HEAD), cosines),
            (row_spec(HEAD), sines),
        ]
        + [(pl.BlockSpec((1, D, width), lambda r, at=at: (at, 0, 0)), weights) for at in range(3)],
        [
            (
                pl.BlockSpec((step, 3 * width), lambda r: (batch * 2 + r, 0)),
                jax.ShapeDtypeStruct((MB * rows, 3 * width), bf16),
                True,
            ),
            (
                pl.BlockSpec((step, D), lambda r: (r, 0)),
                jax.ShapeDtypeStruct((rows, D), bf16),
                False,
            ),
        ],
        kept,
        (2,),
        [],
        pl.CostEstimate(flops=6 * rows * D * width, bytes_accessed=8 * rows * D, transcendentals=0),
        "unpack_heads",
    )


def nt(left, right):
    return lax.dot_general(left, right, (((1,), (1,)), ((), ())), preferred_element_type=f32)


def nn(left, right):
    return lax.dot_general(left, right, (((1,), (0,)), ((), ())), preferred_element_type=f32)


def key_query_iotas(keys):
    key_at = lax.broadcasted_iota(jnp.int32, (keys, PAIR), 0)
    query_at = lax.broadcasted_iota(jnp.int32, (keys, PAIR), 1)
    return key_at, query_at


def causal_mask():
    key_at, query_at = key_query_iotas(PAIR)
    return key_at <= query_at


def apart_mask(above):
    key_at, query_at = key_query_iotas(above + PAIR)
    key_at = key_at - above
    own = (key_at <= query_at) & ((key_at < BLK) == (query_at < BLK))
    return own | (key_at < 0)


def softmax_parts(queries, trunk_keys, near_keys, mask):
    near = jnp.where(mask, nt(near_keys, queries), -1e30)
    top = jnp.max(near, axis=0, keepdims=True)
    if trunk_keys is None:
        near = jnp.exp((near - top) * SCALING)
        scale = 1.0 / jnp.sum(near, axis=0, keepdims=True)
        return None, near * scale
    far = nt(trunk_keys, queries)
    top = jnp.maximum(top, jnp.max(far, axis=0, keepdims=True))
    near = jnp.exp((near - top) * SCALING)
    far = jnp.exp((far - top) * SCALING)
    scale = 1.0 / (jnp.sum(near, axis=0, keepdims=True) + jnp.sum(far, axis=0, keepdims=True))
    return far * scale, near * scale


def places(order_ref, tree):
    def at(within):
        slot = order_ref[tree * TREE_BLOCKS + within]
        return lax.div(slot, SEG_DEV), lax.rem(slot, SEG_DEV)

    return at


def load(ref, which, *spots):
    parts = [ref[group, which, row] for group, row in spots]
    return parts[0] if len(parts) == 1 else jnp.concatenate(parts, axis=0)


def across(values):
    return jnp.transpose(values.astype(f32)).astype(bf16)


def forward_kernel(trees, order_ref, x_ref, y_ref, k_ref, vt_ref):
    def one_tree(tree, carry):
        at = places(order_ref, tree)
        for within in range(TRUNK):
            rows = slice(within * BLK, (within + 1) * BLK)
            spot = at(within)
            k_ref[rows, :] = load(x_ref, 1, spot)
            vt_ref[:, rows] = across(load(x_ref, 2, spot))

        def attend(spots, far_rows, near_keys, near_values, mask):
            queries = load(x_ref, 0, *spots)
            far, near = softmax_parts(
                queries, k_ref[:far_rows, :] if far_rows else None, near_keys, mask
            )
            summed = nn(across(near_values), near.astype(bf16))
            if far_rows:
                summed = summed + nn(vt_ref[:, :far_rows], far.astype(bf16))
            rows = jnp.transpose(summed).astype(bf16)
            y_ref[spots[0][0], spots[0][1]] = rows[:BLK]
            y_ref[spots[1][0], spots[1][1]] = rows[BLK:]

        causal = causal_mask()
        for pair in range(TRUNK // 2):
            spots = (at(2 * pair), at(2 * pair + 1))
            attend(spots, pair * PAIR, load(x_ref, 1, *spots), load(x_ref, 2, *spots), causal)
        apart = apart_mask(0)
        for pair in range(BRANCHES // 2):
            spots = (at(TRUNK + 2 * pair), at(TRUNK + 2 * pair + 1))
            attend(spots, TRUNK_ROWS, load(x_ref, 1, *spots), load(x_ref, 2, *spots), apart)
        under = apart_mask(BLK)
        for branch in range(BRANCHES):
            first = TRUNK + BRANCHES + LEAVES * branch
            spots = (at(first), at(first + 1))
            near = (at(TRUNK + branch),) + spots
            attend(spots, TRUNK_ROWS, load(x_ref, 1, *near), load(x_ref, 2, *near), under)
        return carry

    lax.fori_loop(0, trees, one_tree, 0)


def attend_forward(order, packed):
    groups = packed.shape[0]
    blocks = packed.shape[2]
    trees = groups * blocks // TREE_BLOCKS
    pairs = trees * TREE_BLOCKS * BLK * 1100
    return pl.pallas_call(
        functools.partial(forward_kernel, trees),
        in_specs=[
            pl.BlockSpec(memory_space=pltpu.SMEM),
            pl.BlockSpec(memory_space=pltpu.VMEM),
        ],
        out_specs=pl.BlockSpec(memory_space=pltpu.VMEM),
        out_shape=jax.ShapeDtypeStruct((groups, blocks, BLK, HEAD), bf16),
        scratch_shapes=[
            pltpu.VMEM((TRUNK_ROWS, HEAD), bf16),
            pltpu.VMEM((HEAD, TRUNK_ROWS), bf16),
        ],
        compiler_params=pltpu.CompilerParams(vmem_limit_bytes=VMEM_LIMIT),
        cost_estimate=pl.CostEstimate(
            flops=pairs * HEAD * 4, bytes_accessed=packed.size * 3, transcendentals=pairs
        ),
        name="attend_forward",
    )(order, packed)


def backward_kernel(
    trees, order_ref, x_ref, dy_ref, out_ref, k_ref, kt_ref, v_ref, dk_ref, dv_ref, dkb_ref, dvb_ref
):
    def one_tree(tree, carry):
        at = places(order_ref, tree)
        for within in range(TRUNK):
            rows = slice(within * BLK, (within + 1) * BLK)
            spot = at(within)
            keys = load(x_ref, 1, spot)
            k_ref[rows, :] = keys
            kt_ref[:, rows] = across(keys)
            v_ref[rows, :] = load(x_ref, 2, spot)

        def attend(spots, far_rows, near_spots, mask, start):
            queries = load(x_ref, 0, *spots)
            grads = jnp.concatenate(
                [dy_ref[spots[0][0], spots[0][1]], dy_ref[spots[1][0], spots[1][1]]], axis=0
            )
            near_keys = load(x_ref, 1, *near_spots)
            near_values = load(x_ref, 2, *near_spots)
            far, near = softmax_parts(
                queries, k_ref[:far_rows, :] if far_rows else None, near_keys, mask
            )
            near_grad = nt(near_values, grads)
            inner = jnp.sum(near * near_grad, axis=0, keepdims=True)
            if far_rows:
                far_grad = nt(v_ref[:far_rows, :], grads)
                inner = inner + jnp.sum(far * far_grad, axis=0, keepdims=True)
                far_score = (far * (far_grad - inner)).astype(bf16)
                far_dk = nn(far_score, queries)
                far_dv = nn(far.astype(bf16), grads)
                if start:
                    dk_ref[:far_rows, :] = far_dk
                    dv_ref[:far_rows, :] = far_dv
                else:
                    dk_ref[:far_rows, :] += far_dk
                    dv_ref[:far_rows, :] += far_dv
            near_score = (near * (near_grad - inner)).astype(bf16)
            turned = nn(across(near_keys), near_score)
            if far_rows:
                turned = turned + nn(kt_ref[:, :far_rows], far_score)
            rows = (jnp.transpose(turned) * SCALING).astype(bf16)
            out_ref[spots[0][0], 0, spots[0][1]] = rows[:BLK]
            out_ref[spots[1][0], 0, spots[1][1]] = rows[BLK:]
            return nn(near_score, queries), nn(near.astype(bf16), grads)

        def store(spot, key_grad, value_grad):
            out_ref[spot[0], 1, spot[1]] = (key_grad * SCALING).astype(bf16)
            out_ref[spot[0], 2, spot[1]] = value_grad.astype(bf16)

        under = apart_mask(BLK)
        for branch in range(BRANCHES):
            first = TRUNK + BRANCHES + LEAVES * branch
            spots = (at(first), at(first + 1))
            key_grad, value_grad = attend(
                spots, TRUNK_ROWS, (at(TRUNK + branch),) + spots, under, branch == 0
            )
            dkb_ref[branch] = key_grad[:BLK]
            dvb_ref[branch] = value_grad[:BLK]
            store(spots[0], key_grad[BLK : 2 * BLK], value_grad[BLK : 2 * BLK])
            store(spots[1], key_grad[2 * BLK :], value_grad[2 * BLK :])
        apart = apart_mask(0)
        for pair in range(BRANCHES // 2):
            spots = (at(TRUNK + 2 * pair), at(TRUNK + 2 * pair + 1))
            key_grad, value_grad = attend(spots, TRUNK_ROWS, spots, apart, False)
            for half in range(2):
                rows = slice(half * BLK, (half + 1) * BLK)
                branch = 2 * pair + half
                store(
                    spots[half], key_grad[rows] + dkb_ref[branch], value_grad[rows] + dvb_ref[branch]
                )
        causal = causal_mask()
        for pair in reversed(range(TRUNK // 2)):
            spots = (at(2 * pair), at(2 * pair + 1))
            key_grad, value_grad = attend(spots, pair * PAIR, spots, causal, False)
            for half in range(2):
                rows = slice(half * BLK, (half + 1) * BLK)
                held = slice(pair * PAIR + half * BLK, pair * PAIR + (half + 1) * BLK)
                store(
                    spots[half],
                    key_grad[rows] + dk_ref[held, :],
                    value_grad[rows] + dv_ref[held, :],
                )
        return carry

    lax.fori_loop(0, trees, one_tree, 0)


def attend_backward(order, packed, grads):
    groups = packed.shape[0]
    blocks = packed.shape[2]
    trees = groups * blocks // TREE_BLOCKS
    pairs = trees * TREE_BLOCKS * BLK * 1100
    return pl.pallas_call(
        functools.partial(backward_kernel, trees),
        in_specs=[
            pl.BlockSpec(memory_space=pltpu.SMEM),
            pl.BlockSpec(memory_space=pltpu.VMEM),
            pl.BlockSpec(memory_space=pltpu.VMEM),
        ],
        out_specs=pl.BlockSpec(memory_space=pltpu.VMEM),
        out_shape=jax.ShapeDtypeStruct(packed.shape, bf16),
        scratch_shapes=[
            pltpu.VMEM((TRUNK_ROWS, HEAD), bf16),
            pltpu.VMEM((HEAD, TRUNK_ROWS), bf16),
            pltpu.VMEM((TRUNK_ROWS, HEAD), bf16),
            pltpu.VMEM((TRUNK_ROWS, HEAD), f32),
            pltpu.VMEM((TRUNK_ROWS, HEAD), f32),
            pltpu.VMEM((BRANCHES, BLK, HEAD), f32),
            pltpu.VMEM((BRANCHES, BLK, HEAD), f32),
        ],
        compiler_params=pltpu.CompilerParams(vmem_limit_bytes=VMEM_LIMIT),
        cost_estimate=pl.CostEstimate(
            flops=pairs * HEAD * 10, bytes_accessed=packed.size * 5, transcendentals=pairs
        ),
        name="attend_backward",
    )(order, packed, grads)


def mean_square(values):
    return jnp.mean(values * values, axis=-1, keepdims=True)


def norm_back(gradient, normed, inverse, gain_vec):
    weighted = gradient * gain_vec
    return inverse * (weighted - normed * jnp.mean(normed * weighted, axis=-1, keepdims=True))


def chunk_call(kernel, ins, outs, kept, grid, scratch, cost, name):
    count = len(ins)
    specs = [spec for spec, _ in ins]
    values = [value for _, value in ins]
    aliases = {}
    if kept is not None:
        whole = [at for at, out in enumerate(outs) if out[2]]
        for at, value in zip(whole, kept):
            aliases[len(values)] = at
            specs.append(pl.BlockSpec(memory_space=pl.ANY))
            values.append(value)
    extra = len(values) - count

    def body(*refs):
        kernel(*refs[:count], *refs[count + extra :])

    return pl.pallas_call(
        body,
        grid=grid,
        in_specs=specs,
        out_specs=[out[0] for out in outs],
        out_shape=[out[1] for out in outs],
        scratch_shapes=scratch,
        input_output_aliases=aliases,
        compiler_params=pltpu.CompilerParams(vmem_limit_bytes=VMEM_LIMIT),
        cost_estimate=cost,
        name=name,
    )(*values)


def forward_chunk_kernel(
    place,
    core_ref,
    gain_ref,
    y_hbm,
    x_hbm,
    woa_hbm,
    wob_hbm,
    wg_hbm,
    wr_hbm,
    proj_hbm,
    low_hbm,
    act_hbm,
    silu_hbm,
    slope_hbm,
    part_hbm,
    y_ref,
    x_ref,
    row_ref,
    gate_ref,
    up_ref,
    exact_ref,
    proj_ref,
    low_ref,
    act_ref,
    silu_ref,
    slope_ref,
    part_ref,
    y_sem,
    x_sem,
    row_sems,
    gate_sems,
    up_sems,
    out_sems,
    part_sems,
):
    at, batch, part = place
    rows = y_ref.shape[0]
    units = act_ref.shape[1]
    tiles = D // TILE
    half = tiles // 2
    unit_tiles = units // TILE
    here = pl.ds(at * rows, rows)

    def tile(index):
        return pl.ds(pl.multiple_of(index * TILE, TILE), TILE)

    def out_tile(source, index):
        slot = index if source is woa_hbm else index + half
        return pltpu.make_async_copy(
            source.at[tile(index), :], row_ref.at[slot], row_sems.at[slot]
        )

    def unit_copies(index):
        slot = lax.rem(index, 2)
        return (
            pltpu.make_async_copy(wg_hbm.at[0, :, tile(index)], gate_ref.at[slot], gate_sems.at[slot]),
            pltpu.make_async_copy(wr_hbm.at[0, :, tile(index)], up_ref.at[slot], up_sems.at[slot]),
        )

    def down_copy(index):
        return pltpu.make_async_copy(
            wr_hbm.at[1, tile(index), :], row_ref.at[index, :, pl.ds(0, units)], row_sems.at[index]
        )

    def row_wait(index, width):
        pltpu.make_async_copy(
            woa_hbm.at[pl.ds(0, TILE), pl.ds(0, width)],
            row_ref.at[index, :, pl.ds(0, width)],
            row_sems.at[index],
        ).wait()

    y_copy = pltpu.make_async_copy(y_hbm.at[pl.ds(part * rows, rows), :], y_ref, y_sem)
    x_copy = pltpu.make_async_copy(x_hbm.at[batch, pl.ds(part * rows, rows), :], x_ref, x_sem)
    y_copy.start()
    for index in range(half):
        out_tile(woa_hbm, index).start()
    x_copy.start()
    y_copy.wait()

    def project_tile(index, carry):
        row_wait(index, D)

        @pl.when(index < half)
        def _():
            out_tile(wob_hbm, index).start()

        @pl.when(index >= half)
        def _():
            for copy in unit_copies(index - half):
                copy.start()

        side = jnp.where(index < half, core_ref[0], 1 - core_ref[0])
        columns = tile(side * half + lax.rem(index, half))
        exact_ref[:, columns] = nt(y_ref[...], row_ref[index])
        return carry

    lax.fori_loop(0, tiles, project_tile, 0)
    x_copy.wait()
    proj = exact_ref[...]
    inverse = lax.rsqrt(mean_square(proj) + EPSILON)
    proj_ref[...] = proj.astype(bf16)
    low_ref[...] = (x_ref[...].astype(f32) + proj * inverse * gain_ref[...]).astype(bf16)
    outs = [
        pltpu.make_async_copy(proj_ref, proj_hbm.at[here, :], out_sems.at[0]),
        pltpu.make_async_copy(low_ref, low_hbm.at[here, :], out_sems.at[1]),
        pltpu.make_async_copy(act_ref, act_hbm.at[here, :], out_sems.at[2]),
        pltpu.make_async_copy(silu_ref, silu_hbm.at[here, :], out_sems.at[3]),
        pltpu.make_async_copy(slope_ref, slope_hbm.at[here, :], out_sems.at[4]),
    ]
    outs[0].start()
    outs[1].start()

    def unit_tile(index, carry):
        slot = lax.rem(index, 2)
        for copy in unit_copies(index):
            copy.wait()
        low = low_ref[...]
        gate = nn(low, gate_ref[slot])
        up = nn(low, up_ref[slot])

        @pl.when(index + 2 < unit_tiles)
        def _():
            for copy in unit_copies(index + 2):
                copy.start()

        @pl.when(index + 2 >= unit_tiles)
        def _():
            first = (index + 2 - unit_tiles) * half
            for more in range(half):
                down_copy(first + more).start()

        sigmoid = 1.0 / (1.0 + jnp.exp(-gate))
        silu = gate * sigmoid
        columns = tile(index)
        act_ref[:, columns] = (silu * up).astype(bf16)
        silu_ref[:, columns] = silu.astype(bf16)
        slope_ref[:, columns] = (up * sigmoid * (1.0 + gate * (1.0 - sigmoid))).astype(bf16)
        return carry

    lax.fori_loop(0, unit_tiles, unit_tile, 0)
    for copy in outs[2:]:
        copy.start()

    def part_copy(index):
        columns = tile(index)
        return pltpu.make_async_copy(
            part_ref.at[:, columns], part_hbm.at[:, columns], part_sems.at[index]
        )

    def down_tile(index, carry):
        row_wait(index, units)
        part_ref[:, tile(index)] = nt(act_ref[...], row_ref[index, :, :units]).astype(bf16)
        part_copy(index).start()
        return carry

    lax.fori_loop(0, tiles, down_tile, 0)
    for index in range(tiles):
        part_copy(index).wait()
    for copy in outs:
        copy.wait()


def forward_chunk(at, batch, part, rows, y_all, tokens, gain, w_out, w_mlp, kept):
    core, w_out_a, w_out_b = w_out
    w_gate, w_rest = w_mlp
    units = w_gate.shape[2]
    total = tokens.shape[0] * tokens.shape[1]
    tiles = D // TILE
    anywhere = pl.BlockSpec(memory_space=pl.ANY)
    wide = jax.ShapeDtypeStruct((total, units), bf16)
    narrow = jax.ShapeDtypeStruct((total, D), bf16)
    dma = pltpu.SemaphoreType.DMA
    return chunk_call(
        functools.partial(forward_chunk_kernel, (at, batch, part)),
        [
            (pl.BlockSpec(memory_space=pltpu.SMEM), core),
            (pl.BlockSpec(memory_space=pltpu.VMEM), gain),
            (anywhere, y_all),
            (anywhere, tokens),
            (anywhere, w_out_a),
            (anywhere, w_out_b),
            (anywhere, w_gate),
            (anywhere, w_rest),
        ],
        [
            (anywhere, narrow, True),
            (anywhere, narrow, True),
            (anywhere, wide, True),
            (anywhere, wide, True),
            (anywhere, wide, True),
            (anywhere, jax.ShapeDtypeStruct((rows, D), bf16), False),
        ],
        kept,
        (),
        [
            pltpu.VMEM((rows, D), bf16),
            pltpu.VMEM((rows, D), bf16),
            pltpu.VMEM((tiles, TILE, D), bf16),
            pltpu.VMEM((2, D, TILE), bf16),
            pltpu.VMEM((2, D, TILE), bf16),
            pltpu.VMEM((rows, D), f32),
            pltpu.VMEM((rows, D), bf16),
            pltpu.VMEM((rows, D), bf16),
            pltpu.VMEM((rows, units), bf16),
            pltpu.VMEM((rows, units), bf16),
            pltpu.VMEM((rows, units), bf16),
            pltpu.VMEM((rows, D), bf16),
            dma,
            dma,
            dma((tiles,)),
            dma((2,)),
            dma((2,)),
            dma((5,)),
            dma((tiles,)),
        ],
        pl.CostEstimate(
            flops=2 * rows * D * (D + 3 * units),
            bytes_accessed=2 * D * (D + 3 * units) + 16 * rows * D,
            transcendentals=rows * units,
        ),
        "forward_chunk",
    )


def middle_chunk_kernel(
    place,
    attn_gain_ref,
    gain_ref,
    sum_hbm,
    proj_hbm,
    x_hbm,
    grad_hbm,
    silu_hbm,
    slope_hbm,
    wg_hbm,
    wr_hbm,
    output_hbm,
    low_hbm,
    gate_hbm,
    up_hbm,
    gain_part_ref,
    part_hbm,
    sum_ref,
    proj_ref,
    x_ref,
    grad_ref,
    silu_ref,
    slope_ref,
    down_ref,
    wg_ref,
    wu_ref,
    output_ref,
    low_ref,
    gates_ref,
    ups_ref,
    part_ref,
    in_sems,
    down_sems,
    wg_sems,
    wu_sems,
    out_sems,
    part_sems,
):
    at, batch, part = place
    rows = sum_ref.shape[0]
    units = silu_ref.shape[1]
    tiles = D // TILE
    half = tiles // 2
    unit_tiles = units // TILE
    here = pl.ds(at * rows, rows)
    inside = pl.ds(part * rows, rows)

    def tile(index):
        return pl.ds(pl.multiple_of(index * TILE, TILE), TILE)

    def down_copy(index):
        slot = lax.rem(index, 2)
        return pltpu.make_async_copy(
            wr_hbm.at[1, :, tile(index)], down_ref.at[slot], down_sems.at[slot]
        )

    def row_copies(index):
        slot = lax.rem(index, half)
        return (
            pltpu.make_async_copy(wg_hbm.at[0, tile(index), :], wg_ref.at[slot], wg_sems.at[slot]),
            pltpu.make_async_copy(wr_hbm.at[0, tile(index), :], wu_ref.at[slot], wu_sems.at[slot]),
        )

    ins = [
        pltpu.make_async_copy(sum_hbm, sum_ref, in_sems.at[0]),
        pltpu.make_async_copy(grad_hbm.at[batch, inside, :], grad_ref, in_sems.at[1]),
        pltpu.make_async_copy(proj_hbm.at[here, :], proj_ref, in_sems.at[2]),
        pltpu.make_async_copy(x_hbm.at[batch, inside, :], x_ref, in_sems.at[3]),
        pltpu.make_async_copy(silu_hbm.at[here, :], silu_ref, in_sems.at[4]),
        pltpu.make_async_copy(slope_hbm.at[here, :], slope_ref, in_sems.at[5]),
    ]
    ins[0].start()
    ins[1].start()
    down_copy(0).start()
    ins[4].start()
    ins[5].start()
    down_copy(1).start()
    ins[2].start()
    ins[3].start()
    ins[0].wait()
    ins[1].wait()
    mlp = sum_ref[...].astype(f32)
    mlp_inverse = lax.rsqrt(mean_square(mlp) + EPSILON)
    normed = mlp * mlp_inverse
    grad = grad_ref[...]
    gain_part_ref[...] = jnp.sum(grad * normed, axis=0, keepdims=True)
    low_ref[...] = norm_back(grad, normed, mlp_inverse, gain_ref[...]).astype(bf16)
    outs = [
        pltpu.make_async_copy(output_ref, output_hbm.at[here, :], out_sems.at[0]),
        pltpu.make_async_copy(low_ref, low_hbm.at[here, :], out_sems.at[1]),
        pltpu.make_async_copy(gates_ref, gate_hbm.at[here, :], out_sems.at[2]),
        pltpu.make_async_copy(ups_ref, up_hbm.at[here, :], out_sems.at[3]),
    ]
    outs[1].start()
    ins[4].wait()
    ins[5].wait()

    def unit_tile(index, carry):
        down_copy(index).wait()
        act_grad = nn(low_ref[...], down_ref[lax.rem(index, 2)])

        @pl.when(index + 2 < unit_tiles)
        def _():
            down_copy(index + 2).start()

        @pl.when(index + 2 >= unit_tiles)
        def _():
            for copy in row_copies(index + 2 - unit_tiles):
                copy.start()

        columns = tile(index)
        ups_ref[:, columns] = (act_grad * silu_ref[:, columns].astype(f32)).astype(bf16)
        gates_ref[:, columns] = (act_grad * slope_ref[:, columns].astype(f32)).astype(bf16)
        return carry

    lax.fori_loop(0, unit_tiles, unit_tile, 0)
    outs[2].start()
    outs[3].start()
    ins[2].wait()
    ins[3].wait()
    proj = proj_ref[...].astype(f32)
    inverse = lax.rsqrt(mean_square(proj) + EPSILON)
    hidden = x_ref[...].astype(f32) + proj * inverse * attn_gain_ref[...]
    mlp = sum_ref[...].astype(f32)
    output_ref[...] = (hidden + mlp * mlp_inverse * gain_ref[...]).astype(bf16)
    outs[0].start()

    def part_copy(index):
        columns = tile(index)
        return pltpu.make_async_copy(
            part_ref.at[:, columns], part_hbm.at[:, columns], part_sems.at[index]
        )

    def row_tile(index, carry):
        slot = lax.rem(index, half)
        for copy in row_copies(index):
            copy.wait()
        part_ref[:, tile(index)] = (
            nt(gates_ref[...], wg_ref[slot]) + nt(ups_ref[...], wu_ref[slot])
        ).astype(bf16)
        part_copy(index).start()

        @pl.when(index + half < tiles)
        def _():
            for copy in row_copies(index + half):
                copy.start()

        return carry

    lax.fori_loop(0, tiles, row_tile, 0)
    for index in range(tiles):
        part_copy(index).wait()
    for copy in outs:
        copy.wait()


def middle_chunk(
    at, batch, part, rows, mlp_sum, proj, tokens, grad, attn_gain, gain, silu, slope, w_mlp, kept
):
    w_gate, w_rest = w_mlp
    units = w_gate.shape[2]
    total = proj.shape[0]
    tiles = D // TILE
    half = tiles // 2
    vmem = pl.BlockSpec(memory_space=pltpu.VMEM)
    anywhere = pl.BlockSpec(memory_space=pl.ANY)
    wide = jax.ShapeDtypeStruct((total, units), bf16)
    narrow = jax.ShapeDtypeStruct((total, D), bf16)
    dma = pltpu.SemaphoreType.DMA
    return chunk_call(
        functools.partial(middle_chunk_kernel, (at, batch, part)),
        [
            (vmem, attn_gain),
            (vmem, gain),
            (anywhere, mlp_sum),
            (anywhere, proj),
            (anywhere, tokens),
            (anywhere, grad),
            (anywhere, silu),
            (anywhere, slope),
            (anywhere, w_gate),
            (anywhere, w_rest),
        ],
        [
            (anywhere, narrow, True),
            (anywhere, narrow, True),
            (anywhere, wide, True),
            (anywhere, wide, True),
            (vmem, jax.ShapeDtypeStruct((1, D), f32), False),
            (anywhere, jax.ShapeDtypeStruct((rows, D), bf16), False),
        ],
        kept,
        (),
        [
            pltpu.VMEM((rows, D), bf16),
            pltpu.VMEM((rows, D), bf16),
            pltpu.VMEM((rows, D), bf16),
            pltpu.VMEM((rows, D), f32),
            pltpu.VMEM((rows, units), bf16),
            pltpu.VMEM((rows, units), bf16),
            pltpu.VMEM((2, D, TILE), bf16),
            pltpu.VMEM((half, TILE, units), bf16),
            pltpu.VMEM((half, TILE, units), bf16),
            pltpu.VMEM((rows, D), bf16),
            pltpu.VMEM((rows, D), bf16),
            pltpu.VMEM((rows, units), bf16),
            pltpu.VMEM((rows, units), bf16),
            pltpu.VMEM((rows, D), bf16),
            dma((6,)),
            dma((2,)),
            dma((half,)),
            dma((half,)),
            dma((4,)),
            dma((tiles,)),
        ],
        pl.CostEstimate(
            flops=2 * rows * D * 3 * units,
            bytes_accessed=2 * D * 3 * units + 24 * rows * D,
            transcendentals=rows,
        ),
        "middle_chunk",
    )


def backward_chunk_kernel(
    heads, sum_ref, grad_ref, proj_ref, gain_ref, wo_ref, hidden_ref, low_ref, dy_ref, gain_part_ref
):
    hidden_grad = grad_ref[...] + sum_ref[...].astype(f32)
    proj = proj_ref[...].astype(f32)
    inverse = lax.rsqrt(mean_square(proj) + EPSILON)
    normed = proj * inverse
    hidden_ref[...] = hidden_grad
    gain_part_ref[...] = jnp.sum(hidden_grad * normed, axis=0, keepdims=True)
    low = norm_back(hidden_grad, normed, inverse, gain_ref[...]).astype(bf16)
    low_ref[...] = low
    grad = nn(low, wo_ref[...])
    for head in range(heads):
        dy_ref[head] = grad[:, head_cols(head)].astype(bf16)


def backward_chunk(at, batch, part, rows, branch_sum, grad, proj, gain, w_attn, kept):
    total = proj.shape[0]
    width = w_attn.shape[2]
    heads = width // HEAD
    whole = pl.BlockSpec((rows, D), lambda s: (at, 0))
    line = pl.BlockSpec((1, D), lambda s: (0, 0))
    return chunk_call(
        functools.partial(backward_chunk_kernel, heads),
        [
            (pl.BlockSpec((rows, D), lambda s: (0, 0)), branch_sum),
            (pl.BlockSpec((None, rows, D), lambda s: (batch, part, 0)), grad),
            (whole, proj),
            (line, gain),
            (pl.BlockSpec((None, D, width), lambda s: (3, 0, 0)), w_attn),
        ],
        [
            (whole, jax.ShapeDtypeStruct((total, D), f32), True),
            (whole, jax.ShapeDtypeStruct((total, D), bf16), True),
            (
                pl.BlockSpec((heads, rows, HEAD), lambda s: (0, at, 0)),
                jax.ShapeDtypeStruct((heads, total, HEAD), bf16),
                True,
            ),
            (line, jax.ShapeDtypeStruct((1, D), f32), False),
        ],
        kept,
        (1,),
        [],
        pl.CostEstimate(
            flops=2 * rows * D * width, bytes_accessed=16 * rows * D, transcendentals=rows
        ),
        "backward_chunk",
    )


def weight_sum_kernel(count, left_ref, right_ref, out_ref):
    units = out_ref.shape[2]
    for at in range(count):
        out_ref[at] = lax.dot_general(
            left_ref[...],
            right_ref[:, at * units : (at + 1) * units],
            (((0,), (0,)), ((), ())),
            preferred_element_type=f32,
        ).astype(bf16)


def weight_sum(first, slots, count, left, right, kept):
    rows, depth = left.shape
    units = right.shape[1] // slots
    return chunk_call(
        functools.partial(weight_sum_kernel, slots),
        [
            (pl.BlockSpec((rows, TILE), lambda s: (0, s)), left),
            (pl.BlockSpec((rows, slots * units), lambda s: (0, 0)), right),
        ],
        [
            (
                pl.BlockSpec((slots, TILE, units), lambda s: (first // slots, s, 0)),
                jax.ShapeDtypeStruct((count, depth, units), bf16),
                True,
            )
        ],
        kept,
        (depth // TILE,),
        [],
        pl.CostEstimate(
            flops=2 * rows * depth * units * slots,
            bytes_accessed=2 * slots * (rows * depth + rows * units + depth * units),
            transcendentals=0,
        ),
        "weight_sum",
    )


def shards(
    layer_input,
    cotangent,
    w_query,
    w_key,
    w_value,
    w_output,
    w_gate,
    w_up,
    w_down,
    query_gain,
    key_gain,
    attn_gain,
    mlp_gain,
    slot_parent,
    slot_depth,
):
    dp_index = lax.axis_index("dp")
    tp_index = lax.axis_index("tensor")
    dp_count = lax.axis_size("dp")
    tp_count = lax.axis_size("tensor")
    rows = layer_input.shape[1]
    share = rows // tp_count
    width = w_query.shape[1]
    heads = width // HEAD
    hidden_width = w_gate.shape[1]
    items = heads * MB
    copies = dp_count // items

    def gather_stack(*pieces):
        return lax.all_gather(jnp.stack(pieces), "dp", axis=1, tiled=True)

    def scatter_rows(total, dimension=0):
        return lax.psum_scatter(
            total.astype(bf16), "dp", scatter_dimension=dimension, tiled=True
        )

    def exchange(pieces):
        flat = pieces.reshape((items, -1, HEAD))
        if copies > 1:
            flat = jnp.tile(flat, (copies, 1, 1))
        return lax.all_to_all(flat, "dp", split_axis=0, concat_axis=0, tiled=True)

    def give_back(pieces):
        flat = pieces.reshape((dp_count, -1, HEAD))
        return lax.all_to_all(flat, "dp", split_axis=0, concat_axis=0, tiled=True)[:items]

    w_attn = gather_stack(w_query, w_key, w_value, jnp.transpose(w_output))
    w_gate_all = gather_stack(w_gate)

    order = tree_order(slot_parent, slot_depth)
    my_batch = lax.rem(lax.rem(dp_index, items), MB)
    my_order = lax.dynamic_index_in_dim(order, my_batch, 0, keepdims=False)
    my_depth = lax.dynamic_slice_in_dim(slot_depth, dp_index * SEG_DEV, SEG_DEV, 1)
    cosines, sines = rope_tables(my_depth)

    q_raw, k_raw, squares = project(layer_input, w_attn, (0, 1), True)
    squares = jnp.transpose(squares.reshape(MB * rows, 2))
    (v_raw,) = project(layer_input, w_attn, (2,), False)
    squares = small_sum(squares, "tensor", tp_count)
    inverse = jnp.transpose(lax.rsqrt(squares / D + EPSILON)).reshape(MB, rows, 2)
    gains = jnp.concatenate([query_gain, key_gain])[None, :]
    packed = pack_heads(q_raw, k_raw, v_raw, inverse, gains, cosines, sines, heads)
    w_out_begun = begin_output_weight(w_attn[3], packed, dp_index, dp_count, tp_count)
    packed = follow(exchange(packed), w_out_begun[1:]).reshape(dp_count, 3, SEG_DEV, BLK, HEAD)
    w_out = end_output_weight(w_out_begun, packed, dp_index, dp_count, tp_count)
    w_mlp = (w_gate_all, gather_stack(*follow((w_up, jnp.transpose(w_down)), packed)))

    attended = give_back(attend_forward(my_order, packed))
    attended = attended.reshape(heads, MB, rows, HEAD).transpose(1, 2, 0, 3)
    attended = attended.reshape(MB, rows, width)

    parts = 2
    step = rows // parts
    spots = [(batch, part) for batch in range(MB) for part in range(parts)]
    begun = go_on_all_gather(begin_all_gather(attended[0], tp_count), tp_count)
    gathered, hop = end_all_gather(begun, tp_count)
    everything = [gathered]
    begun = [begun]
    for batch in range(1, MB):
        begun.append(begin_all_gather(follow(attended[batch], hop), tp_count))
    sums = SumLine(tp_count)
    attn_gain_row = attn_gain[None, :]
    mlp_gain_row = mlp_gain[None, :]
    chunks = len(spots)
    state = dict(forward=None, middle=None, backward=None)
    mlp_gain_parts = []
    attn_gain_parts = []

    def forward(at, after):
        batch, part = spots[at]
        if batch == len(everything):
            early = sums.terms[0] if sums.terms else None
            going = go_on_all_gather(begun[batch], tp_count)
            everything.append(end_all_gather(going, tp_count, early)[0])
        *state["forward"], term = forward_chunk(
            at,
            batch,
            part,
            step,
            follow(everything[batch], after),
            layer_input,
            attn_gain_row,
            w_out,
            w_mlp,
            state["forward"],
        )
        return term

    def middle(at, after):
        batch, part = spots[at]
        proj, _, _, silu, slope = state["forward"]
        *kept, gain_part, term = middle_chunk(
            at,
            batch,
            part,
            step,
            follow(sums.sums[at], after),
            proj,
            layer_input,
            cotangent,
            attn_gain_row,
            mlp_gain_row,
            silu,
            slope,
            w_mlp,
            state["middle"],
        )
        state["middle"] = kept
        mlp_gain_parts.append(gain_part)
        return term

    def backward(at, after):
        batch, part = spots[at]
        *kept, gain_part = backward_chunk(
            at,
            batch,
            part,
            step,
            follow(sums.sums[chunks + at], after),
            cotangent,
            state["forward"][0],
            attn_gain_row,
            w_attn,
            state["backward"],
        )
        state["backward"] = kept
        attn_gain_parts.append(gain_part)
        return gain_part

    sums.enter(forward(0, None))
    sums.enter(forward(1, None))
    last = None
    mlp_total = None
    for at in range(2 * chunks + 2):
        after = sums.terms[-1] if last is None and tp_count == 4 else last
        moved = tuple(sums.advance(after)) or None
        coming = at + 2
        if coming < chunks:
            last = forward(coming, moved)
            sums.enter(last)
        elif coming < 2 * chunks:
            last = middle(coming - chunks, moved)
            sums.enter(last)
        else:
            last = backward(coming - 2 * chunks, moved)
            turn_at = coming - 2 * chunks
            output, mlp_grad, gate_grad, up_grad = state["middle"]
            hidden_low, act = state["forward"][1:3]
            left, right = (
                (hidden_low, gate_grad),
                (hidden_low, up_grad),
                (mlp_grad, act),
                (None, None),
            )[turn_at]
            if left is not None:
                mlp_total = weight_sum(turn_at, 1, 3, follow(left, last), right, mlp_total)
                last = mlp_total[0]
        if coming == 3 * chunks - 1:
            break
    hidden_grad, proj_grad, attn_grad = state["backward"]
    mlp_weight_grad = scatter_rows(follow(mlp_total[0], attn_grad), 1)
    attended = attended.reshape(MB * rows, width)
    attn_total = weight_sum(3, 1, 4, proj_grad, follow(attended, attn_grad), None)

    attn_grad = follow(exchange(attn_grad), attn_total)
    attn_grad = attn_grad.reshape(dp_count, SEG_DEV, BLK, HEAD)
    back = give_back(attend_backward(my_order, packed, attn_grad))
    back = back.reshape(heads, MB, 3, rows, HEAD)
    inner, gain_part = inner_sums(back, q_raw, k_raw, inverse, gains, cosines, sines, heads)
    means = small_sum(jnp.transpose(inner.reshape(-1, 2)), "tensor", tp_count) / D
    means = jnp.transpose(means).reshape(MB, rows, 2)
    qkv_grad = None
    terms = []
    for batch in range(MB):
        *qkv_grad, term = unpack_heads(
            batch, back, q_raw, k_raw, inverse, means, gains, cosines, sines, w_attn, heads, qkv_grad
        )
        terms.append(term)
    mlp_weight_grads = [
        mlp_weight_grad[0].astype(f32),
        mlp_weight_grad[1].astype(f32),
        jnp.transpose(mlp_weight_grad[2].astype(f32)),
    ]
    parts, first_operands, second_operands = line_reduce_scatter(terms, tp_count, mlp_weight_grads)
    tokens = layer_input.reshape(MB * rows, D)
    qkv_grad = qkv_grad[0]
    attn_total = weight_sum(0, 3, 4, tokens, qkv_grad, attn_total)
    attn_total = follow(attn_total[0], (mlp_weight_grad, first_operands))
    attn_weight_grad = scatter_rows(attn_total, 1)
    attn_weight_grads = [attn_weight_grad[at].astype(f32) for at in range(4)]
    attn_weight_grads[3] = jnp.transpose(attn_weight_grads[3])
    parts[-1] = (follow(parts[-1][0], attn_weight_grads),) + parts[-1][1:]
    input_grad = jnp.zeros((MB, share, D), f32)
    for batch, part in enumerate(parts):
        mine = lax.dynamic_slice_in_dim(hidden_grad, batch * rows + tp_index * share, share, 0)
        mine = mine + sum(piece.astype(f32) for piece in part)
        input_grad = lax.dynamic_update_slice(input_grad, mine[None], (batch, 0, 0))

    gain_sums = jnp.concatenate(
        [
            gain_part[0],
            sum(attn_gain_parts)[0],
            sum(mlp_gain_parts)[0],
        ]
    )
    gain_sums = follow(gain_sums.reshape(-1, HEAD), second_operands)
    gain_sums = small_sum(gain_sums, "dp", dp_count).reshape(-1)
    return (
        output.reshape(MB, rows, D),
        input_grad,
        *attn_weight_grads,
        *mlp_weight_grads,
        gain_sums[:width],
        gain_sums[width : 2 * width],
        gain_sums[2 * width : 2 * width + D],
        gain_sums[2 * width + D :],
    )


def solution(mesh):
    in_specs = (
        P(None, "dp", None),
        P(None, "dp", None),
        P("dp", "tensor"),
        P("dp", "tensor"),
        P("dp", "tensor"),
        P("tensor", "dp"),
        P("dp", "tensor"),
        P("dp", "tensor"),
        P("tensor", "dp"),
        P("tensor"),
        P("tensor"),
        P(),
        P(),
        P(),
        P(),
    )
    out_specs = (
        P(None, "dp", None),
        P(None, ("dp", "tensor"), None),
        P("dp", "tensor"),
        P("dp", "tensor"),
        P("dp", "tensor"),
        P("tensor", "dp"),
        P("dp", "tensor"),
        P("dp", "tensor"),
        P("tensor", "dp"),
        P("tensor"),
        P("tensor"),
        P(),
        P(),
    )
    return jax.shard_map(shards, mesh=mesh, in_specs=in_specs, out_specs=out_specs, check_vma=False)
```

```python
import functools

import jax
import jax.numpy as jnp
from jax import lax
from jax.experimental import pallas as pl
from jax.experimental.pallas import tpu as pltpu
from jax.sharding import PartitionSpec as P

D = 2048
HEADS = 16
HEAD = D // HEADS
BLK = 128
TRUNK = 8
BRANCHES = 4
LEAVES = 2
TREE_BLOCKS = 20
MB = 2
SEG_DEV = 5
PAIR = 2 * BLK
TRUNK_ROWS = TRUNK * BLK
TILE = 512

EPSILON = 1e-06
ROPE_BASE = 500000.0
SCALING = HEAD ** (-0.5)
VMEM_LIMIT = 42 * 1024 * 1024

f32 = jnp.float32
bf16 = jnp.bfloat16


def tree_order(parents, depths):
    blocks = parents.shape[1]
    ids = jnp.arange(blocks, dtype=jnp.int32)

    def follow(table, index):
        hot = index[:, :, None] == ids[None, None, :]
        return jnp.sum(jnp.where(hot, table[:, None, :], 0), axis=-1)

    up2 = follow(parents, parents)
    up4 = follow(up2, up2)
    up8 = follow(up4, up4)
    root = follow(up8, up8)
    is_leaf = depths == TRUNK + 1
    above = jnp.where(is_leaf, parents, 0)
    key = ((root * (TRUNK + 2) + depths) * blocks + above) * blocks + ids[None, :]
    rank = jnp.sum((key[:, None, :] < key[:, :, None]).astype(jnp.int32), axis=-1)
    return jnp.sum(
        jnp.where(rank[:, None, :] == ids[None, :, None], ids[None, None, :], 0), axis=-1
    ).astype(jnp.int32)


def rope_tables(depths):
    half = HEAD // 2
    offsets = jnp.arange(BLK, dtype=jnp.int32)
    places = (depths[:, :, None] * BLK + offsets).reshape(depths.shape[0], -1).astype(f32)
    frequency = ROPE_BASE ** (-2.0 * jnp.arange(half, dtype=f32) / HEAD)
    angles = places[:, :, None] * frequency
    cosines = jnp.cos(angles)
    sines = jnp.sin(angles)
    return (
        jnp.concatenate([cosines, cosines], -1),
        jnp.concatenate([-sines, sines], -1),
    )


def low_sum(*parts):
    total = parts[0].astype(f32)
    for part in parts[1:]:
        total = total + part.astype(f32)
    return total.astype(bf16)


def follow(values, after):
    if after is None:
        return values
    return lax.optimization_barrier((values, after))[0]


def small_sum(values, axis, count):
    step = 1
    while step < count:
        values = values + lax.ppermute(values, axis, [(i, i ^ step) for i in range(count)])
        step *= 2
    return values


class SumLine:
    def __init__(self, count):
        self.count = count
        index = lax.axis_index("tensor")
        self.inner = (index == 1) | (index == 2)
        self.terms = []
        self.inward = []
        self.sides = []
        self.across = []
        self.totals = []
        self.outward = []
        self.sums = []

    def enter(self, term):
        if self.count != 4:
            self.sums.append(lax.psum(term, "tensor"))
            return
        self.terms.append(term)
        self.inward.append(lax.ppermute(term, "tensor", [(0, 1), (3, 2)]))

    def advance(self, after):
        if self.count != 4:
            return []
        moved = []
        if len(self.sides) < len(self.terms):
            at = len(self.sides)
            side = low_sum(follow(self.terms[at], after), self.inward[at])
            self.sides.append(side)
            moved.append(side)
        at = len(self.totals)
        if at < len(self.sides) - 1 or (at < len(self.sides) and not moved):
            total = low_sum(follow(self.sides[at], after), self.across[at])
            self.totals.append(total)
            moved.append(total)
        at = len(self.sums)
        if at < len(self.outward):
            self.sums.append(
                jnp.where(self.inner, follow(self.totals[at], after), self.outward[at])
            )
        if len(self.across) < len(self.sides):
            self.across.append(lax.ppermute(self.sides[-1], "tensor", [(1, 2), (2, 1)]))
        if len(self.outward) < len(self.totals):
            self.outward.append(lax.ppermute(self.totals[-1], "tensor", [(1, 0), (2, 3)]))
        return moved


def line_reduce_scatter(batches, count, late):
    if count != 4:
        return [
            (lax.psum_scatter(values, "tensor", scatter_dimension=0, tiled=True),)
            for values in batches
        ], None, None
    index = lax.axis_index("tensor")
    rights = []
    lefts = []
    blocks = [item.reshape(count, item.shape[0] // count, item.shape[1]) for item in batches]

    def block(item, at):
        return lax.dynamic_index_in_dim(item, lax.rem(at + 2 * count, count), 0, keepdims=False)

    operands = []
    for stage in range(count - 1):
        to_right = [(i, i + 1) for i in range(stage + 1)]
        to_left = [(count - 1 - i, count - 2 - i) for i in range(stage + 1)]
        for at, item in enumerate(blocks):
            right = block(item, index + count - 1 - stage)
            left = block(item, index - count + 1 + stage)
            before = max(at - 1, 0)
            if stage:
                arrived = follow((rights[at], lefts[at]), (rights[before], lefts[before]))
                right = low_sum(right, arrived[0])
                left = low_sum(left, arrived[1])
            elif at:
                right, left = follow((right, left), (rights[before], lefts[before]))
            if stage:
                if stage == 1 and at == len(blocks) - 1:
                    right, left = follow((right, left), late)
                rights[at] = lax.ppermute(right, "tensor", to_right)
                lefts[at] = lax.ppermute(left, "tensor", to_left)
            else:
                rights.append(lax.ppermute(right, "tensor", to_right))
                lefts.append(lax.ppermute(left, "tensor", to_left))
            operands.append((right, left))
    sums = [
        (block(item, index), right, left) for item, right, left in zip(blocks, rights, lefts)
    ]
    return sums, operands[1], operands[len(blocks)]


def begin_all_gather(values, count):
    if count != 4:
        return values, None
    right = lax.ppermute(values, "tensor", [(0, 1), (1, 2), (2, 3)])
    left = lax.ppermute(values, "tensor", [(3, 2), (2, 1), (1, 0)])
    return values, (right, left)


def go_on_all_gather(begun, count):
    values, first = begun
    if count != 4:
        return values, None, None
    right = lax.ppermute(first[0], "tensor", [(1, 2), (2, 3)])
    left = lax.ppermute(first[1], "tensor", [(2, 1), (1, 0)])
    return values, first, (right, left)


def end_all_gather(begun, count, after=None):
    values, first, second = begun
    if count != 4:
        return lax.all_gather(values, "tensor", axis=1, tiled=True), None
    index = lax.axis_index("tensor")
    width = values.shape[1]
    right, left = follow(second, after)
    right = lax.ppermute(right, "tensor", [(2, 3)])
    left = lax.ppermute(left, "tensor", [(1, 0)])
    whole = jnp.zeros((values.shape[0], count * width), values.dtype)
    pieces = (
        values,
        jnp.where(index >= 1, first[0], left),
        jnp.where(index >= 2, second[0], second[1]),
        jnp.where(index >= 3, right, first[1]),
    )
    for back, piece in enumerate(pieces):
        place = lax.rem(index - back + count, count) * width
        whole = lax.dynamic_update_slice(whole, piece, (0, place))
    return whole, (right, left)


def begin_output_weight(own, after, dp_index, dp_count, count):
    if count != 4 or dp_count % 2:
        return own, None, None
    half = own.shape[0] // 2
    mine = lax.dynamic_slice_in_dim(follow(own, after), lax.rem(dp_index, 2) * half, half, 0)
    return go_on_all_gather(begin_all_gather(mine, count), count)


def end_output_weight(begun, after, dp_index, dp_count, count):
    if count != 4 or dp_count % 2:
        whole = lax.all_gather(begun[0], "tensor", axis=1, tiled=True)
        half = whole.shape[0] // 2
        return jnp.zeros((1,), jnp.int32), whole[:half], whole[half:]
    mine, _ = end_all_gather(begun, count, after)
    other = lax.ppermute(mine, "dp", [(i, i ^ 1) for i in range(dp_count)])
    return lax.rem(dp_index, 2).astype(jnp.int32).reshape(1), mine, other


def turn(values, cosines, sines):
    return values * cosines + pltpu.roll(values, HEAD // 2, 1) * sines


def head_cols(head, group=0, heads=0):
    start = (group * heads + head) * HEAD
    return slice(start, start + HEAD)


def project_kernel(x_ref, *refs):
    count = len(refs) // 2 if len(refs) > 2 else 1
    weights, outs = refs[:count], refs[count:]
    for at in range(count):
        raw = jnp.dot(x_ref[0], weights[at][0], preferred_element_type=f32)
        outs[at][0] = raw.astype(outs[at].dtype)
        if len(outs) > count:
            outs[count][0, :, at : at + 1] = jnp.sum(raw * raw, axis=1, keepdims=True)


def project(tokens, weights, which, squares):
    batches, rows, _ = tokens.shape
    width = weights.shape[2]
    step = rows // 2
    dtype = f32 if squares else bf16
    out_specs = [pl.BlockSpec((1, step, width), lambda b, r: (b, r, 0))] * len(which)
    out_shape = [jax.ShapeDtypeStruct((batches, rows, width), dtype)] * len(which)
    if squares:
        out_specs.append(pl.BlockSpec((1, step, len(which)), lambda b, r: (b, r, 0)))
        out_shape.append(jax.ShapeDtypeStruct((batches, rows, len(which)), f32))
    return pl.pallas_call(
        project_kernel,
        grid=(batches, rows // step),
        in_specs=[pl.BlockSpec((1, step, D), lambda b, r: (b, r, 0))]
        + [pl.BlockSpec((1, D, width), lambda b, r, at=at: (at, 0, 0)) for at in which],
        out_specs=out_specs,
        out_shape=out_shape,
        compiler_params=pltpu.CompilerParams(vmem_limit_bytes=VMEM_LIMIT),
        cost_estimate=pl.CostEstimate(
            flops=2 * batches * rows * D * width * len(which),
            bytes_accessed=2 * batches * rows * D + 2 * D * width * len(which),
            transcendentals=0,
        ),
        name="project",
    )(tokens, *([weights] * len(which)))


def pack_kernel(heads, q_ref, k_ref, v_ref, inv_ref, gain_ref, cos_ref, sin_ref, out_ref):
    cosines = cos_ref[0]
    sines = sin_ref[0]
    for head in range(heads):
        for which in range(2):
            cols = head_cols(head, which, heads)
            raw_ref = (q_ref, k_ref)[which]
            normed = raw_ref[0, :, head_cols(head)] * inv_ref[0, :, which : which + 1] * gain_ref[:, cols]
            out_ref[head, 0, which] = turn(normed, cosines, sines).astype(bf16)
        out_ref[head, 0, 2] = v_ref[0, :, head_cols(head)]


def pack_heads(q_raw, k_raw, v_raw, inverse, gains, cosines, sines, heads):
    rows = q_raw.shape[1]
    step = rows // 2
    width = heads * HEAD
    return pl.pallas_call(
        functools.partial(pack_kernel, heads),
        grid=(MB, rows // step),
        in_specs=[
            pl.BlockSpec((1, step, width), lambda b, r: (b, r, 0)),
            pl.BlockSpec((1, step, width), lambda b, r: (b, r, 0)),
            pl.BlockSpec((1, step, width), lambda b, r: (b, r, 0)),
            pl.BlockSpec((1, step, 2), lambda b, r: (b, r, 0)),
            pl.BlockSpec((1, 2 * width), lambda b, r: (0, 0)),
            pl.BlockSpec((1, step, HEAD), lambda b, r: (b, r, 0)),
            pl.BlockSpec((1, step, HEAD), lambda b, r: (b, r, 0)),
        ],
        out_specs=pl.BlockSpec((heads, 1, 3, step, HEAD), lambda b, r: (0, b, 0, r, 0)),
        out_shape=jax.ShapeDtypeStruct((heads, MB, 3, rows, HEAD), bf16),
        name="pack_heads",
    )(q_raw, k_raw, v_raw, inverse, gains, cosines, sines)


def inner_kernel(heads, back_ref, q_ref, k_ref, inv_ref, gain_ref, cos_ref, sin_ref, inner_ref, part_ref):
    cosines = cos_ref[0]
    sines = -sin_ref[0]

    @pl.when((pl.program_id(0) == 0) & (pl.program_id(1) == 0))
    def _():
        part_ref[...] = jnp.zeros_like(part_ref)

    for which in range(2):
        total = None
        for head in range(heads):
            cols = head_cols(head, which, heads)
            straight = turn(back_ref[head, 0, which].astype(f32), cosines, sines)
            hat = (q_ref, k_ref)[which][0, :, head_cols(head)] * inv_ref[0, :, which : which + 1]
            product = straight * hat
            part_ref[:, cols] += jnp.sum(product, axis=0, keepdims=True)
            weighted = product * gain_ref[:, cols]
            total = weighted if total is None else total + weighted
        inner_ref[0, :, which : which + 1] = jnp.sum(total, axis=1, keepdims=True)


def inner_sums(back, q_raw, k_raw, inverse, gains, cosines, sines, heads):
    rows = q_raw.shape[1]
    step = rows // 2
    width = heads * HEAD
    return pl.pallas_call(
        functools.partial(inner_kernel, heads),
        grid=(MB, rows // step),
        in_specs=[
            pl.BlockSpec((heads, 1, 2, step, HEAD), lambda b, r: (0, b, 0, r, 0)),
            pl.BlockSpec((1, step, width), lambda b, r: (b, r, 0)),
            pl.BlockSpec((1, step, width), lambda b, r: (b, r, 0)),
            pl.BlockSpec((1, step, 2), lambda b, r: (b, r, 0)),
            pl.BlockSpec((1, 2 * width), lambda b, r: (0, 0)),
            pl.BlockSpec((1, step, HEAD), lambda b, r: (b, r, 0)),
            pl.BlockSpec((1, step, HEAD), lambda b, r: (b, r, 0)),
        ],
        out_specs=[
            pl.BlockSpec((1, step, 2), lambda b, r: (b, r, 0)),
            pl.BlockSpec((1, 2 * width), lambda b, r: (0, 0)),
        ],
        out_shape=[
            jax.ShapeDtypeStruct((MB, rows, 2), f32),
            jax.ShapeDtypeStruct((1, 2 * width), f32),
        ],
        name="inner_sums",
    )(back, q_raw, k_raw, inverse, gains, cosines, sines)


def unpack_kernel(
    heads,
    back_ref,
    q_ref,
    k_ref,
    inv_ref,
    mean_ref,
    gain_ref,
    cos_ref,
    sin_ref,
    wq_ref,
    wk_ref,
    wv_ref,
    grad_ref,
    term_ref,
):
    cosines = cos_ref[0]
    sines = -sin_ref[0]
    width = heads * HEAD
    for head in range(heads):
        for which in range(2):
            cols = head_cols(head, which, heads)
            inverse = inv_ref[0, :, which : which + 1]
            straight = turn(back_ref[head, 0, which].astype(f32), cosines, sines)
            hat = (q_ref, k_ref)[which][0, :, head_cols(head)] * inverse
            grad = inverse * (straight * gain_ref[:, cols] - hat * mean_ref[0, :, which : which + 1])
            grad_ref[:, cols] = grad.astype(bf16)
        grad_ref[:, head_cols(head, 2, heads)] = back_ref[head, 0, 2]
    term = nt(grad_ref[:, :width], wq_ref[0])
    term = term + nt(grad_ref[:, width : 2 * width], wk_ref[0])
    term = term + nt(grad_ref[:, 2 * width :], wv_ref[0])
    term_ref[...] = term.astype(bf16)


def unpack_heads(
    batch, back, q_raw, k_raw, inverse, means, gains, cosines, sines, weights, heads, kept
):
    rows = q_raw.shape[1]
    step = rows // 2
    width = heads * HEAD
    row_spec = lambda cols: pl.BlockSpec((1, step, cols), lambda r: (batch, r, 0))
    return chunk_call(
        functools.partial(unpack_kernel, heads),
        [
            (pl.BlockSpec((heads, 1, 3, step, HEAD), lambda r: (0, batch, 0, r, 0)), back),
            (row_spec(width), q_raw),
            (row_spec(width), k_raw),
            (row_spec(2), inverse),
            (row_spec(2), means),
            (pl.BlockSpec((1, 2 * width), lambda r: (0, 0)), gains),
            (row_spec(HEAD), cosines),
            (row_spec(HEAD), sines),
        ]
        + [(pl.BlockSpec((1, D, width), lambda r, at=at: (at, 0, 0)), weights) for at in range(3)],
        [
            (
                pl.BlockSpec((step, 3 * width), lambda r: (batch * 2 + r, 0)),
                jax.ShapeDtypeStruct((MB * rows, 3 * width), bf16),
                True,
            ),
            (
                pl.BlockSpec((step, D), lambda r: (r, 0)),
                jax.ShapeDtypeStruct((rows, D), bf16),
                False,
            ),
        ],
        kept,
        (2,),
        [],
        pl.CostEstimate(flops=6 * rows * D * width, bytes_accessed=8 * rows * D, transcendentals=0),
        "unpack_heads",
    )


def nt(left, right):
    return lax.dot_general(left, right, (((1,), (1,)), ((), ())), preferred_element_type=f32)


def nn(left, right):
    return lax.dot_general(left, right, (((1,), (0,)), ((), ())), preferred_element_type=f32)


def key_query_iotas(keys):
    key_at = lax.broadcasted_iota(jnp.int32, (keys, PAIR), 0)
    query_at = lax.broadcasted_iota(jnp.int32, (keys, PAIR), 1)
    return key_at, query_at


def causal_mask():
    key_at, query_at = key_query_iotas(PAIR)
    return key_at <= query_at


def apart_mask(above):
    key_at, query_at = key_query_iotas(above + PAIR)
    key_at = key_at - above
    own = (key_at <= query_at) & ((key_at < BLK) == (query_at < BLK))
    return own | (key_at < 0)


def softmax_parts(queries, trunk_keys, near_keys, mask):
    near = jnp.where(mask, nt(near_keys, queries), -1e30)
    top = jnp.max(near, axis=0, keepdims=True)
    if trunk_keys is None:
        near = jnp.exp((near - top) * SCALING)
        scale = 1.0 / jnp.sum(near, axis=0, keepdims=True)
        return None, near * scale
    far = nt(trunk_keys, queries)
    top = jnp.maximum(top, jnp.max(far, axis=0, keepdims=True))
    near = jnp.exp((near - top) * SCALING)
    far = jnp.exp((far - top) * SCALING)
    scale = 1.0 / (jnp.sum(near, axis=0, keepdims=True) + jnp.sum(far, axis=0, keepdims=True))
    return far * scale, near * scale


def places(order_ref, tree):
    def at(within):
        slot = order_ref[tree * TREE_BLOCKS + within]
        return lax.div(slot, SEG_DEV), lax.rem(slot, SEG_DEV)

    return at


def load(ref, which, *spots):
    parts = [ref[group, which, row] for group, row in spots]
    return parts[0] if len(parts) == 1 else jnp.concatenate(parts, axis=0)


def across(values):
    return jnp.transpose(values.astype(f32)).astype(bf16)


def forward_kernel(trees, order_ref, x_ref, y_ref, k_ref, vt_ref):
    def one_tree(tree, carry):
        at = places(order_ref, tree)
        for within in range(TRUNK):
            rows = slice(within * BLK, (within + 1) * BLK)
            spot = at(within)
            k_ref[rows, :] = load(x_ref, 1, spot)
            vt_ref[:, rows] = across(load(x_ref, 2, spot))

        def attend(spots, far_rows, near_keys, near_values, mask):
            queries = load(x_ref, 0, *spots)
            far, near = softmax_parts(
                queries, k_ref[:far_rows, :] if far_rows else None, near_keys, mask
            )
            summed = nn(across(near_values), near.astype(bf16))
            if far_rows:
                summed = summed + nn(vt_ref[:, :far_rows], far.astype(bf16))
            rows = jnp.transpose(summed).astype(bf16)
            y_ref[spots[0][0], spots[0][1]] = rows[:BLK]
            y_ref[spots[1][0], spots[1][1]] = rows[BLK:]

        causal = causal_mask()
        for pair in range(TRUNK // 2):
            spots = (at(2 * pair), at(2 * pair + 1))
            attend(spots, pair * PAIR, load(x_ref, 1, *spots), load(x_ref, 2, *spots), causal)
        apart = apart_mask(0)
        for pair in range(BRANCHES // 2):
            spots = (at(TRUNK + 2 * pair), at(TRUNK + 2 * pair + 1))
            attend(spots, TRUNK_ROWS, load(x_ref, 1, *spots), load(x_ref, 2, *spots), apart)
        under = apart_mask(BLK)
        for branch in range(BRANCHES):
            first = TRUNK + BRANCHES + LEAVES * branch
            spots = (at(first), at(first + 1))
            near = (at(TRUNK + branch),) + spots
            attend(spots, TRUNK_ROWS, load(x_ref, 1, *near), load(x_ref, 2, *near), under)
        return carry

    lax.fori_loop(0, trees, one_tree, 0)


def attend_forward(order, packed):
    groups = packed.shape[0]
    blocks = packed.shape[2]
    trees = groups * blocks // TREE_BLOCKS
    pairs = trees * TREE_BLOCKS * BLK * 1100
    return pl.pallas_call(
        functools.partial(forward_kernel, trees),
        in_specs=[
            pl.BlockSpec(memory_space=pltpu.SMEM),
            pl.BlockSpec(memory_space=pltpu.VMEM),
        ],
        out_specs=pl.BlockSpec(memory_space=pltpu.VMEM),
        out_shape=jax.ShapeDtypeStruct((groups, blocks, BLK, HEAD), bf16),
        scratch_shapes=[
            pltpu.VMEM((TRUNK_ROWS, HEAD), bf16),
            pltpu.VMEM((HEAD, TRUNK_ROWS), bf16),
        ],
        compiler_params=pltpu.CompilerParams(vmem_limit_bytes=VMEM_LIMIT),
        cost_estimate=pl.CostEstimate(
            flops=pairs * HEAD * 4, bytes_accessed=packed.size * 3, transcendentals=pairs
        ),
        name="attend_forward",
    )(order, packed)


def backward_kernel(
    trees, order_ref, x_ref, dy_ref, out_ref, k_ref, kt_ref, v_ref, dk_ref, dv_ref, dkb_ref, dvb_ref
):
    def one_tree(tree, carry):
        at = places(order_ref, tree)
        for within in range(TRUNK):
            rows = slice(within * BLK, (within + 1) * BLK)
            spot = at(within)
            keys = load(x_ref, 1, spot)
            k_ref[rows, :] = keys
            kt_ref[:, rows] = across(keys)
            v_ref[rows, :] = load(x_ref, 2, spot)

        def attend(spots, far_rows, near_spots, mask, start):
            queries = load(x_ref, 0, *spots)
            grads = jnp.concatenate(
                [dy_ref[spots[0][0], spots[0][1]], dy_ref[spots[1][0], spots[1][1]]], axis=0
            )
            near_keys = load(x_ref, 1, *near_spots)
            near_values = load(x_ref, 2, *near_spots)
            far, near = softmax_parts(
                queries, k_ref[:far_rows, :] if far_rows else None, near_keys, mask
            )
            near_grad = nt(near_values, grads)
            inner = jnp.sum(near * near_grad, axis=0, keepdims=True)
            if far_rows:
                far_grad = nt(v_ref[:far_rows, :], grads)
                inner = inner + jnp.sum(far * far_grad, axis=0, keepdims=True)
                far_score = (far * (far_grad - inner)).astype(bf16)
                far_dk = nn(far_score, queries)
                far_dv = nn(far.astype(bf16), grads)
                if start:
                    dk_ref[:far_rows, :] = far_dk
                    dv_ref[:far_rows, :] = far_dv
                else:
                    dk_ref[:far_rows, :] += far_dk
                    dv_ref[:far_rows, :] += far_dv
            near_score = (near * (near_grad - inner)).astype(bf16)
            turned = nn(across(near_keys), near_score)
            if far_rows:
                turned = turned + nn(kt_ref[:, :far_rows], far_score)
            rows = (jnp.transpose(turned) * SCALING).astype(bf16)
            out_ref[spots[0][0], 0, spots[0][1]] = rows[:BLK]
            out_ref[spots[1][0], 0, spots[1][1]] = rows[BLK:]
            return nn(near_score, queries), nn(near.astype(bf16), grads)

        def store(spot, key_grad, value_grad):
            out_ref[spot[0], 1, spot[1]] = (key_grad * SCALING).astype(bf16)
            out_ref[spot[0], 2, spot[1]] = value_grad.astype(bf16)

        under = apart_mask(BLK)
        for branch in range(BRANCHES):
            first = TRUNK + BRANCHES + LEAVES * branch
            spots = (at(first), at(first + 1))
            key_grad, value_grad = attend(
                spots, TRUNK_ROWS, (at(TRUNK + branch),) + spots, under, branch == 0
            )
            dkb_ref[branch] = key_grad[:BLK]
            dvb_ref[branch] = value_grad[:BLK]
            store(spots[0], key_grad[BLK : 2 * BLK], value_grad[BLK : 2 * BLK])
            store(spots[1], key_grad[2 * BLK :], value_grad[2 * BLK :])
        apart = apart_mask(0)
        for pair in range(BRANCHES // 2):
            spots = (at(TRUNK + 2 * pair), at(TRUNK + 2 * pair + 1))
            key_grad, value_grad = attend(spots, TRUNK_ROWS, spots, apart, False)
            for half in range(2):
                rows = slice(half * BLK, (half + 1) * BLK)
                branch = 2 * pair + half
                store(
                    spots[half], key_grad[rows] + dkb_ref[branch], value_grad[rows] + dvb_ref[branch]
                )
        causal = causal_mask()
        for pair in reversed(range(TRUNK // 2)):
            spots = (at(2 * pair), at(2 * pair + 1))
            key_grad, value_grad = attend(spots, pair * PAIR, spots, causal, False)
            for half in range(2):
                rows = slice(half * BLK, (half + 1) * BLK)
                held = slice(pair * PAIR + half * BLK, pair * PAIR + (half + 1) * BLK)
                store(
                    spots[half],
                    key_grad[rows] + dk_ref[held, :],
                    value_grad[rows] + dv_ref[held, :],
                )
        return carry

    lax.fori_loop(0, trees, one_tree, 0)


def attend_backward(order, packed, grads):
    groups = packed.shape[0]
    blocks = packed.shape[2]
    trees = groups * blocks // TREE_BLOCKS
    pairs = trees * TREE_BLOCKS * BLK * 1100
    return pl.pallas_call(
        functools.partial(backward_kernel, trees),
        in_specs=[
            pl.BlockSpec(memory_space=pltpu.SMEM),
            pl.BlockSpec(memory_space=pltpu.VMEM),
            pl.BlockSpec(memory_space=pltpu.VMEM),
        ],
        out_specs=pl.BlockSpec(memory_space=pltpu.VMEM),
        out_shape=jax.ShapeDtypeStruct(packed.shape, bf16),
        scratch_shapes=[
            pltpu.VMEM((TRUNK_ROWS, HEAD), bf16),
            pltpu.VMEM((HEAD, TRUNK_ROWS), bf16),
            pltpu.VMEM((TRUNK_ROWS, HEAD), bf16),
            pltpu.VMEM((TRUNK_ROWS, HEAD), f32),
            pltpu.VMEM((TRUNK_ROWS, HEAD), f32),
            pltpu.VMEM((BRANCHES, BLK, HEAD), f32),
            pltpu.VMEM((BRANCHES, BLK, HEAD), f32),
        ],
        compiler_params=pltpu.CompilerParams(vmem_limit_bytes=VMEM_LIMIT),
        cost_estimate=pl.CostEstimate(
            flops=pairs * HEAD * 10, bytes_accessed=packed.size * 5, transcendentals=pairs
        ),
        name="attend_backward",
    )(order, packed, grads)


def mean_square(values):
    return jnp.mean(values * values, axis=-1, keepdims=True)


def norm_back(gradient, normed, inverse, gain_vec):
    weighted = gradient * gain_vec
    return inverse * (weighted - normed * jnp.mean(normed * weighted, axis=-1, keepdims=True))


def chunk_call(kernel, ins, outs, kept, grid, scratch, cost, name):
    count = len(ins)
    specs = [spec for spec, _ in ins]
    values = [value for _, value in ins]
    aliases = {}
    if kept is not None:
        whole = [at for at, out in enumerate(outs) if out[2]]
        for at, value in zip(whole, kept):
            aliases[len(values)] = at
            specs.append(pl.BlockSpec(memory_space=pl.ANY))
            values.append(value)
    extra = len(values) - count

    def body(*refs):
        kernel(*refs[:count], *refs[count + extra :])

    return pl.pallas_call(
        body,
        grid=grid,
        in_specs=specs,
        out_specs=[out[0] for out in outs],
        out_shape=[out[1] for out in outs],
        scratch_shapes=scratch,
        input_output_aliases=aliases,
        compiler_params=pltpu.CompilerParams(vmem_limit_bytes=VMEM_LIMIT),
        cost_estimate=cost,
        name=name,
    )(*values)


def forward_chunk_kernel(
    place,
    core_ref,
    gain_ref,
    y_hbm,
    x_hbm,
    woa_hbm,
    wob_hbm,
    wg_hbm,
    wr_hbm,
    proj_hbm,
    low_hbm,
    act_hbm,
    silu_hbm,
    slope_hbm,
    part_hbm,
    y_ref,
    x_ref,
    row_ref,
    gate_ref,
    up_ref,
    exact_ref,
    proj_ref,
    low_ref,
    act_ref,
    silu_ref,
    slope_ref,
    part_ref,
    y_sem,
    x_sem,
    row_sems,
    gate_sems,
    up_sems,
    out_sems,
    part_sems,
):
    at, batch, part = place
    rows = y_ref.shape[0]
    units = act_ref.shape[1]
    tiles = D // TILE
    half = tiles // 2
    unit_tiles = units // TILE
    here = pl.ds(at * rows, rows)

    def tile(index):
        return pl.ds(pl.multiple_of(index * TILE, TILE), TILE)

    def out_tile(source, index):
        slot = index if source is woa_hbm else index + half
        return pltpu.make_async_copy(
            source.at[tile(index), :], row_ref.at[slot], row_sems.at[slot]
        )

    def unit_copies(index):
        slot = lax.rem(index, 2)
        return (
            pltpu.make_async_copy(wg_hbm.at[0, :, tile(index)], gate_ref.at[slot], gate_sems.at[slot]),
            pltpu.make_async_copy(wr_hbm.at[0, :, tile(index)], up_ref.at[slot], up_sems.at[slot]),
        )

    def down_copy(index):
        return pltpu.make_async_copy(
            wr_hbm.at[1, tile(index), :], row_ref.at[index, :, pl.ds(0, units)], row_sems.at[index]
        )

    def row_wait(index, width):
        pltpu.make_async_copy(
            woa_hbm.at[pl.ds(0, TILE), pl.ds(0, width)],
            row_ref.at[index, :, pl.ds(0, width)],
            row_sems.at[index],
        ).wait()

    y_copy = pltpu.make_async_copy(y_hbm.at[pl.ds(part * rows, rows), :], y_ref, y_sem)
    x_copy = pltpu.make_async_copy(x_hbm.at[batch, pl.ds(part * rows, rows), :], x_ref, x_sem)
    y_copy.start()
    for index in range(half):
        out_tile(woa_hbm, index).start()
    x_copy.start()
    y_copy.wait()

    def project_tile(index, carry):
        row_wait(index, D)

        @pl.when(index < half)
        def _():
            out_tile(wob_hbm, index).start()

        @pl.when(index >= half)
        def _():
            for copy in unit_copies(index - half):
                copy.start()

        side = jnp.where(index < half, core_ref[0], 1 - core_ref[0])
        columns = tile(side * half + lax.rem(index, half))
        exact_ref[:, columns] = nt(y_ref[...], row_ref[index])
        return carry

    lax.fori_loop(0, tiles, project_tile, 0)
    x_copy.wait()
    proj = exact_ref[...]
    inverse = lax.rsqrt(mean_square(proj) + EPSILON)
    proj_ref[...] = proj.astype(bf16)
    low_ref[...] = (x_ref[...].astype(f32) + proj * inverse * gain_ref[...]).astype(bf16)
    outs = [
        pltpu.make_async_copy(proj_ref, proj_hbm.at[here, :], out_sems.at[0]),
        pltpu.make_async_copy(low_ref, low_hbm.at[here, :], out_sems.at[1]),
        pltpu.make_async_copy(act_ref, act_hbm.at[here, :], out_sems.at[2]),
        pltpu.make_async_copy(silu_ref, silu_hbm.at[here, :], out_sems.at[3]),
        pltpu.make_async_copy(slope_ref, slope_hbm.at[here, :], out_sems.at[4]),
    ]
    outs[0].start()
    outs[1].start()

    def unit_tile(index, carry):
        slot = lax.rem(index, 2)
        for copy in unit_copies(index):
            copy.wait()
        low = low_ref[...]
        gate = nn(low, gate_ref[slot])
        up = nn(low, up_ref[slot])

        @pl.when(index + 2 < unit_tiles)
        def _():
            for copy in unit_copies(index + 2):
                copy.start()

        @pl.when(index + 2 >= unit_tiles)
        def _():
            first = (index + 2 - unit_tiles) * half
            for more in range(half):
                down_copy(first + more).start()

        sigmoid = 1.0 / (1.0 + jnp.exp(-gate))
        silu = gate * sigmoid
        columns = tile(index)
        act_ref[:, columns] = (silu * up).astype(bf16)
        silu_ref[:, columns] = silu.astype(bf16)
        slope_ref[:, columns] = (up * sigmoid * (1.0 + gate * (1.0 - sigmoid))).astype(bf16)
        return carry

    lax.fori_loop(0, unit_tiles, unit_tile, 0)
    for copy in outs[2:]:
        copy.start()

    def part_copy(index):
        columns = tile(index)
        return pltpu.make_async_copy(
            part_ref.at[:, columns], part_hbm.at[:, columns], part_sems.at[index]
        )

    def down_tile(index, carry):
        row_wait(index, units)
        part_ref[:, tile(index)] = nt(act_ref[...], row_ref[index, :, :units]).astype(bf16)
        part_copy(index).start()
        return carry

    lax.fori_loop(0, tiles, down_tile, 0)
    for index in range(tiles):
        part_copy(index).wait()
    for copy in outs:
        copy.wait()


def forward_chunk(at, batch, part, rows, y_all, tokens, gain, w_out, w_mlp, kept):
    core, w_out_a, w_out_b = w_out
    w_gate, w_rest = w_mlp
    units = w_gate.shape[2]
    total = tokens.shape[0] * tokens.shape[1]
    tiles = D // TILE
    anywhere = pl.BlockSpec(memory_space=pl.ANY)
    wide = jax.ShapeDtypeStruct((total, units), bf16)
    narrow = jax.ShapeDtypeStruct((total, D), bf16)
    dma = pltpu.SemaphoreType.DMA
    return chunk_call(
        functools.partial(forward_chunk_kernel, (at, batch, part)),
        [
            (pl.BlockSpec(memory_space=pltpu.SMEM), core),
            (pl.BlockSpec(memory_space=pltpu.VMEM), gain),
            (anywhere, y_all),
            (anywhere, tokens),
            (anywhere, w_out_a),
            (anywhere, w_out_b),
            (anywhere, w_gate),
            (anywhere, w_rest),
        ],
        [
            (anywhere, narrow, True),
            (anywhere, narrow, True),
            (anywhere, wide, True),
            (anywhere, wide, True),
            (anywhere, wide, True),
            (anywhere, jax.ShapeDtypeStruct((rows, D), bf16), False),
        ],
        kept,
        (),
        [
            pltpu.VMEM((rows, D), bf16),
            pltpu.VMEM((rows, D), bf16),
            pltpu.VMEM((tiles, TILE, D), bf16),
            pltpu.VMEM((2, D, TILE), bf16),
            pltpu.VMEM((2, D, TILE), bf16),
            pltpu.VMEM((rows, D), f32),
            pltpu.VMEM((rows, D), bf16),
            pltpu.VMEM((rows, D), bf16),
            pltpu.VMEM((rows, units), bf16),
            pltpu.VMEM((rows, units), bf16),
            pltpu.VMEM((rows, units), bf16),
            pltpu.VMEM((rows, D), bf16),
            dma,
            dma,
            dma((tiles,)),
            dma((2,)),
            dma((2,)),
            dma((5,)),
            dma((tiles,)),
        ],
        pl.CostEstimate(
            flops=2 * rows * D * (D + 3 * units),
            bytes_accessed=2 * D * (D + 3 * units) + 16 * rows * D,
            transcendentals=rows * units,
        ),
        "forward_chunk",
    )


def middle_chunk_kernel(
    place,
    attn_gain_ref,
    gain_ref,
    sum_hbm,
    proj_hbm,
    x_hbm,
    grad_hbm,
    silu_hbm,
    slope_hbm,
    wg_hbm,
    wr_hbm,
    output_hbm,
    low_hbm,
    gate_hbm,
    up_hbm,
    gain_part_ref,
    part_hbm,
    sum_ref,
    proj_ref,
    x_ref,
    grad_ref,
    silu_ref,
    slope_ref,
    down_ref,
    wg_ref,
    wu_ref,
    output_ref,
    low_ref,
    gates_ref,
    ups_ref,
    part_ref,
    in_sems,
    down_sems,
    wg_sems,
    wu_sems,
    out_sems,
    part_sems,
):
    at, batch, part = place
    rows = sum_ref.shape[0]
    units = silu_ref.shape[1]
    tiles = D // TILE
    half = tiles // 2
    unit_tiles = units // TILE
    here = pl.ds(at * rows, rows)
    inside = pl.ds(part * rows, rows)

    def tile(index):
        return pl.ds(pl.multiple_of(index * TILE, TILE), TILE)

    def down_copy(index):
        slot = lax.rem(index, 2)
        return pltpu.make_async_copy(
            wr_hbm.at[1, :, tile(index)], down_ref.at[slot], down_sems.at[slot]
        )

    def row_copies(index):
        slot = lax.rem(index, half)
        return (
            pltpu.make_async_copy(wg_hbm.at[0, tile(index), :], wg_ref.at[slot], wg_sems.at[slot]),
            pltpu.make_async_copy(wr_hbm.at[0, tile(index), :], wu_ref.at[slot], wu_sems.at[slot]),
        )

    ins = [
        pltpu.make_async_copy(sum_hbm, sum_ref, in_sems.at[0]),
        pltpu.make_async_copy(grad_hbm.at[batch, inside, :], grad_ref, in_sems.at[1]),
        pltpu.make_async_copy(proj_hbm.at[here, :], proj_ref, in_sems.at[2]),
        pltpu.make_async_copy(x_hbm.at[batch, inside, :], x_ref, in_sems.at[3]),
        pltpu.make_async_copy(silu_hbm.at[here, :], silu_ref, in_sems.at[4]),
        pltpu.make_async_copy(slope_hbm.at[here, :], slope_ref, in_sems.at[5]),
    ]
    ins[0].start()
    ins[1].start()
    down_copy(0).start()
    ins[4].start()
    ins[5].start()
    down_copy(1).start()
    ins[2].start()
    ins[3].start()
    ins[0].wait()
    ins[1].wait()
    mlp = sum_ref[...].astype(f32)
    mlp_inverse = lax.rsqrt(mean_square(mlp) + EPSILON)
    normed = mlp * mlp_inverse
    grad = grad_ref[...]
    gain_part_ref[...] = jnp.sum(grad * normed, axis=0, keepdims=True)
    low_ref[...] = norm_back(grad, normed, mlp_inverse, gain_ref[...]).astype(bf16)
    outs = [
        pltpu.make_async_copy(output_ref, output_hbm.at[here, :], out_sems.at[0]),
        pltpu.make_async_copy(low_ref, low_hbm.at[here, :], out_sems.at[1]),
        pltpu.make_async_copy(gates_ref, gate_hbm.at[here, :], out_sems.at[2]),
        pltpu.make_async_copy(ups_ref, up_hbm.at[here, :], out_sems.at[3]),
    ]
    outs[1].start()
    ins[4].wait()
    ins[5].wait()

    def unit_tile(index, carry):
        down_copy(index).wait()
        act_grad = nn(low_ref[...], down_ref[lax.rem(index, 2)])

        @pl.when(index + 2 < unit_tiles)
        def _():
            down_copy(index + 2).start()

        @pl.when(index + 2 >= unit_tiles)
        def _():
            for copy in row_copies(index + 2 - unit_tiles):
                copy.start()

        columns = tile(index)
        ups_ref[:, columns] = (act_grad * silu_ref[:, columns].astype(f32)).astype(bf16)
        gates_ref[:, columns] = (act_grad * slope_ref[:, columns].astype(f32)).astype(bf16)
        return carry

    lax.fori_loop(0, unit_tiles, unit_tile, 0)
    outs[2].start()
    outs[3].start()
    ins[2].wait()
    ins[3].wait()
    proj = proj_ref[...].astype(f32)
    inverse = lax.rsqrt(mean_square(proj) + EPSILON)
    hidden = x_ref[...].astype(f32) + proj * inverse * attn_gain_ref[...]
    mlp = sum_ref[...].astype(f32)
    output_ref[...] = (hidden + mlp * mlp_inverse * gain_ref[...]).astype(bf16)
    outs[0].start()

    def part_copy(index):
        columns = tile(index)
        return pltpu.make_async_copy(
            part_ref.at[:, columns], part_hbm.at[:, columns], part_sems.at[index]
        )

    def row_tile(index, carry):
        slot = lax.rem(index, half)
        for copy in row_copies(index):
            copy.wait()
        part_ref[:, tile(index)] = (
            nt(gates_ref[...], wg_ref[slot]) + nt(ups_ref[...], wu_ref[slot])
        ).astype(bf16)
        part_copy(index).start()

        @pl.when(index + half < tiles)
        def _():
            for copy in row_copies(index + half):
                copy.start()

        return carry

    lax.fori_loop(0, tiles, row_tile, 0)
    for index in range(tiles):
        part_copy(index).wait()
    for copy in outs:
        copy.wait()


def middle_chunk(
    at, batch, part, rows, mlp_sum, proj, tokens, grad, attn_gain, gain, silu, slope, w_mlp, kept
):
    w_gate, w_rest = w_mlp
    units = w_gate.shape[2]
    total = proj.shape[0]
    tiles = D // TILE
    half = tiles // 2
    vmem = pl.BlockSpec(memory_space=pltpu.VMEM)
    anywhere = pl.BlockSpec(memory_space=pl.ANY)
    wide = jax.ShapeDtypeStruct((total, units), bf16)
    narrow = jax.ShapeDtypeStruct((total, D), bf16)
    dma = pltpu.SemaphoreType.DMA
    return chunk_call(
        functools.partial(middle_chunk_kernel, (at, batch, part)),
        [
            (vmem, attn_gain),
            (vmem, gain),
            (anywhere, mlp_sum),
            (anywhere, proj),
            (anywhere, tokens),
            (anywhere, grad),
            (anywhere, silu),
            (anywhere, slope),
            (anywhere, w_gate),
            (anywhere, w_rest),
        ],
        [
            (anywhere, narrow, True),
            (anywhere, narrow, True),
            (anywhere, wide, True),
            (anywhere, wide, True),
            (vmem, jax.ShapeDtypeStruct((1, D), f32), False),
            (anywhere, jax.ShapeDtypeStruct((rows, D), bf16), False),
        ],
        kept,
        (),
        [
            pltpu.VMEM((rows, D), bf16),
            pltpu.VMEM((rows, D), bf16),
            pltpu.VMEM((rows, D), bf16),
            pltpu.VMEM((rows, D), f32),
            pltpu.VMEM((rows, units), bf16),
            pltpu.VMEM((rows, units), bf16),
            pltpu.VMEM((2, D, TILE), bf16),
            pltpu.VMEM((half, TILE, units), bf16),
            pltpu.VMEM((half, TILE, units), bf16),
            pltpu.VMEM((rows, D), bf16),
            pltpu.VMEM((rows, D), bf16),
            pltpu.VMEM((rows, units), bf16),
            pltpu.VMEM((rows, units), bf16),
            pltpu.VMEM((rows, D), bf16),
            dma((6,)),
            dma((2,)),
            dma((half,)),
            dma((half,)),
            dma((4,)),
            dma((tiles,)),
        ],
        pl.CostEstimate(
            flops=2 * rows * D * 3 * units,
            bytes_accessed=2 * D * 3 * units + 24 * rows * D,
            transcendentals=rows,
        ),
        "middle_chunk",
    )


def backward_chunk_kernel(
    heads, sum_ref, grad_ref, proj_ref, gain_ref, wo_ref, hidden_ref, low_ref, dy_ref, gain_part_ref
):
    hidden_grad = grad_ref[...] + sum_ref[...].astype(f32)
    proj = proj_ref[...].astype(f32)
    inverse = lax.rsqrt(mean_square(proj) + EPSILON)
    normed = proj * inverse
    hidden_ref[...] = hidden_grad
    gain_part_ref[...] = jnp.sum(hidden_grad * normed, axis=0, keepdims=True)
    low = norm_back(hidden_grad, normed, inverse, gain_ref[...]).astype(bf16)
    low_ref[...] = low
    grad = nn(low, wo_ref[...])
    for head in range(heads):
        dy_ref[head] = grad[:, head_cols(head)].astype(bf16)


def backward_chunk(at, batch, part, rows, branch_sum, grad, proj, gain, w_attn, kept):
    total = proj.shape[0]
    width = w_attn.shape[2]
    heads = width // HEAD
    whole = pl.BlockSpec((rows, D), lambda s: (at, 0))
    line = pl.BlockSpec((1, D), lambda s: (0, 0))
    return chunk_call(
        functools.partial(backward_chunk_kernel, heads),
        [
            (pl.BlockSpec((rows, D), lambda s: (0, 0)), branch_sum),
            (pl.BlockSpec((None, rows, D), lambda s: (batch, part, 0)), grad),
            (whole, proj),
            (line, gain),
            (pl.BlockSpec((None, D, width), lambda s: (3, 0, 0)), w_attn),
        ],
        [
            (whole, jax.ShapeDtypeStruct((total, D), f32), True),
            (whole, jax.ShapeDtypeStruct((total, D), bf16), True),
            (
                pl.BlockSpec((heads, rows, HEAD), lambda s: (0, at, 0)),
                jax.ShapeDtypeStruct((heads, total, HEAD), bf16),
                True,
            ),
            (line, jax.ShapeDtypeStruct((1, D), f32), False),
        ],
        kept,
        (1,),
        [],
        pl.CostEstimate(
            flops=2 * rows * D * width, bytes_accessed=16 * rows * D, transcendentals=rows
        ),
        "backward_chunk",
    )


def weight_sum_kernel(count, left_ref, right_ref, out_ref):
    units = out_ref.shape[2]
    for at in range(count):
        out_ref[at] = lax.dot_general(
            left_ref[...],
            right_ref[:, at * units : (at + 1) * units],
            (((0,), (0,)), ((), ())),
            preferred_element_type=f32,
        ).astype(bf16)


def weight_sum(first, slots, count, left, right, kept):
    rows, depth = left.shape
    units = right.shape[1] // slots
    return chunk_call(
        functools.partial(weight_sum_kernel, slots),
        [
            (pl.BlockSpec((rows, TILE), lambda s: (0, s)), left),
            (pl.BlockSpec((rows, slots * units), lambda s: (0, 0)), right),
        ],
        [
            (
                pl.BlockSpec((slots, TILE, units), lambda s: (first // slots, s, 0)),
                jax.ShapeDtypeStruct((count, depth, units), bf16),
                True,
            )
        ],
        kept,
        (depth // TILE,),
        [],
        pl.CostEstimate(
            flops=2 * rows * depth * units * slots,
            bytes_accessed=2 * slots * (rows * depth + rows * units + depth * units),
            transcendentals=0,
        ),
        "weight_sum",
    )


def shards(
    layer_input,
    cotangent,
    w_query,
    w_key,
    w_value,
    w_output,
    w_gate,
    w_up,
    w_down,
    query_gain,
    key_gain,
    attn_gain,
    mlp_gain,
    slot_parent,
    slot_depth,
):
    dp_index = lax.axis_index("dp")
    tp_index = lax.axis_index("tensor")
    dp_count = lax.axis_size("dp")
    tp_count = lax.axis_size("tensor")
    rows = layer_input.shape[1]
    share = rows // tp_count
    width = w_query.shape[1]
    heads = width // HEAD
    hidden_width = w_gate.shape[1]
    items = heads * MB
    copies = dp_count // items

    def gather_stack(*pieces):
        return lax.all_gather(jnp.stack(pieces), "dp", axis=1, tiled=True)

    def scatter_rows(total, dimension=0):
        return lax.psum_scatter(
            total.astype(bf16), "dp", scatter_dimension=dimension, tiled=True
        )

    def exchange(pieces):
        flat = pieces.reshape((items, -1, HEAD))
        if copies > 1:
            flat = jnp.tile(flat, (copies, 1, 1))
        return lax.all_to_all(flat, "dp", split_axis=0, concat_axis=0, tiled=True)

    def give_back(pieces):
        flat = pieces.reshape((dp_count, -1, HEAD))
        return lax.all_to_all(flat, "dp", split_axis=0, concat_axis=0, tiled=True)[:items]

    w_attn = gather_stack(w_query, w_key, w_value, jnp.transpose(w_output))
    w_gate_all = gather_stack(w_gate)

    order = tree_order(slot_parent, slot_depth)
    my_batch = lax.rem(lax.rem(dp_index, items), MB)
    my_order = lax.dynamic_index_in_dim(order, my_batch, 0, keepdims=False)
    my_depth = lax.dynamic_slice_in_dim(slot_depth, dp_index * SEG_DEV, SEG_DEV, 1)
    cosines, sines = rope_tables(my_depth)

    q_raw, k_raw, squares = project(layer_input, w_attn, (0, 1), True)
    squares = jnp.transpose(squares.reshape(MB * rows, 2))
    (v_raw,) = project(layer_input, w_attn, (2,), False)
    squares = small_sum(squares, "tensor", tp_count)
    inverse = jnp.transpose(lax.rsqrt(squares / D + EPSILON)).reshape(MB, rows, 2)
    gains = jnp.concatenate([query_gain, key_gain])[None, :]
    packed = pack_heads(q_raw, k_raw, v_raw, inverse, gains, cosines, sines, heads)
    w_out_begun = begin_output_weight(w_attn[3], packed, dp_index, dp_count, tp_count)
    packed = follow(exchange(packed), w_out_begun[1:]).reshape(dp_count, 3, SEG_DEV, BLK, HEAD)
    w_out = end_output_weight(w_out_begun, packed, dp_index, dp_count, tp_count)
    w_mlp = (w_gate_all, gather_stack(*follow((w_up, jnp.transpose(w_down)), packed)))

    attended = give_back(attend_forward(my_order, packed))
    attended = attended.reshape(heads, MB, rows, HEAD).transpose(1, 2, 0, 3)
    attended = attended.reshape(MB, rows, width)

    parts = 2
    step = rows // parts
    spots = [(batch, part) for batch in range(MB) for part in range(parts)]
    begun = go_on_all_gather(begin_all_gather(attended[0], tp_count), tp_count)
    gathered, hop = end_all_gather(begun, tp_count)
    everything = [gathered]
    begun = [begun]
    for batch in range(1, MB):
        begun.append(begin_all_gather(follow(attended[batch], hop), tp_count))
    sums = SumLine(tp_count)
    attn_gain_row = attn_gain[None, :]
    mlp_gain_row = mlp_gain[None, :]
    chunks = len(spots)
    state = dict(forward=None, middle=None, backward=None)
    mlp_gain_parts = []
    attn_gain_parts = []

    def forward(at, after):
        batch, part = spots[at]
        if batch == len(everything):
            early = sums.terms[0] if sums.terms else None
            going = go_on_all_gather(begun[batch], tp_count)
            everything.append(end_all_gather(going, tp_count, early)[0])
        *state["forward"], term = forward_chunk(
            at,
            batch,
            part,
            step,
            follow(everything[batch], after),
            layer_input,
            attn_gain_row,
            w_out,
            w_mlp,
            state["forward"],
        )
        return term

    def middle(at, after):
        batch, part = spots[at]
        proj, _, _, silu, slope = state["forward"]
        *kept, gain_part, term = middle_chunk(
            at,
            batch,
            part,
            step,
            follow(sums.sums[at], after),
            proj,
            layer_input,
            cotangent,
            attn_gain_row,
            mlp_gain_row,
            silu,
            slope,
            w_mlp,
            state["middle"],
        )
        state["middle"] = kept
        mlp_gain_parts.append(gain_part)
        return term

    def backward(at, after):
        batch, part = spots[at]
        *kept, gain_part = backward_chunk(
            at,
            batch,
            part,
            step,
            follow(sums.sums[chunks + at], after),
            cotangent,
            state["forward"][0],
            attn_gain_row,
            w_attn,
            state["backward"],
        )
        state["backward"] = kept
        attn_gain_parts.append(gain_part)
        return gain_part

    sums.enter(forward(0, None))
    sums.enter(forward(1, None))
    last = None
    mlp_total = None
    for at in range(2 * chunks + 2):
        after = sums.terms[-1] if last is None and tp_count == 4 else last
        moved = tuple(sums.advance(after)) or None
        coming = at + 2
        if coming < chunks:
            last = forward(coming, moved)
            sums.enter(last)
        elif coming < 2 * chunks:
            last = middle(coming - chunks, moved)
            sums.enter(last)
        else:
            last = backward(coming - 2 * chunks, moved)
            turn_at = coming - 2 * chunks
            output, mlp_grad, gate_grad, up_grad = state["middle"]
            hidden_low, act = state["forward"][1:3]
            left, right = (
                (hidden_low, gate_grad),
                (hidden_low, up_grad),
                (mlp_grad, act),
                (None, None),
            )[turn_at]
            if left is not None:
                mlp_total = weight_sum(turn_at, 1, 3, follow(left, last), right, mlp_total)
                last = mlp_total[0]
        if coming == 3 * chunks - 1:
            break
    hidden_grad, proj_grad, attn_grad = state["backward"]
    mlp_weight_grad = scatter_rows(follow(mlp_total[0], attn_grad), 1)
    attended = attended.reshape(MB * rows, width)
    attn_total = weight_sum(3, 1, 4, proj_grad, follow(attended, attn_grad), None)

    attn_grad = follow(exchange(attn_grad), attn_total)
    attn_grad = attn_grad.reshape(dp_count, SEG_DEV, BLK, HEAD)
    back = give_back(attend_backward(my_order, packed, attn_grad))
    back = back.reshape(heads, MB, 3, rows, HEAD)
    inner, gain_part = inner_sums(back, q_raw, k_raw, inverse, gains, cosines, sines, heads)
    means = small_sum(jnp.transpose(inner.reshape(-1, 2)), "tensor", tp_count) / D
    means = jnp.transpose(means).reshape(MB, rows, 2)
    qkv_grad = None
    terms = []
    for batch in range(MB):
        *qkv_grad, term = unpack_heads(
            batch, back, q_raw, k_raw, inverse, means, gains, cosines, sines, w_attn, heads, qkv_grad
        )
        terms.append(term)
    mlp_weight_grads = [
        mlp_weight_grad[0].astype(f32),
        mlp_weight_grad[1].astype(f32),
        jnp.transpose(mlp_weight_grad[2].astype(f32)),
    ]
    parts, first_operands, second_operands = line_reduce_scatter(terms, tp_count, mlp_weight_grads)
    tokens = layer_input.reshape(MB * rows, D)
    qkv_grad = qkv_grad[0]
    attn_total = weight_sum(0, 3, 4, tokens, qkv_grad, attn_total)
    attn_total = follow(attn_total[0], (mlp_weight_grad, first_operands))
    attn_weight_grad = scatter_rows(attn_total, 1)
    attn_weight_grads = [attn_weight_grad[at].astype(f32) for at in range(4)]
    attn_weight_grads[3] = jnp.transpose(attn_weight_grads[3])
    parts[-1] = (follow(parts[-1][0], attn_weight_grads),) + parts[-1][1:]
    input_grad = jnp.zeros((MB, share, D), f32)
    for batch, part in enumerate(parts):
        mine = lax.dynamic_slice_in_dim(hidden_grad, batch * rows + tp_index * share, share, 0)
        mine = mine + sum(piece.astype(f32) for piece in part)
        input_grad = lax.dynamic_update_slice(input_grad, mine[None], (batch, 0, 0))

    gain_sums = jnp.concatenate(
        [
            gain_part[0],
            sum(attn_gain_parts)[0],
            sum(mlp_gain_parts)[0],
        ]
    )
    gain_sums = follow(gain_sums.reshape(-1, HEAD), second_operands)
    gain_sums = small_sum(gain_sums, "dp", dp_count).reshape(-1)
    return (
        output.reshape(MB, rows, D),
        input_grad,
        *attn_weight_grads,
        *mlp_weight_grads,
        gain_sums[:width],
        gain_sums[width : 2 * width],
        gain_sums[2 * width : 2 * width + D],
        gain_sums[2 * width + D :],
    )


def solution(mesh):
    in_specs = (
        P(None, "dp", None),
        P(None, "dp", None),
        P("dp", "tensor"),
        P("dp", "tensor"),
        P("dp", "tensor"),
        P("tensor", "dp"),
        P("dp", "tensor"),
        P("dp", "tensor"),
        P("tensor", "dp"),
        P("tensor"),
        P("tensor"),
        P(),
        P(),
        P(),
        P(),
    )
    out_specs = (
        P(None, "dp", None),
        P(None, ("dp", "tensor"), None),
        P("dp", "tensor"),
        P("dp", "tensor"),
        P("dp", "tensor"),
        P("tensor", "dp"),
        P("dp", "tensor"),
        P("dp", "tensor"),
        P("tensor", "dp"),
        P("tensor"),
        P("tensor"),
        P(),
        P(),
    )
    return jax.shard_map(shards, mesh=mesh, in_specs=in_specs, out_specs=out_specs, check_vma=False)
```
